128 devices in a mesh: ang: 16 (over x_lo, y, core), slab: 8 (over z, x_hi).
Axes of the slice: x: 4 (x_hi: 2, x_lo: 2; x = x_hi * 2 + x_lo), y: 4, z: 4, core: 2. Of those that a mesh axis runs over, the one named last changes fastest.
Arguments:
- object_field: bfloat16 [2, 8, 1024, 1024], P(None, 'slab'), may hold values from -2 to 2
- probe_field: float32 [2, 256, 256], replicated, may hold values from -6 to 6
- diffraction: float32 [16, 8, 8, 256, 256], P('ang', 'slab'), may hold values from 0.1 to 3
- scan_offsets: int32 [16, 8, 8, 2], P('ang', 'slab'), may hold values from 0 to 768
- counts: int32 [8, 16], P('slab', 'ang'), may hold values from 1 to 8, 64 in all within a row
- band_weights: bfloat16 [16, 8, 2, 4], P(None, 'slab'), may hold values from 0.049804688 to 0.44921875
- band_offsets: int32 [16, 8, 2], P(None, 'slab'), may hold values from -64 to 64
Outputs:
- object_grad: float32 [1024, 2, 8, 1024], P('ang', None, 'slab')
- probe_grad: float32 [2, 256, 256], replicated
The draws below stay inside these ranges and needn't reach their ends.
Inputs may be any that keep to these rules, and one draw needn't show every extreme that they name: In every group the counts over the 16 angles sum to 64; some angle of every group has exactly 8.
All inputs are finite; a program needn't handle non-finite values.
Results may differ from the reference program's by a relative error of at most 0.005.
Values may be sent and summed in bfloat16 or wider, within the bound.
A program may use at most 128 MiB of HBM per device.

```python
import math
import jax
import jax.numpy as jnp
import numpy as np
from jax import lax

PATCH = 256
GRID = 1024
TAPS = 4
SLOTS = 8
SHIFT = 64
ANGLES = 16
NSLAB = 8
NZ = 8
TOTAL_COL = 64
POSITIONS = 512


def plant(result, own_key, low, high):
    shape = result.shape
    place = [jax.random.randint(jax.random.fold_in(own_key, axis), (), 0, shape[axis]) for axis in range(len(shape))]
    result = result.at[tuple(place)].set(low)
    longest = shape.index(max(shape))
    place[longest] = (place[longest] + 1) % shape[longest]
    return result.at[tuple(place)].set(high)


def block_scale(rng, dims, pieces, low, top_value):
    loudness = 1.0
    for position, parts in pieces:
        draws = jax.random.uniform(jax.random.fold_in(jax.random.fold_in(rng, 6), position), (parts,), jnp.float32, low / len(pieces), top_value / len(pieces))
        loudness = loudness * jnp.repeat(jnp.exp(draws), dims[position] // parts).reshape((-1,) + (1,) * (len(dims) - 1 - position))
    return loudness


def split_up(amount, total, most, lean):
    portions = [(1 << 20) // math.isqrt(rank ** lean) + 1 for rank in range(2, amount + 1)]
    rest, given = total - most - (amount - 1), [1] * (amount - 1)
    while rest > 0:
        candidates = [i for i in range(amount - 1) if given[i] < most]
        pool, left = sum([portions[i] for i in candidates]), rest
        for i in candidates:
            more = min(most - given[i], max(1, left * portions[i] // pool), rest)
            given[i] = given[i] + more
            rest = rest - more
    return np.array([most] + given)


def ragged_sizes(stream_key, amount, total, limit, skew):
    if amount == 2:
        one = jax.random.randint(stream_key, (), max(1, total - limit), min(limit, total - 1) + 1)
        return jnp.stack([one, total - one])
    sizes = jnp.asarray(split_up(amount, total, limit, skew), jnp.int32)
    pairs = (amount - 1) // 2
    giver, sink = sizes[1:1 + 2 * pairs:2], sizes[2:2 + 2 * pairs:2]
    margin = jnp.minimum(giver - 1, limit - sink)
    passed = jax.random.randint(jax.random.fold_in(stream_key, 1), (pairs,), 0, 1 << 20) % (margin + 1)
    sizes = sizes.at[1:1 + 2 * pairs:2].set(giver - passed).at[2:2 + 2 * pairs:2].set(sink + passed)
    return sizes[jax.random.permutation(jax.random.fold_in(stream_key, 2), amount)]


def scatter_about(rng, shape, deviation, most, shards=(), kind=jnp.bfloat16):
    drawn = deviation * jax.random.normal(rng, shape, jnp.float32)
    if shards:
        drawn = drawn * block_scale(rng, shape, shards, -0.22, 0.18)
    return jnp.clip(drawn, -most, most).astype(kind)


def setup_inputs(seed: int = 0) -> dict:
    splits = jax.random.split(jax.random.key(seed), 8)
    return {
        "object_field": scatter_about(splits[0], (2, NZ, GRID, GRID), NZ ** -0.5, 2.0, ((1, 8),)),
        "probe_field": scatter_about(splits[1], (2, PATCH, PATCH), 1.0, 6.0, (), jnp.float32),
        "diffraction": jnp.clip(jnp.exp(math.log(3.0) - 3.4011974 * jax.random.uniform(splits[2], (ANGLES, NSLAB, SLOTS, PATCH, PATCH), jnp.float32) ** block_scale(splits[2], (ANGLES, NSLAB, SLOTS, PATCH, PATCH), ((0, 16), (1, 8)), -0.2, 0.2)), 0.1, 3.0),
        "scan_offsets": plant(jax.random.randint(splits[3], (ANGLES, NSLAB, SLOTS, 2), 0, GRID - PATCH + 1), jax.random.fold_in(splits[3], 1), 0, GRID - PATCH).astype(jnp.int32),
        "counts": jax.vmap(lambda own: ragged_sizes(own, ANGLES, TOTAL_COL, SLOTS, 2))(jax.random.split(splits[4], NSLAB)).reshape((NSLAB, ANGLES)).astype(jnp.int32),
        "band_weights": jnp.clip(0.049804688 + 0.39941406 * jax.random.uniform(splits[5], (ANGLES, NZ, 2, TAPS), jnp.float32) ** block_scale(splits[5], (ANGLES, NZ, 2, TAPS), ((1, 8),), -0.2, 0.2), 0.049804688, 0.44921875).astype(jnp.bfloat16),
        "band_offsets": plant(jax.random.randint(splits[6], (ANGLES, NZ, 2), -SHIFT, SHIFT + 1), jax.random.fold_in(splits[6], 1), -SHIFT, SHIFT).astype(jnp.int32),
    }


def band_apply(source, weights, offsets, along_axis, flip_sign):
    extent = source.shape[along_axis]
    base_ids = jnp.arange(extent, dtype=jnp.int32)
    summed = jnp.zeros_like(source)
    for tap_index in range(weights.shape[1]):
        shifted = base_ids[None, :] + flip_sign * (offsets[:, None] + (tap_index - 1))
        inside = (shifted >= 0) & (shifted < extent)
        clipped = jnp.clip(shifted, 0, extent - 1).astype(jnp.int32)
        if along_axis == 2:
            indices = jnp.broadcast_to(clipped[None, :, :, None], source.shape)
            keep = jnp.broadcast_to(inside[None, :, :, None], source.shape)
        else:
            indices = jnp.broadcast_to(clipped[None, :, None, :], source.shape)
            keep = jnp.broadcast_to(inside[None, :, None, :], source.shape)
        picked = jnp.take_along_axis(source, indices, axis=along_axis)
        tap_weight = weights[:, tap_index].astype(jnp.float32)[None, :, None, None]
        summed = summed + jnp.where(keep, picked, jnp.zeros_like(picked)) * tap_weight
    return summed

def reference(object_field, probe_field, diffraction, scan_offsets, counts, band_weights, band_offsets):
    norm_factor = 1.0 / jnp.sqrt(jnp.float32(POSITIONS))
    probe_c = lax.complex(probe_field[0], probe_field[1])
    object_wide = object_field.astype(jnp.float32)
    grad_sum = jnp.zeros(object_field.shape, jnp.float32)
    probe_acc = jnp.zeros_like(probe_c)
    slot_ids = jnp.arange(SLOTS, dtype=jnp.int32)
    for angle_id in range(ANGLES):
        weights_y = band_weights[angle_id, :, 0]
        offsets_y = band_offsets[angle_id, :, 0]
        weights_x = band_weights[angle_id, :, 1]
        offsets_x = band_offsets[angle_id, :, 1]
        lifted = band_apply(object_wide, weights_y, offsets_y, 2, 1)
        lifted = lax.optimization_barrier(lifted.astype(jnp.bfloat16)).astype(jnp.float32)
        projection = lax.optimization_barrier(jnp.sum(band_apply(lifted, weights_x, offsets_x, 3, 1), axis=1))
        corners = scan_offsets[angle_id].reshape(-1, 2)
        patches = jax.vmap(lambda corner: lax.dynamic_slice(projection, (jnp.int32(0), corner[0], corner[1]), (2, PATCH, PATCH)))(corners)
        live_mask = (slot_ids[None, :] < counts[:, angle_id][:, None]).reshape(-1).astype(jnp.float32)
        intensity = diffraction[angle_id].reshape(-1, PATCH, PATCH)
        patch_c = lax.complex(patches[:, 0], patches[:, 1])
        far = jnp.fft.fft2(probe_c[None] * patch_c, norm='ortho')
        misfit = far.real * far.real + far.imag * far.imag - intensity
        chi = jnp.fft.ifft2(misfit * far, norm='ortho') * (norm_factor * live_mask)[:, None, None]
        patch_grad = jnp.conj(probe_c)[None] * chi
        probe_acc = probe_acc + lax.optimization_barrier(jnp.sum(jnp.conj(patch_c) * chi, axis=0))
        stacked = jnp.stack([patch_grad.real, patch_grad.imag], axis=1)

        def add_patch(slot_id, image):
            corner = corners[slot_id]
            window = lax.dynamic_slice(image, (jnp.int32(0), corner[0], corner[1]), (2, PATCH, PATCH))
            return lax.dynamic_update_slice(image, window + stacked[slot_id], (jnp.int32(0), corner[0], corner[1]))
        image = lax.fori_loop(0, corners.shape[0], add_patch, jnp.zeros((2, GRID, GRID), stacked.dtype))
        image = lax.optimization_barrier(image.astype(jnp.bfloat16)).astype(jnp.float32)
        spread_image = jnp.broadcast_to(image[:, None], (2, NZ, GRID, GRID))
        back = band_apply(spread_image, weights_y, offsets_y, 2, -1)
        back = lax.optimization_barrier(back.astype(jnp.bfloat16)).astype(jnp.float32)
        grad_sum = grad_sum + band_apply(back, weights_x, offsets_x, 3, -1)
    object_grad = jnp.transpose(grad_sum, (2, 0, 1, 3))
    probe_grad = jnp.stack([probe_acc.real, probe_acc.imag])
    return (object_grad, probe_grad)
```

```python
import functools
import math

import jax
import jax.numpy as jnp
import numpy as np
from jax import lax
from jax.experimental import pallas as pl
from jax.experimental.pallas import tpu as pltpu
from jax.sharding import PartitionSpec as P

MESH = pl.DeviceIdType.MESH
F32 = jnp.float32
BF16 = jnp.bfloat16
GRID = 1024
PATCH = 256
SLOTS = 8
NSLAB = 8
ROWS = GRID // NSLAB
HALF = ROWS // 2
PAD = 128
HALO = 80
POSITIONS = 512
VMEM_LIMIT = 56 << 20


def block_of(slab):
    return (slab % 2) * 4 + slab // 2


def slab_of(block):
    return (block % 4) * 2 + block // 4


def band(shape, axis_out, start, weights, step):
    inner = lax.broadcasted_iota(jnp.int32, shape, 1 - axis_out)
    outer = lax.broadcasted_iota(jnp.int32, shape, axis_out)
    distance = (inner - outer).astype(F32)
    summed = jnp.zeros(shape, F32)
    for tap, weight in enumerate(weights):
        summed = jnp.where(distance == start + step * tap, weight, summed)
    return summed.astype(BF16)


def encode(values):
    return (values * jnp.abs(values)).astype(BF16)


def decode(codes):
    square = codes.astype(F32)
    return square * lax.rsqrt(jnp.maximum(jnp.abs(square), 1e-37))


def dot(left, right):
    return jnp.dot(left, right, preferred_element_type=F32)


WIDE = GRID // 2
LEFT = pl.ds(0, WIDE)
RIGHT = pl.ds(WIDE, WIDE)


class Post:
    def __init__(self, sends, recvs):
        self.sends = sends
        self.recvs = recvs
        self.opened = []

    def go(self, src, dst, peer):
        k = len(self.opened)
        copy = pltpu.make_async_remote_copy(
            src_ref=src, dst_ref=dst, send_sem=self.sends.at[k], recv_sem=self.recvs.at[k],
            device_id=peer, device_id_type=MESH,
        )
        copy.start()
        self.opened.append(copy)
        return copy

    def finish(self):
        for copy in self.opened:
            copy.wait_send()


class Place:
    def __init__(self):
        self.ang = lax.axis_index("ang")
        self.me = lax.axis_index("slab")
        self.z = self.me // 2
        self.xh = self.me % 2

    def slab(self, dz, other):
        x = 1 - self.xh if other else self.xh
        return lax.rem(self.z + dz, 4) * 2 + x

    def peer(self, dz, other):
        return (self.ang, self.slab(dz, other))

    def block(self, dz, other):
        return block_of(self.slab(dz, other))


class Ring:
    def __init__(self, post, place, bufs, own, first):
        self.post, self.place = post, place
        self.hr, self.fs, self.fr = bufs
        self.own, self.first = own, first

    def start(self):
        self.halves = [
            self.post.go(self.first(k), self.hr.at[k], self.place.peer((1, 3)[k], 0))
            for k in range(2)
        ]

    def middle(self):
        self.whole = []
        for k, dz in enumerate((1, 3)):
            lo = HALF * k
            self.fs[k, HALF - lo : ROWS - lo, :] = encode(self.own(dz, HALF - lo, HALF))
            self.halves[k].wait_recv()
            both = self.own(dz, lo, HALF) + decode(self.hr[k])
            self.fs[k, lo : lo + HALF, :] = encode(both)
            self.whole.append(self.post.go(self.fs.at[k], self.fr.at[k], self.place.peer(dz, 0)))

    def end(self):
        for copy in self.whole:
            copy.wait_recv()
        return self.own(0, 0, ROWS) + decode(self.fr[0]) + decode(self.fr[1])


class Reduce:
    def __init__(self, post, place, part, bufs, own, ref):
        hs, hr, fs, fr, xs, xr = bufs
        self.post, self.place, self.own, self.ref = post, place, own, ref
        self.hs, self.xs, self.xr = hs.at[part], xs.at[part], xr.at[part]
        self.rings = []
        for chain, other in enumerate((1, 0)):
            self.rings.append(
                Ring(
                    post, place, (hr.at[part, chain], fs.at[part, chain], fr.at[part, chain]),
                    functools.partial(self.left, other),
                    functools.partial(self.left_first, other, chain),
                )
            )
        self.rings.append(
            Ring(
                post, place, (hr.at[part, 2], fs.at[part, 2], fr.at[part, 2]),
                self.right, self.right_first,
            )
        )
        self.crossing = {}

    def left(self, other, dz, lo, n):
        return self.own(dz, other, lo, n, LEFT)

    def left_first(self, other, chain, k):
        return self.ref(2, other, HALF * k, HALF, LEFT, self.hs.at[chain, k])

    def right(self, dz, lo, n):
        return self.own(dz, 0, lo, n, RIGHT) + decode(self.xr[dz, lo : lo + n, :])

    def right_first(self, k):
        self.hs[2, k] = encode(self.right(2, HALF * k, HALF))
        return self.hs.at[2, k]

    def start_far(self, other):
        self.rings[1 - other].start()

    def start_cross(self, dz):
        src = self.ref(dz, 1, 0, ROWS, RIGHT, self.xs.at[dz])
        self.crossing[dz] = self.post.go(src, self.xr.at[dz], self.place.peer(0, 1))

    def stage1(self):
        self.rings[0].middle()
        self.rings[1].middle()

    def stage2(self):
        self.crossing[2].wait_recv()
        self.rings[2].start()

    def stage3(self):
        self.xs[4] = encode(self.rings[0].end())
        self.crossing[4] = self.post.go(self.xs.at[4], self.xr.at[4], self.place.peer(0, 1))

    def stage4(self):
        self.crossing[1].wait_recv()
        self.crossing[3].wait_recv()
        self.rings[2].middle()

    def stage5(self):
        mine = self.rings[1].end()
        self.crossing[4].wait_recv()
        return mine + decode(self.xr[4])

    def stage6(self):
        self.crossing[0].wait_recv()
        return self.rings[2].end()


def reduce_scratch():
    code = BF16
    return [
        pltpu.VMEM((2, 3, 2, HALF, WIDE), code),
        pltpu.VMEM((2, 3, 2, HALF, WIDE), code),
        pltpu.VMEM((2, 3, 2, ROWS, WIDE), code),
        pltpu.VMEM((2, 3, 2, ROWS, WIDE), code),
        pltpu.VMEM((2, 5, ROWS, WIDE), code),
        pltpu.VMEM((2, 5, ROWS, WIDE), code),
    ]


class Gather:
    def __init__(self, post, place, part, whole):
        self.post, self.place, self.part, self.whole = post, place, part, whole

    def span(self, dz, other, cols, lo=0, n=ROWS):
        start = pl.multiple_of(self.place.block(dz, other) * ROWS + lo, HALF)
        return self.whole.at[self.part, pl.ds(start, n), cols]

    def send(self, dz, other, cols, to_dz, to_other, lo=0, n=ROWS):
        span = self.span(dz, other, cols, lo, n)
        return self.post.go(span, span, self.place.peer(to_dz, to_other))

    def spread(self, other, cols):
        return [self.send(0, other, cols, dz, 0) for dz in (1, 3)]

    def relay(self, other, cols, pair):
        pair[0].wait_recv()
        first = self.send(3, other, cols, 1, 0, 0, HALF)
        pair[1].wait_recv()
        return [first, self.send(1, other, cols, 3, 0, HALF, HALF)]

    def stage0(self):
        self.cross_left = self.send(0, 0, LEFT, 0, 1)
        self.right = self.spread(0, RIGHT)
        self.cross_right = [self.send(0, 0, RIGHT, 0, 1)]
        self.left = self.spread(0, LEFT)

    def stage1(self):
        self.right_far = self.relay(0, RIGHT, self.right)
        for dz in (3, 1):
            self.cross_right.append(self.send(dz, 0, RIGHT, 0, 1))

    def stage2(self):
        self.cross_left.wait_recv()
        self.left_other = self.spread(1, LEFT)

    def stage3(self):
        self.left_far = self.relay(0, LEFT, self.left)

    def stage4(self):
        for copy in self.right_far:
            copy.wait_recv()
        self.cross_right.append(self.send(2, 0, RIGHT, 0, 1))

    def stage5(self):
        self.left_far += self.relay(1, LEFT, self.left_other)

    def stage6(self):
        for copy in self.left_far + self.cross_right:
            copy.wait_recv()


def greet(place):
    barrier = pltpu.get_barrier_semaphore()
    for dz in range(4):
        for other in range(2):
            if (dz, other) != (0, 0):
                pl.semaphore_signal(
                    barrier, inc=1, device_id=place.peer(dz, other), device_id_type=MESH
                )
    return barrier


def run_reduces(first, second, done):
    first.stage1()
    second.stage1()
    first.stage2()
    first.stage3()
    second.stage2()
    first.stage4()
    second.stage3()
    left = first.stage5()
    right = first.stage6()
    done(0, left, right)
    second.stage4()
    left = second.stage5()
    right = second.stage6()
    done(1, left, right)


def forward_kernel(
    offs, wts, par, obj, proj, par_all,
    opad, lift, t0, t1, dbuf, hs, hr, fs, fr, xs, xr,
    load_sem, sends, recvs,
):
    place = Place()
    barrier = greet(place)
    load = pltpu.make_async_copy(obj, opad.at[:, pl.ds(PAD, GRID), :], load_sem)
    load.start()
    opad[:, :PAD, :] = jnp.zeros((2, PAD, GRID), BF16)
    opad[:, PAD + GRID :, :] = jnp.zeros((2, PAD, GRID), BF16)
    lift[:, :PAD] = jnp.zeros((2 * ROWS, PAD), BF16)
    lift[:, PAD + GRID :] = jnp.zeros((2 * ROWS, PAD), BF16)
    off_y = offs[0]
    off_x = offs[1]
    t0[...] = band(t0.shape, 0, (off_y + PAD - 1).astype(F32), [wts[t] for t in range(4)], 1)
    t1[...] = band(t1.shape, 1, (off_x + PAD - 1).astype(F32), [wts[4 + t] for t in range(4)], 1)
    load.wait()

    par_all[pl.ds(place.me, 1)] = par[...][None]
    pl.semaphore_wait(barrier, NSLAB - 1)
    post = Post(sends, recvs)
    par_copies = []
    for dz in range(4):
        for other in range(2):
            if (dz, other) != (0, 0):
                span = par_all.at[place.me]
                par_copies.append(post.go(span, span, place.peer(dz, other)))

    def slot(dz, other):
        return 2 * dz + other

    def project(dz, other):
        start = pl.multiple_of(place.block(dz, other) * ROWS, ROWS)
        for part in range(2):
            rows = opad[part, pl.ds(start, 3 * PAD), :]
            lift[part * ROWS : (part + 1) * ROWS, PAD : PAD + GRID] = dot(t0[...], rows).astype(BF16)
        for q in range(GRID // 256):
            tile = dot(lift[:, 256 * q : 256 * q + 512], t1[...])
            dbuf[slot(dz, other), :, :, 256 * q : 256 * q + 256] = tile.reshape(2, ROWS, 256)

    bufs = (hs, hr, fs, fr, xs, xr)
    reduces = []
    for part in range(2):

        def own(dz, other, lo, n, cols, part=part):
            return dbuf[slot(dz, other), part, pl.ds(lo, n), cols]

        def ref(dz, other, lo, n, cols, room, part=part):
            room[...] = encode(own(dz, other, lo, n, cols, part))
            return room

        reduces.append(Reduce(post, place, part, bufs, own, ref))
    for dz, other in ((2, 1), (2, 0), (1, 1), (3, 1), (0, 1), (1, 0), (3, 0), (0, 0)):
        project(dz, other)
        for reduce in reduces:
            if dz == 2:
                reduce.start_far(other)
            if other == 1:
                reduce.start_cross(dz)
    rows = pl.ds(pl.multiple_of(place.block(0, 0) * ROWS, ROWS), ROWS)
    gathers = [Gather(post, place, part, proj) for part in range(2)]

    def done(part, left, right):
        proj[part, rows, LEFT] = encode(left)
        proj[part, rows, RIGHT] = encode(right)
        gathers[part].stage0()

    run_reduces(reduces[0], reduces[1], done)
    for k in range(1, 7):
        for gather in gathers:
            getattr(gather, "stage%d" % k)()
    for copy in par_copies:
        copy.wait_recv()
    post.finish()


def forward(offs, wts, par, obj):
    return pl.pallas_call(
        forward_kernel,
        out_shape=(
            jax.ShapeDtypeStruct((2, GRID, GRID), BF16),
            jax.ShapeDtypeStruct((NSLAB, 16, 512), F32),
        ),
        in_specs=[
            pl.BlockSpec(memory_space=pltpu.SMEM),
            pl.BlockSpec(memory_space=pltpu.SMEM),
            pl.BlockSpec(memory_space=pltpu.VMEM),
            pl.BlockSpec(memory_space=pl.ANY),
        ],
        out_specs=(
            pl.BlockSpec(memory_space=pltpu.VMEM),
            pl.BlockSpec(memory_space=pltpu.VMEM),
        ),
        scratch_shapes=[
            pltpu.VMEM((2, GRID + 2 * PAD, GRID), BF16),
            pltpu.VMEM((2 * ROWS, GRID + 2 * PAD), BF16),
            pltpu.VMEM((ROWS, 3 * PAD), BF16),
            pltpu.VMEM((512, 256), BF16),
            pltpu.VMEM((NSLAB, 2, ROWS, GRID), F32),
        ]
        + reduce_scratch()
        + [
            pltpu.SemaphoreType.DMA,
            pltpu.SemaphoreType.DMA((96,)),
            pltpu.SemaphoreType.DMA((96,)),
        ],
        compiler_params=pltpu.CompilerParams(
            collective_id=0, has_side_effects=True, vmem_limit_bytes=VMEM_LIMIT
        ),
        name="forward",
    )(offs, wts, par, obj)


def dft_tables():
    index = np.arange(PATCH)
    phase = 2.0 * np.pi * ((index[:, None] * index[None, :]) % PATCH) / PATCH
    cosines = np.cos(phase) / math.sqrt(PATCH)
    sines = np.sin(phase) / math.sqrt(PATCH)
    whole = np.block([[cosines, -sines], [sines, cosines]]).astype(np.float32)
    high = whole.astype(jnp.bfloat16)
    low = (whole - high.astype(np.float32)).astype(jnp.bfloat16)
    across = np.concatenate([high, high, low], axis=1)
    across_t = np.concatenate([high.T, high.T, low.T], axis=1)
    return across_t, np.ascontiguousarray(across_t.T), across, np.ascontiguousarray(across.T)


def split_join(values, axis):
    high = values.astype(BF16)
    low = (values - high.astype(F32)).astype(BF16)
    return jnp.concatenate([high, low, high], axis=axis)


def slots_kernel(
    corners, count, proj, probe, diff, left_f, right_f, left_i, right_i,
    image, probe_part, wide, total,
):
    slot = pl.program_id(0)

    @pl.when(slot == 0)
    def _():
        for tile in range(GRID // 128):
            wide[:, tile] = decode(proj[:, :, 128 * tile : 128 * tile + 128])
        total[...] = jnp.zeros(total.shape, F32)
        probe_part[...] = jnp.zeros(probe_part.shape, F32)

    @pl.when(slot < count[0])
    def _():
        row = corners[slot, 0]
        col = corners[slot, 1]
        turn = lax.rem(col, 128)
        tile = col // 128
        lane = lax.broadcasted_iota(jnp.int32, (PATCH, 128), 1)
        early = lane < turn
        patch = []
        for part in range(2):
            window = [wide[part, tile + k, pl.ds(row, PATCH), :] for k in range(3)]
            joined = jnp.concatenate([jnp.where(early, window[2], window[0]), window[1]], axis=1)
            patch.append(pltpu.roll(joined, lax.rem(PATCH - turn, PATCH), 1))
        patch_re, patch_im = patch
        probe_re = probe[0]
        probe_im = probe[1]
        wave = jnp.concatenate(
            [
                probe_re * patch_re - probe_im * patch_im,
                probe_re * patch_im + probe_im * patch_re,
            ],
            axis=0,
        )
        half = dot(left_f[...], split_join(wave, 0))
        half = jnp.concatenate([half[:PATCH], half[PATCH:]], axis=1)
        far = dot(split_join(half, 1), right_f[...])
        far_re = far[:, :PATCH]
        far_im = far[:, PATCH:]
        misfit = (far_re * far_re + far_im * far_im - diff[0]) * (1.0 / math.sqrt(POSITIONS))
        resid = jnp.concatenate([misfit * far_re, misfit * far_im], axis=0)
        inner = dot(left_i[...], split_join(resid, 0))
        inner = jnp.concatenate([inner[:PATCH], inner[PATCH:]], axis=1)
        chi = dot(split_join(inner, 1), right_i[...])
        chi_re = chi[:, :PATCH]
        chi_im = chi[:, PATCH:]
        probe_part[0] += patch_re * chi_re + patch_im * chi_im
        probe_part[1] += patch_re * chi_im - patch_im * chi_re
        grads = (
            probe_re * chi_re + probe_im * chi_im,
            probe_re * chi_im - probe_im * chi_re,
        )
        zero = jnp.zeros((PATCH, 128), F32)
        for part in range(2):
            turned = pltpu.roll(grads[part], turn, 1)
            head = turned[:, :128]
            spread = (jnp.where(early, zero, head), turned[:, 128:], jnp.where(early, head, zero))
            for k in range(3):
                total[part, tile + k, pl.ds(row, PATCH), :] += spread[k]

    @pl.when(slot == SLOTS - 1)
    def _():
        for tile in range(GRID // 128):
            image[:, :, 128 * tile : 128 * tile + 128] = encode(total[:, tile])


def slots(corners, count, proj, probe, diffraction):
    tables = [jnp.asarray(t) for t in dft_tables()]
    whole = pl.BlockSpec(memory_space=pltpu.VMEM)
    scalar = pl.BlockSpec(memory_space=pltpu.SMEM)
    return pl.pallas_call(
        slots_kernel,
        grid=(SLOTS,),
        out_shape=(
            jax.ShapeDtypeStruct((2, GRID, GRID), BF16),
            jax.ShapeDtypeStruct((2, PATCH, PATCH), F32),
        ),
        in_specs=[
            scalar, scalar, whole, whole,
            pl.BlockSpec((1, PATCH, PATCH), lambda i: (i, 0, 0)),
            whole, whole, whole, whole,
        ],
        out_specs=(whole, whole),
        scratch_shapes=[
            pltpu.VMEM((2, GRID // 128 + 1, GRID, 128), F32),
            pltpu.VMEM((2, GRID // 128 + 1, GRID, 128), F32),
        ],
        compiler_params=pltpu.CompilerParams(vmem_limit_bytes=VMEM_LIMIT),
        name="slots",
    )(corners, count, proj, probe, diffraction, *tables)


def backward_kernel(
    image, par_all, probe_part, result, probe_out,
    t0, t1, ext, padded, gbuf, cbuf, hbuf, bbuf, fin,
    pbuf, pacc, pcore, py, pxl, psum, hs, hr, fs, fr, xs, xr,
    sends, recvs, fsend, frecv,
):
    place = Place()
    ang, me, z, xh = place.ang, place.me, place.z, place.xh
    core = lax.rem(ang, 2)
    chip = ang // 2
    y = lax.rem(chip, 4)
    xl = chip // 4
    mine = place.block(0, 0)

    def ang_id(xl_, y_, core_):
        return (xl_ * 4 + y_) * 2 + core_

    def chip_peer(j):
        return (lax.rem(chip + j, 8) * 2 + core, me)

    core_peer = (ang_id(xl, y, 1 - core), me)
    turn_peer = (ang_id(xh, z, core), y * 2 + xl)
    stays = jnp.logical_and(xl == xh, y == z)
    above = (ang, slab_of(lax.rem(mine + NSLAB - 1, NSLAB)))
    below = (ang, slab_of(lax.rem(mine + 1, NSLAB)))

    barrier = greet(place)
    for j in range(1, NSLAB):
        pl.semaphore_signal(barrier, inc=1, device_id=chip_peer(j), device_id_type=MESH)
    pl.semaphore_signal(barrier, inc=1, device_id=core_peer, device_id_type=MESH)

    @pl.when(jnp.logical_not(stays))
    def _():
        pl.semaphore_signal(barrier, inc=1, device_id=turn_peer, device_id_type=MESH)

    def tables(s, carry):
        rows = [par_all[s, k : k + 1, :] for k in range(10)]
        t0[pl.ds(pl.multiple_of(s * ROWS, ROWS), ROWS), :] = band(
            (ROWS, 384), 0, HALO + 1 - rows[8][:, :384], [r[:, :384] for r in rows[:4]], -1
        )
        t1[s] = band((512, 256), 1, PAD + 1 - rows[9][:, :256], [r[:, :256] for r in rows[4:8]], -1)
        return carry

    lax.fori_loop(0, NSLAB, tables, 0)
    ext[:, HALO + ROWS + HALO :, :] = jnp.zeros((2, 384 - ROWS - 2 * HALO, GRID), BF16)
    padded[:, :PAD] = jnp.zeros((NSLAB * ROWS, PAD), BF16)
    padded[:, PAD + GRID :] = jnp.zeros((NSLAB * ROWS, PAD), BF16)
    pl.semaphore_wait(barrier, 2 * (NSLAB - 1) + 1 + jnp.where(stays, 0, 1))

    post = Post(sends, recvs)
    peers = [(dz, other) for dz in range(4) for other in range(2)][1:]
    bufs = (hs, hr, fs, fr, xs, xr)
    reduces = []
    for part in range(2):

        def ref(dz, other, lo, n, cols, room, part=part):
            start = pl.multiple_of(place.block(dz, other) * ROWS + lo, HALF)
            return image.at[part, pl.ds(start, n), cols]

        def own(dz, other, lo, n, cols, part=part, ref=ref):
            return decode(ref(dz, other, lo, n, cols, None)[...])

        reduces.append(Reduce(post, place, part, bufs, own, ref))
    first, second = reduces

    def open_reduce(reduce):
        for dz in (2, 1, 3, 0):
            reduce.start_cross(dz)
            if dz == 2:
                reduce.start_far(1)
                reduce.start_far(0)

    halos = {}

    def finish_reduce(part, reduce):
        ext[part, HALO : HALO + ROWS, LEFT] = reduce.stage5().astype(BF16)
        ext[part, HALO : HALO + ROWS, RIGHT] = reduce.stage6().astype(BF16)
        halos[part] = [
            post.go(ext.at[part, pl.ds(HALO, HALO), :], ext.at[part, pl.ds(HALO + ROWS, HALO), :], above),
            post.go(ext.at[part, pl.ds(ROWS, HALO), :], ext.at[part, pl.ds(0, HALO), :], below),
        ]

    cores = {}

    def spread_slices(part):
        for copy in halos[part]:
            copy.wait_recv()

        @pl.when(mine == 0)
        def _():
            ext[part, :HALO, :] = jnp.zeros((HALO, GRID), BF16)

        @pl.when(mine == NSLAB - 1)
        def _():
            ext[part, HALO + ROWS : 2 * HALO + ROWS, :] = jnp.zeros((HALO, GRID), BF16)

        for q in range(GRID // 256):
            cols = pl.ds(256 * q, 256)
            padded[:, PAD + 256 * q : PAD + 256 * q + 256] = dot(t0[...], ext[part, :, cols]).astype(BF16)

        def slice_step(s, carry):
            rows = pl.ds(pl.multiple_of(s * ROWS, ROWS), ROWS)
            stack = jnp.concatenate(
                [padded[rows, 256 * q : 256 * q + 512] for q in range(GRID // 256)], axis=0
            )
            tiles = encode(dot(stack, t1[s]))
            for q in range(GRID // 256):
                cols = slice(256 * q, 256 * q + 256)
                for half in range(2):
                    lo = ROWS * q + HALF * half
                    gbuf[part, half, s, :, cols] = tiles[lo : lo + HALF]
            return carry

        cores[part] = []
        for k in range(2):
            lax.fori_loop(4 * k, 4 * k + 4, slice_step, 0)
            group = pl.ds(4 * k, 4)
            cores[part].append(
                post.go(gbuf.at[part, 1 - core, group], cbuf.at[part, group], core_peer)
            )

    chips = {}

    def combine(part):
        for copy in cores[part]:
            copy.wait_recv()
        chips[part] = []
        for j in (4, 6, 2, 5, 7, 1, 3, 0):
            target = lax.rem(chip + j, 8)
            s = lax.rem(target, 4) * 2 + target // 4
            both = decode(gbuf[part, core, s]) + decode(cbuf[part, s])
            hbuf[part, j] = encode(both)
            if j:
                chips[part].append(post.go(hbuf.at[part, j], bbuf.at[part, j], chip_peer(j)))

    def turn_copy(part):
        return pltpu.make_async_remote_copy(
            src_ref=fin.at[part], dst_ref=result.at[part], send_sem=fsend.at[part],
            recv_sem=frecv.at[part], device_id=turn_peer, device_id_type=MESH,
        )

    def settle(part):
        for copy in chips[part]:
            copy.wait_recv()
        total = decode(hbuf[part, 0])
        for j in range(1, NSLAB):
            total = total + decode(bbuf[part, j])
        fin[part] = encode(total)

        @pl.when(stays)
        def _():
            result[part] = fin[part]

        @pl.when(jnp.logical_not(stays))
        def _():
            turn_copy(part).start()

    open_reduce(first)
    probe_copies = []
    for dz, other in peers:
        dest = place.slab(dz, other)
        rows = pl.ds(pl.multiple_of(dest * 64, 64), 64)
        probe_copies.append(
            post.go(probe_part.at[rows, :], pbuf.at[2 * dz + other], place.peer(dz, other))
        )
    first.stage1()
    open_reduce(second)
    first.stage2()
    first.stage3()
    first.stage4()
    second.stage1()
    second.stage2()
    finish_reduce(0, first)
    second.stage3()

    total = probe_part[pl.ds(pl.multiple_of(me * 64, 64), 64), :]
    for copy, (dz, other) in zip(probe_copies, peers):
        copy.wait_recv()
        total = total + pbuf[2 * dz + other]
    pacc[...] = total
    core_probe = post.go(pacc, pcore, core_peer)

    second.stage4()
    spread_slices(0)
    finish_reduce(1, second)

    core_probe.wait_recv()
    psum[0] = pacc[...] + pcore[...]
    y_copies = [
        post.go(psum.at[0], py.at[j], (ang_id(xl, lax.rem(y + j, 4), core), me)) for j in range(1, 4)
    ]
    combine(0)
    spread_slices(1)
    for copy in y_copies:
        copy.wait_recv()
    psum[1] = (psum[0] + py[1]) + (py[2] + py[3])
    xl_probe = post.go(psum.at[1], pxl, (ang_id(1 - xl, y, core), me))
    combine(1)
    settle(0)
    xl_probe.wait_recv()
    span = probe_out.at[pl.ds(pl.multiple_of(me * 64, 64), 64), :]
    span[...] = psum[1] + pxl[...]
    out_copies = [post.go(span, span, place.peer(*peer)) for peer in peers]
    settle(1)
    for copy in out_copies:
        copy.wait_recv()

    @pl.when(jnp.logical_not(stays))
    def _():
        turn_copy(0).wait()
        turn_copy(1).wait()

    post.finish()


def backward(image, par_all, probe_part):
    whole = pl.BlockSpec(memory_space=pltpu.VMEM)
    dma = pltpu.SemaphoreType.DMA
    return pl.pallas_call(
        backward_kernel,
        out_shape=(
            jax.ShapeDtypeStruct((2, HALF, GRID), BF16),
            jax.ShapeDtypeStruct((2 * PATCH, PATCH), F32),
        ),
        in_specs=[whole] * 3,
        out_specs=(whole, whole),
        scratch_shapes=[
            pltpu.VMEM((NSLAB * ROWS, 384), BF16),
            pltpu.VMEM((NSLAB, 512, 256), BF16),
            pltpu.VMEM((2, 384, GRID), BF16),
            pltpu.VMEM((NSLAB * ROWS, GRID + 2 * PAD), BF16),
            pltpu.VMEM((2, 2, NSLAB, HALF, GRID), BF16),
            pltpu.VMEM((2, NSLAB, HALF, GRID), BF16),
            pltpu.VMEM((2, NSLAB, HALF, GRID), BF16),
            pltpu.VMEM((2, NSLAB, HALF, GRID), BF16),
            pltpu.VMEM((2, HALF, GRID), BF16),
            pltpu.VMEM((NSLAB, 64, PATCH), F32),
            pltpu.VMEM((64, PATCH), F32),
            pltpu.VMEM((64, PATCH), F32),
            pltpu.VMEM((4, 64, PATCH), F32),
            pltpu.VMEM((64, PATCH), F32),
            pltpu.VMEM((2, 64, PATCH), F32),
        ]
        + reduce_scratch()
        + [dma((96,)), dma((96,)), dma((2,)), dma((2,))],
        compiler_params=pltpu.CompilerParams(
            collective_id=1, has_side_effects=True, vmem_limit_bytes=VMEM_LIMIT
        ),
        name="backward",
    )(image, par_all, probe_part)


def per_device(
    object_field, probe_field, diffraction, scan_offsets, counts, band_weights, band_offsets
):
    ang = lax.axis_index("ang")
    weights = lax.dynamic_index_in_dim(band_weights, ang, 0, keepdims=False)[0]
    offsets = lax.dynamic_index_in_dim(band_offsets, ang, 0, keepdims=False)[0]
    weights = weights.astype(F32).reshape(8)
    par = jnp.concatenate([weights, offsets.astype(F32), jnp.zeros((6,), F32)])
    par = jnp.broadcast_to(par[:, None], (16, 512))
    proj, par_all = forward(offsets, weights, par, object_field.reshape(2, GRID, GRID))
    image, probe_part = slots(
        scan_offsets[0, 0], counts[0], proj, probe_field, diffraction[0, 0]
    )
    result, probe_out = backward(image, par_all, probe_part.reshape(2 * PATCH, PATCH))
    object_grad = decode(jnp.transpose(result, (1, 0, 2)))[:, :, None, :]
    return (object_grad, probe_out.reshape(2, PATCH, PATCH))


def solution(mesh):
    placed = (
        P(None, "slab", None, None),
        P(),
        P("ang", "slab", None, None, None),
        P("ang", "slab", None, None),
        P("slab", "ang"),
        P(None, "slab", None, None),
        P(None, "slab", None),
    )
    return jax.shard_map(
        per_device,
        mesh=mesh,
        in_specs=placed,
        out_specs=(P("ang", None, "slab", None), P()),
        check_vma=False,
    )
```

```python
import functools
import math

import jax
import jax.numpy as jnp
import numpy as np
from jax import lax
from jax.experimental import pallas as pl
from jax.experimental.pallas import tpu as pltpu
from jax.sharding import PartitionSpec as P

MESH = pl.DeviceIdType.MESH
F32 = jnp.float32
BF16 = jnp.bfloat16
GRID = 1024
PATCH = 256
SLOTS = 8
NSLAB = 8
ROWS = GRID // NSLAB
HALF = ROWS // 2
PAD = 128
HALO = 80
POSITIONS = 512
VMEM_LIMIT = 56 << 20


def block_of(slab):
    return (slab % 2) * 4 + slab // 2


def slab_of(block):
    return (block % 4) * 2 + block // 4


def band(shape, axis_out, start, weights, step):
    inner = lax.broadcasted_iota(jnp.int32, shape, 1 - axis_out)
    outer = lax.broadcasted_iota(jnp.int32, shape, axis_out)
    distance = (inner - outer).astype(F32)
    summed = jnp.zeros(shape, F32)
    for tap, weight in enumerate(weights):
        summed = jnp.where(distance == start + step * tap, weight, summed)
    return summed.astype(BF16)


def encode(values):
    return (values * jnp.abs(values)).astype(BF16)


def decode(codes):
    square = codes.astype(F32)
    return square * lax.rsqrt(jnp.maximum(jnp.abs(square), 1e-37))


def encode_fine(values):
    square = values * jnp.abs(values) * 2.0**32
    return (square * jnp.abs(square)).astype(BF16)


def decode_fine(codes):
    fourth = codes.astype(F32)
    square = fourth * lax.rsqrt(jnp.maximum(jnp.abs(fourth), 1e-37))
    return square * (lax.rsqrt(jnp.maximum(jnp.abs(square), 1e-30)) * 2.0**-16)


def dot(left, right):
    return jnp.dot(left, right, preferred_element_type=F32)


WIDE = GRID // 2
LEFT = pl.ds(0, WIDE)
RIGHT = pl.ds(WIDE, WIDE)


class Post:
    def __init__(self, sends, recvs):
        self.sends = sends
        self.recvs = recvs
        self.opened = []

    def go(self, src, dst, peer):
        k = len(self.opened)
        copy = pltpu.make_async_remote_copy(
            src_ref=src, dst_ref=dst, send_sem=self.sends.at[k], recv_sem=self.recvs.at[k],
            device_id=peer, device_id_type=MESH,
        )
        copy.start()
        self.opened.append(copy)
        return copy

    def finish(self):
        for copy in self.opened:
            copy.wait_send()


class Place:
    def __init__(self):
        self.ang = lax.axis_index("ang")
        self.me = lax.axis_index("slab")
        self.z = self.me // 2
        self.xh = self.me % 2

    def slab(self, dz, other):
        x = 1 - self.xh if other else self.xh
        return lax.rem(self.z + dz, 4) * 2 + x

    def peer(self, dz, other):
        return (self.ang, self.slab(dz, other))

    def block(self, dz, other):
        return block_of(self.slab(dz, other))


class Ring:
    def __init__(self, post, place, bufs, own, first, codec):
        self.post, self.place = post, place
        self.encode, self.decode = codec
        self.hr, self.fs, self.fr = bufs
        self.own, self.first = own, first

    def start(self):
        self.halves = [
            self.post.go(self.first(k), self.hr.at[k], self.place.peer((1, 3)[k], 0))
            for k in range(2)
        ]

    def middle(self):
        self.whole = []
        for k, dz in enumerate((1, 3)):
            lo = HALF * k
            self.fs[k, HALF - lo : ROWS - lo, :] = self.encode(self.own(dz, HALF - lo, HALF))
            self.halves[k].wait_recv()
            both = self.own(dz, lo, HALF) + self.decode(self.hr[k])
            self.fs[k, lo : lo + HALF, :] = self.encode(both)
            self.whole.append(self.post.go(self.fs.at[k], self.fr.at[k], self.place.peer(dz, 0)))

    def end(self):
        for copy in self.whole:
            copy.wait_recv()
        return self.own(0, 0, ROWS) + self.decode(self.fr[0]) + self.decode(self.fr[1])


class Reduce:
    def __init__(self, post, place, part, bufs, own, ref, codec):
        hs, hr, fs, fr, xs, xr = bufs
        self.post, self.place, self.own, self.ref = post, place, own, ref
        self.encode, self.decode = codec
        self.hs, self.xs, self.xr = hs.at[part], xs.at[part], xr.at[part]
        self.rings = []
        for chain, other in enumerate((1, 0)):
            self.rings.append(
                Ring(
                    post, place, (hr.at[part, chain], fs.at[part, chain], fr.at[part, chain]),
                    functools.partial(self.left, other),
                    functools.partial(self.left_first, other, chain), codec,
                )
            )
        self.rings.append(
            Ring(
                post, place, (hr.at[part, 2], fs.at[part, 2], fr.at[part, 2]),
                self.right, self.right_first, codec,
            )
        )
        self.crossing = {}

    def left(self, other, dz, lo, n):
        return self.own(dz, other, lo, n, LEFT)

    def left_first(self, other, chain, k):
        return self.ref(2, other, HALF * k, HALF, LEFT, self.hs.at[chain, k])

    def right(self, dz, lo, n):
        return self.own(dz, 0, lo, n, RIGHT) + self.decode(self.xr[dz, lo : lo + n, :])

    def right_first(self, k):
        self.hs[2, k] = self.encode(self.right(2, HALF * k, HALF))
        return self.hs.at[2, k]

    def start_far(self, other):
        self.rings[1 - other].start()

    def start_cross(self, dz):
        src = self.ref(dz, 1, 0, ROWS, RIGHT, self.xs.at[dz])
        self.crossing[dz] = self.post.go(src, self.xr.at[dz], self.place.peer(0, 1))

    def stage1(self):
        self.rings[0].middle()
        self.rings[1].middle()

    def stage2(self):
        self.crossing[2].wait_recv()
        self.rings[2].start()

    def stage3(self):
        self.xs[4] = self.encode(self.rings[0].end())
        self.crossing[4] = self.post.go(self.xs.at[4], self.xr.at[4], self.place.peer(0, 1))

    def stage4(self):
        self.crossing[1].wait_recv()
        self.crossing[3].wait_recv()
        self.rings[2].middle()

    def stage5(self):
        mine = self.rings[1].end()
        self.crossing[4].wait_recv()
        return mine + self.decode(self.xr[4])

    def stage6(self):
        self.crossing[0].wait_recv()
        return self.rings[2].end()


def reduce_scratch():
    code = BF16
    return [
        pltpu.VMEM((2, 3, 2, HALF, WIDE), code),
        pltpu.VMEM((2, 3, 2, HALF, WIDE), code),
        pltpu.VMEM((2, 3, 2, ROWS, WIDE), code),
        pltpu.VMEM((2, 3, 2, ROWS, WIDE), code),
        pltpu.VMEM((2, 5, ROWS, WIDE), code),
        pltpu.VMEM((2, 5, ROWS, WIDE), code),
    ]


class Gather:
    def __init__(self, post, place, part, whole):
        self.post, self.place, self.part, self.whole = post, place, part, whole

    def span(self, dz, other, cols, lo=0, n=ROWS):
        start = pl.multiple_of(self.place.block(dz, other) * ROWS + lo, HALF)
        return self.whole.at[self.part, pl.ds(start, n), cols]

    def send(self, dz, other, cols, to_dz, to_other, lo=0, n=ROWS):
        span = self.span(dz, other, cols, lo, n)
        return self.post.go(span, span, self.place.peer(to_dz, to_other))

    def spread(self, other, cols):
        return [self.send(0, other, cols, dz, 0) for dz in (1, 3)]

    def relay(self, other, cols, pair):
        pair[0].wait_recv()
        first = self.send(3, other, cols, 1, 0, 0, HALF)
        pair[1].wait_recv()
        return [first, self.send(1, other, cols, 3, 0, HALF, HALF)]

    def stage0(self):
        self.cross_left = self.send(0, 0, LEFT, 0, 1)
        self.right = self.spread(0, RIGHT)
        self.cross_right = [self.send(0, 0, RIGHT, 0, 1)]
        self.left = self.spread(0, LEFT)

    def stage1(self):
        self.right_far = self.relay(0, RIGHT, self.right)
        for dz in (3, 1):
            self.cross_right.append(self.send(dz, 0, RIGHT, 0, 1))

    def stage2(self):
        self.cross_left.wait_recv()
        self.left_other = self.spread(1, LEFT)

    def stage3(self):
        self.left_far = self.relay(0, LEFT, self.left)

    def stage4(self):
        for copy in self.right_far:
            copy.wait_recv()
        self.cross_right.append(self.send(2, 0, RIGHT, 0, 1))

    def stage5(self):
        self.left_far += self.relay(1, LEFT, self.left_other)

    def stage6(self):
        for copy in self.left_far + self.cross_right:
            copy.wait_recv()


def greet(place):
    barrier = pltpu.get_barrier_semaphore()
    for dz in range(4):
        for other in range(2):
            if (dz, other) != (0, 0):
                pl.semaphore_signal(
                    barrier, inc=1, device_id=place.peer(dz, other), device_id_type=MESH
                )
    return barrier


def run_reduces(first, second, done):
    first.stage1()
    second.stage1()
    first.stage2()
    first.stage3()
    second.stage2()
    first.stage4()
    second.stage3()
    left = first.stage5()
    right = first.stage6()
    done(0, left, right)
    second.stage4()
    left = second.stage5()
    right = second.stage6()
    done(1, left, right)


def forward_kernel(
    offs, wts, par, obj, proj, par_all,
    opad, lift, t0, t1, dbuf, hs, hr, fs, fr, xs, xr,
    load_sem, sends, recvs,
):
    place = Place()
    barrier = greet(place)
    load = pltpu.make_async_copy(obj, opad.at[:, pl.ds(PAD, GRID), :], load_sem)
    load.start()
    opad[:, :PAD, :] = jnp.zeros((2, PAD, GRID), BF16)
    opad[:, PAD + GRID :, :] = jnp.zeros((2, PAD, GRID), BF16)
    lift[:, :PAD] = jnp.zeros((2 * ROWS, PAD), BF16)
    lift[:, PAD + GRID :] = jnp.zeros((2 * ROWS, PAD), BF16)
    off_y = offs[0]
    off_x = offs[1]
    t0[...] = band(t0.shape, 0, (off_y + PAD - 1).astype(F32), [wts[t] for t in range(4)], 1)
    t1[...] = band(t1.shape, 1, (off_x + PAD - 1).astype(F32), [wts[4 + t] for t in range(4)], 1)
    load.wait()

    par_all[pl.ds(place.me, 1)] = par[...][None]
    pl.semaphore_wait(barrier, NSLAB - 1)
    post = Post(sends, recvs)
    par_copies = []
    for dz in range(4):
        for other in range(2):
            if (dz, other) != (0, 0):
                span = par_all.at[place.me]
                par_copies.append(post.go(span, span, place.peer(dz, other)))

    def slot(dz, other):
        return 2 * dz + other

    def project(dz, other):
        start = pl.multiple_of(place.block(dz, other) * ROWS, ROWS)
        for part in range(2):
            rows = opad[part, pl.ds(start, 3 * PAD), :]
            lift[part * ROWS : (part + 1) * ROWS, PAD : PAD + GRID] = dot(t0[...], rows).astype(BF16)
        for q in range(GRID // 256):
            tile = dot(lift[:, 256 * q : 256 * q + 512], t1[...])
            dbuf[slot(dz, other), :, :, 256 * q : 256 * q + 256] = tile.reshape(2, ROWS, 256)

    bufs = (hs, hr, fs, fr, xs, xr)
    reduces = []
    for part in range(2):

        def own(dz, other, lo, n, cols, part=part):
            return dbuf[slot(dz, other), part, pl.ds(lo, n), cols]

        def ref(dz, other, lo, n, cols, room, part=part):
            room[...] = encode_fine(own(dz, other, lo, n, cols, part))
            return room

        reduces.append(Reduce(post, place, part, bufs, own, ref, (encode_fine, decode_fine)))
    for dz, other in ((2, 1), (2, 0), (1, 1), (3, 1), (0, 1), (1, 0), (3, 0), (0, 0)):
        project(dz, other)
        for reduce in reduces:
            if dz == 2:
                reduce.start_far(other)
            if other == 1:
                reduce.start_cross(dz)
    rows = pl.ds(pl.multiple_of(place.block(0, 0) * ROWS, ROWS), ROWS)
    gathers = [Gather(post, place, part, proj) for part in range(2)]

    def done(part, left, right):
        proj[part, rows, LEFT] = encode_fine(left)
        proj[part, rows, RIGHT] = encode_fine(right)
        gathers[part].stage0()

    run_reduces(reduces[0], reduces[1], done)
    for k in range(1, 7):
        for gather in gathers:
            getattr(gather, "stage%d" % k)()
    for copy in par_copies:
        copy.wait_recv()
    post.finish()


def forward(offs, wts, par, obj):
    return pl.pallas_call(
        forward_kernel,
        out_shape=(
            jax.ShapeDtypeStruct((2, GRID, GRID), BF16),
            jax.ShapeDtypeStruct((NSLAB, 16, 512), F32),
        ),
        in_specs=[
            pl.BlockSpec(memory_space=pltpu.SMEM),
            pl.BlockSpec(memory_space=pltpu.SMEM),
            pl.BlockSpec(memory_space=pltpu.VMEM),
            pl.BlockSpec(memory_space=pl.ANY),
        ],
        out_specs=(
            pl.BlockSpec(memory_space=pltpu.VMEM),
            pl.BlockSpec(memory_space=pltpu.VMEM),
        ),
        scratch_shapes=[
            pltpu.VMEM((2, GRID + 2 * PAD, GRID), BF16),
            pltpu.VMEM((2 * ROWS, GRID + 2 * PAD), BF16),
            pltpu.VMEM((ROWS, 3 * PAD), BF16),
            pltpu.VMEM((512, 256), BF16),
            pltpu.VMEM((NSLAB, 2, ROWS, GRID), F32),
        ]
        + reduce_scratch()
        + [
            pltpu.SemaphoreType.DMA,
            pltpu.SemaphoreType.DMA((96,)),
            pltpu.SemaphoreType.DMA((96,)),
        ],
        compiler_params=pltpu.CompilerParams(
            collective_id=0, has_side_effects=True, vmem_limit_bytes=VMEM_LIMIT
        ),
        name="forward",
    )(offs, wts, par, obj)


def dft_tables():
    index = np.arange(PATCH)
    phase = 2.0 * np.pi * ((index[:, None] * index[None, :]) % PATCH) / PATCH
    cosines = np.cos(phase) / math.sqrt(PATCH)
    sines = np.sin(phase) / math.sqrt(PATCH)
    whole = np.block([[cosines, -sines], [sines, cosines]]).astype(np.float32)
    high = whole.astype(jnp.bfloat16)
    low = (whole - high.astype(np.float32)).astype(jnp.bfloat16)
    across = np.concatenate([high, high, low], axis=0)
    down = np.concatenate([high.T, high.T, low.T], axis=1)
    return [np.ascontiguousarray(t) for t in (down, across, high, high.T)]


def split_join(values, axis):
    high = values.astype(BF16)
    low = (values - high.astype(F32)).astype(BF16)
    return jnp.concatenate([high, low, high], axis=axis)


CHUNKS = 8
CHUNK = GRID // CHUNKS


def slots_kernel(
    corners, count, proj, probe, diff, *refs,
):
    tables, refs = refs[:4], refs[4:]
    image, probe_part, proj_in, diff_in = refs[:4]
    left_f, right_f, left_i, right_i, wide, total, image_out, in_sem, out_sem, sem = refs[4:]

    def chunk_rows(k):
        return pl.ds(pl.multiple_of(k * CHUNK, CHUNK), CHUNK)

    def load(k):
        rows = chunk_rows(k)
        return pltpu.make_async_copy(proj.at[:, rows, :], proj_in.at[:, rows, :], in_sem.at[k])

    def store(k):
        rows = chunk_rows(k)
        return pltpu.make_async_copy(image_out.at[:, rows, :], image.at[:, rows, :], out_sem.at[k])

    for k in range(CHUNKS):
        load(k).start()
    later = [
        pltpu.make_async_copy(src, dst, sem.at[k])
        for k, (src, dst) in enumerate(
            zip(tables + (diff,), (left_f, right_f, left_i, right_i, diff_in))
        )
    ]
    for copy in later:
        copy.start()
    probe_part[...] = jnp.zeros(probe_part.shape, F32)

    def open_chunk(k, carry):
        rows = chunk_rows(k)
        for tile in range(GRID // 128 + 1):
            total[:, tile, rows, :] = jnp.zeros((2, CHUNK, 128), F32)
        load(k).wait()
        for tile in range(GRID // 128):
            wide[:, tile, rows, :] = decode_fine(proj_in[:, rows, 128 * tile : 128 * tile + 128])
        return carry

    lax.fori_loop(0, CHUNKS, open_chunk, 0)
    for copy in later:
        copy.wait()
    live = count[0]
    lane = lax.broadcasted_iota(jnp.int32, (PATCH, 128), 1)
    zero = jnp.zeros((PATCH, 128), F32)
    probe_re = probe[0]
    probe_im = probe[1]

    def pair_step(pair, carry):
        waves = []
        places = []
        for k in range(2):
            slot = 2 * pair + k
            row = corners[slot, 0]
            col = corners[slot, 1]
            turn = lax.rem(col, 128)
            tile = col // 128
            early = lane < turn
            patch = []
            for part in range(2):
                window = [wide[part, tile + m, pl.ds(row, PATCH), :] for m in range(3)]
                joined = jnp.concatenate(
                    [jnp.where(early, window[2], window[0]), window[1]], axis=1
                )
                patch.append(pltpu.roll(joined, lax.rem(PATCH - turn, PATCH), 1))
            places.append((slot, row, turn, tile, early, patch))
            waves.append(
                jnp.concatenate(
                    [
                        probe_re * patch[0] - probe_im * patch[1],
                        probe_re * patch[1] + probe_im * patch[0],
                    ],
                    axis=0,
                )
            )
        half = dot(left_f[...], split_join(jnp.concatenate(waves, axis=1), 0))
        half = jnp.concatenate(
            [
                jnp.concatenate([half[:PATCH, cols], half[PATCH:, cols]], axis=1)
                for cols in (slice(0, PATCH), slice(PATCH, 2 * PATCH))
            ],
            axis=0,
        )
        far = dot(split_join(half, 1), right_f[...])
        resid = []
        for k in range(2):
            slot = places[k][0]
            far_re = far[PATCH * k : PATCH * k + PATCH, :PATCH]
            far_im = far[PATCH * k : PATCH * k + PATCH, PATCH:]
            weight = jnp.where(slot < live, 1.0 / math.sqrt(POSITIONS), 0.0)
            misfit = (far_re * far_re + far_im * far_im - diff_in[slot]) * weight
            resid.append(
                jnp.concatenate(
                    [(misfit * far_re).astype(BF16), (misfit * far_im).astype(BF16)], axis=0
                )
            )
        inner = dot(left_i[...], jnp.concatenate(resid, axis=1)).astype(BF16)
        inner = jnp.concatenate(
            [
                jnp.concatenate([inner[:PATCH, cols], inner[PATCH:, cols]], axis=1)
                for cols in (slice(0, PATCH), slice(PATCH, 2 * PATCH))
            ],
            axis=0,
        )
        chi = dot(inner, right_i[...])
        for k in range(2):
            slot, row, turn, tile, early, patch = places[k]
            chi_re = chi[PATCH * k : PATCH * k + PATCH, :PATCH]
            chi_im = chi[PATCH * k : PATCH * k + PATCH, PATCH:]
            probe_part[0] += patch[0] * chi_re + patch[1] * chi_im
            probe_part[1] += patch[0] * chi_im - patch[1] * chi_re
            grads = (
                probe_re * chi_re + probe_im * chi_im,
                probe_re * chi_im - probe_im * chi_re,
            )
            for part in range(2):
                turned = pltpu.roll(grads[part], turn, 1)
                head = turned[:, :128]
                spread = (
                    jnp.where(early, zero, head), turned[:, 128:], jnp.where(early, head, zero)
                )
                for m in range(3):
                    total[part, tile + m, pl.ds(row, PATCH), :] += spread[m]
        return carry

    lax.fori_loop(0, (live + 1) // 2, pair_step, 0)

    def close_chunk(k, carry):
        rows = chunk_rows(k)
        for tile in range(GRID // 128):
            image_out[:, rows, 128 * tile : 128 * tile + 128] = encode(total[:, tile, rows, :])
        store(k).start()
        return carry

    lax.fori_loop(0, CHUNKS, close_chunk, 0)
    for k in range(CHUNKS):
        store(k).wait()


def slots(corners, count, proj, probe, diffraction):
    tables = [jnp.asarray(t) for t in dft_tables()]
    whole = pl.BlockSpec(memory_space=pltpu.VMEM)
    scalar = pl.BlockSpec(memory_space=pltpu.SMEM)
    far = pl.BlockSpec(memory_space=pl.ANY)
    dma = pltpu.SemaphoreType.DMA
    return pl.pallas_call(
        slots_kernel,
        out_shape=(
            jax.ShapeDtypeStruct((2, GRID, GRID), BF16),
            jax.ShapeDtypeStruct((2, PATCH, PATCH), F32),
        ),
        in_specs=[scalar, scalar, far, whole, far] + [far] * 4,
        out_specs=(far, whole),
        scratch_shapes=[
            pltpu.VMEM((2, GRID, GRID), BF16),
            pltpu.VMEM((SLOTS, PATCH, PATCH), F32),
            pltpu.VMEM((512, 1536), BF16),
            pltpu.VMEM((1536, 512), BF16),
            pltpu.VMEM((512, 512), BF16),
            pltpu.VMEM((512, 512), BF16),
            pltpu.VMEM((2, GRID // 128 + 1, GRID, 128), F32),
            pltpu.VMEM((2, GRID // 128 + 1, GRID, 128), F32),
            pltpu.VMEM((2, GRID, GRID), BF16),
            dma((CHUNKS,)), dma((CHUNKS,)), dma((5,)),
        ],
        compiler_params=pltpu.CompilerParams(vmem_limit_bytes=VMEM_LIMIT),
        name="slots",
    )(corners, count, proj, probe, diffraction, *tables)


def backward_kernel(
    image, par_all, probe_part, result, probe_out,
    t0, t1, ext, padded, gbuf, cbuf, hbuf, bbuf, xsend, xrecv, fin,
    pcode, pbuf, pcore, py, pxl, psum, hs, hr, fs, fr, xs, xr,
    sends, recvs, fsend, frecv,
):
    place = Place()
    ang, me, z, xh = place.ang, place.me, place.z, place.xh
    core = lax.rem(ang, 2)
    chip = ang // 2
    y = lax.rem(chip, 4)
    xl = chip // 4
    mine = place.block(0, 0)

    def ang_id(xl_, y_, core_):
        return (xl_ * 4 + y_) * 2 + core_

    def y_peer(dy):
        return (ang_id(xl, lax.rem(y + dy, 4), core), me)

    xl_peer = (ang_id(1 - xl, y, core), me)
    core_peer = (ang_id(xl, y, 1 - core), me)
    turn_peer = (ang_id(xh, z, core), y * 2 + xl)
    stays = jnp.logical_and(xl == xh, y == z)
    above = (ang, slab_of(lax.rem(mine + NSLAB - 1, NSLAB)))
    below = (ang, slab_of(lax.rem(mine + 1, NSLAB)))

    barrier = greet(place)
    for peer in (y_peer(1), y_peer(2), y_peer(3), xl_peer, core_peer):
        pl.semaphore_signal(barrier, inc=1, device_id=peer, device_id_type=MESH)

    @pl.when(jnp.logical_not(stays))
    def _():
        pl.semaphore_signal(barrier, inc=1, device_id=turn_peer, device_id_type=MESH)

    def tables(s, carry):
        rows = [par_all[s, k : k + 1, :] for k in range(10)]
        t0[pl.ds(pl.multiple_of(s * ROWS, ROWS), ROWS), :] = band(
            (ROWS, 384), 0, HALO + 1 - rows[8][:, :384], [r[:, :384] for r in rows[:4]], -1
        )
        t1[s] = band((512, 256), 1, PAD + 1 - rows[9][:, :256], [r[:, :256] for r in rows[4:8]], -1)
        return carry

    lax.fori_loop(0, NSLAB, tables, 0)
    ext[:, HALO + ROWS + HALO :, :] = jnp.zeros((2, 384 - ROWS - 2 * HALO, GRID), BF16)
    padded[:, :PAD] = jnp.zeros((NSLAB * ROWS, PAD), BF16)
    padded[:, PAD + GRID :] = jnp.zeros((NSLAB * ROWS, PAD), BF16)
    pl.semaphore_wait(barrier, NSLAB - 1 + 5 + jnp.where(stays, 0, 1))

    post = Post(sends, recvs)
    peers = [(dz, other) for dz in range(4) for other in range(2)][1:]
    bufs = (hs, hr, fs, fr, xs, xr)
    reduces = []
    for part in range(2):

        def ref(dz, other, lo, n, cols, room, part=part):
            start = pl.multiple_of(place.block(dz, other) * ROWS + lo, HALF)
            return image.at[part, pl.ds(start, n), cols]

        def own(dz, other, lo, n, cols, part=part, ref=ref):
            return decode(ref(dz, other, lo, n, cols, None)[...])

        reduces.append(Reduce(post, place, part, bufs, own, ref, (encode, decode)))
    first, second = reduces

    def open_reduce(reduce):
        for dz in (2, 1, 3, 0):
            reduce.start_cross(dz)
            if dz == 2:
                reduce.start_far(1)
                reduce.start_far(0)

    halos = {}

    def finish_reduce(part, reduce):
        ext[part, HALO : HALO + ROWS, LEFT] = reduce.stage5().astype(BF16)
        ext[part, HALO : HALO + ROWS, RIGHT] = reduce.stage6().astype(BF16)
        halos[part] = [
            post.go(ext.at[part, pl.ds(HALO, HALO), :], ext.at[part, pl.ds(HALO + ROWS, HALO), :], above),
            post.go(ext.at[part, pl.ds(ROWS, HALO), :], ext.at[part, pl.ds(0, HALO), :], below),
        ]

    chips = {0: [], 1: []}

    def spread_slices(part):
        for copy in halos[part]:
            copy.wait_recv()

        @pl.when(mine == 0)
        def _():
            ext[part, :HALO, :] = jnp.zeros((HALO, GRID), BF16)

        @pl.when(mine == NSLAB - 1)
        def _():
            ext[part, HALO + ROWS : 2 * HALO + ROWS, :] = jnp.zeros((HALO, GRID), BF16)

        for q in range(GRID // 256):
            cols = pl.ds(256 * q, 256)
            padded[:, PAD + 256 * q : PAD + 256 * q + 256] = dot(t0[...], ext[part, :, cols]).astype(BF16)

        cores = {}

        def slice_step(j):
            dy, other = j // 2, j % 2
            s = lax.rem(y + dy, 4) * 2 + (1 - xl if other else xl)
            rows = pl.ds(pl.multiple_of(s * ROWS, ROWS), ROWS)
            stack = jnp.concatenate(
                [padded[rows, 256 * q : 256 * q + 512] for q in range(GRID // 256)], axis=0
            )
            tiles = encode(dot(stack, t1[s]))
            for q in range(GRID // 256):
                cols = slice(256 * q, 256 * q + 256)
                for half in range(2):
                    lo = ROWS * q + HALF * half
                    gbuf[part, half, j, :, cols] = tiles[lo : lo + HALF]
            cores[j] = post.go(gbuf.at[part, 1 - core, j], cbuf.at[part, j], core_peer)

        def combine(j):
            cores[j].wait_recv()
            dy, other = j // 2, j % 2
            both = decode(gbuf[part, core, j]) + decode(cbuf[part, j])
            hbuf[part, dy, other] = encode(both)
            if dy:
                span = hbuf.at[part, dy, other]
                chips[part].append(post.go(span, bbuf.at[part, dy, other], y_peer(dy)))

        order = (5, 4, 3, 7, 2, 6, 1, 0)
        for k, j in enumerate(order):
            slice_step(j)
            if k >= 2:
                combine(order[k - 2])
        combine(order[-2])
        combine(order[-1])

    def turn_copy(part):
        return pltpu.make_async_remote_copy(
            src_ref=fin.at[part], dst_ref=result.at[part], send_sem=fsend.at[part],
            recv_sem=frecv.at[part], device_id=turn_peer, device_id_type=MESH,
        )

    sides = {}

    def y_total(part, other):
        total = decode(hbuf[part, 0, other])
        for dy in range(1, 4):
            total = total + decode(bbuf[part, dy, other])
        return total

    def settle_y(part):
        for copy in chips[part]:
            copy.wait_recv()
        xsend[part] = encode(y_total(part, 1))
        sides[part] = post.go(xsend.at[part], xrecv.at[part], xl_peer)

    def settle(part):
        mine_total = y_total(part, 0)
        sides[part].wait_recv()
        fin[part] = encode(mine_total + decode(xrecv[part]))

        @pl.when(stays)
        def _():
            result[part] = fin[part]

        @pl.when(jnp.logical_not(stays))
        def _():
            turn_copy(part).start()

    open_reduce(first)
    first.stage1()
    open_reduce(second)
    pcode[...] = encode(probe_part[...])
    probe_copies = []
    for dz, other in peers:
        rows = pl.ds(pl.multiple_of(place.slab(dz, other) * 64, 64), 64)
        probe_copies.append(post.go(pcode.at[rows, :], pbuf.at[2 * dz + other], place.peer(dz, other)))
    first.stage2()
    first.stage3()
    first.stage4()
    second.stage1()
    second.stage2()
    finish_reduce(0, first)
    second.stage3()
    second.stage4()

    total = probe_part[pl.ds(pl.multiple_of(me * 64, 64), 64), :]
    for copy, (dz, other) in zip(probe_copies, peers):
        copy.wait_recv()
        total = total + decode(pbuf[2 * dz + other])
    psum[0] = encode(total)
    core_probe = post.go(psum.at[0], pcore, core_peer)

    spread_slices(0)
    core_probe.wait_recv()
    psum[1] = encode(decode(psum[0]) + decode(pcore[...]))
    y_copies = [
        post.go(psum.at[1], py.at[j], y_peer(j)) for j in range(1, 4)
    ]
    finish_reduce(1, second)
    for copy in y_copies:
        copy.wait_recv()
    psum[2] = encode((decode(psum[1]) + decode(py[1])) + (decode(py[2]) + decode(py[3])))
    xl_probe = post.go(psum.at[2], pxl, xl_peer)
    spread_slices(1)
    xl_probe.wait_recv()
    span = probe_out.at[pl.ds(pl.multiple_of(me * 64, 64), 64), :]
    span[...] = encode(decode(psum[2]) + decode(pxl[...]))
    out_copies = [post.go(span, span, place.peer(*peer)) for peer in peers]
    settle_y(0)
    settle(0)
    settle_y(1)
    settle(1)
    for copy in out_copies:
        copy.wait_recv()

    @pl.when(jnp.logical_not(stays))
    def _():
        turn_copy(0).wait()
        turn_copy(1).wait()

    post.finish()


def backward(image, par_all, probe_part):
    whole = pl.BlockSpec(memory_space=pltpu.VMEM)
    dma = pltpu.SemaphoreType.DMA
    return pl.pallas_call(
        backward_kernel,
        out_shape=(
            jax.ShapeDtypeStruct((2, HALF, GRID), BF16),
            jax.ShapeDtypeStruct((2 * PATCH, PATCH), BF16),
        ),
        in_specs=[whole] * 3,
        out_specs=(whole, whole),
        scratch_shapes=[
            pltpu.VMEM((NSLAB * ROWS, 384), BF16),
            pltpu.VMEM((NSLAB, 512, 256), BF16),
            pltpu.VMEM((2, 384, GRID), BF16),
            pltpu.VMEM((NSLAB * ROWS, GRID + 2 * PAD), BF16),
            pltpu.VMEM((2, 2, NSLAB, HALF, GRID), BF16),
            pltpu.VMEM((2, NSLAB, HALF, GRID), BF16),
            pltpu.VMEM((2, 4, 2, HALF, GRID), BF16),
            pltpu.VMEM((2, 4, 2, HALF, GRID), BF16),
            pltpu.VMEM((2, HALF, GRID), BF16),
            pltpu.VMEM((2, HALF, GRID), BF16),
            pltpu.VMEM((2, HALF, GRID), BF16),
            pltpu.VMEM((2 * PATCH, PATCH), BF16),
            pltpu.VMEM((NSLAB, 64, PATCH), BF16),
            pltpu.VMEM((64, PATCH), BF16),
            pltpu.VMEM((4, 64, PATCH), BF16),
            pltpu.VMEM((64, PATCH), BF16),
            pltpu.VMEM((3, 64, PATCH), BF16),
        ]
        + reduce_scratch()
        + [dma((96,)), dma((96,)), dma((2,)), dma((2,))],
        compiler_params=pltpu.CompilerParams(
            collective_id=1, has_side_effects=True, vmem_limit_bytes=VMEM_LIMIT
        ),
        name="backward",
    )(image, par_all, probe_part)


def per_device(
    object_field, probe_field, diffraction, scan_offsets, counts, band_weights, band_offsets
):
    ang = lax.axis_index("ang")
    weights = lax.dynamic_index_in_dim(band_weights, ang, 0, keepdims=False)[0]
    offsets = lax.dynamic_index_in_dim(band_offsets, ang, 0, keepdims=False)[0]
    weights = weights.astype(F32).reshape(8)
    par = jnp.concatenate([weights, offsets.astype(F32), jnp.zeros((6,), F32)])
    par = jnp.broadcast_to(par[:, None], (16, 512))
    proj, par_all = forward(offsets, weights, par, object_field.reshape(2, GRID, GRID))
    image, probe_part = slots(
        scan_offsets[0, 0], counts[0], proj, probe_field, diffraction[0, 0]
    )
    result, probe_out = backward(image, par_all, probe_part.reshape(2 * PATCH, PATCH))
    object_grad = decode(jnp.transpose(result, (1, 0, 2)))[:, :, None, :]
    return (object_grad, decode(probe_out).reshape(2, PATCH, PATCH))


def solution(mesh):
    placed = (
        P(None, "slab", None, None),
        P(),
        P("ang", "slab", None, None, None),
        P("ang", "slab", None, None),
        P("slab", "ang"),
        P(None, "slab", None, None),
        P(None, "slab", None),
    )
    return jax.shard_map(
        per_device,
        mesh=mesh,
        in_specs=placed,
        out_specs=(P("ang", None, "slab", None), P()),
        check_vma=False,
    )
```

```python
import functools
import math

import jax
import jax.numpy as jnp
import numpy as np
from jax import lax
from jax.experimental import pallas as pl
from jax.experimental.pallas import tpu as pltpu
from jax.sharding import PartitionSpec as P

MESH = pl.DeviceIdType.MESH
F32 = jnp.float32
BF16 = jnp.bfloat16
GRID = 1024
PATCH = 256
SLOTS = 8
NSLAB = 8
ROWS = GRID // NSLAB
HALF = ROWS // 2
PAD = 128
HALO = 80
POSITIONS = 512
ANGLES = 16
VMEM_LIMIT = 56 << 20


def block_of(slab):
    return (slab % 2) * 4 + slab // 2


def slab_of(block):
    return (block % 4) * 2 + block // 4


def band(shape, axis_out, start, weights, step):
    inner = lax.broadcasted_iota(jnp.int32, shape, 1 - axis_out)
    outer = lax.broadcasted_iota(jnp.int32, shape, axis_out)
    distance = (inner - outer).astype(F32)
    summed = jnp.zeros(shape, F32)
    for tap, weight in enumerate(weights):
        summed = jnp.where(distance == start + step * tap, weight, summed)
    return summed.astype(BF16)


def encode(values):
    return (values * jnp.abs(values)).astype(BF16)


def decode(codes):
    square = codes.astype(F32)
    return square * lax.rsqrt(jnp.maximum(jnp.abs(square), 1e-37))


def encode_fine(values):
    square = values * jnp.abs(values) * 2.0**32
    return (square * jnp.abs(square)).astype(BF16)


def decode_fine(codes):
    fourth = codes.astype(F32)
    square = fourth * lax.rsqrt(jnp.maximum(jnp.abs(fourth), 1e-37))
    return square * (lax.rsqrt(jnp.maximum(jnp.abs(square), 1e-30)) * 2.0**-16)


def dot(left, right):
    return jnp.dot(left, right, preferred_element_type=F32)


WIDE = GRID // 2
LEFT = pl.ds(0, WIDE)
RIGHT = pl.ds(WIDE, WIDE)


class Post:
    def __init__(self, sends, recvs):
        self.sends = sends
        self.recvs = recvs
        self.opened = []

    def go(self, src, dst, peer):
        k = len(self.opened)
        copy = pltpu.make_async_remote_copy(
            src_ref=src, dst_ref=dst, send_sem=self.sends.at[k], recv_sem=self.recvs.at[k],
            device_id=peer, device_id_type=MESH,
        )
        copy.start()
        self.opened.append(copy)
        return copy

    def finish(self):
        for copy in self.opened:
            copy.wait_send()


class Place:
    def __init__(self):
        self.ang = lax.axis_index("ang")
        self.me = lax.axis_index("slab")
        self.z = self.me // 2
        self.xh = self.me % 2

    def slab(self, dz, other):
        x = 1 - self.xh if other else self.xh
        return lax.rem(self.z + dz, 4) * 2 + x

    def peer(self, dz, other):
        return (self.ang, self.slab(dz, other))

    def block(self, dz, other):
        return block_of(self.slab(dz, other))


class Ring:
    def __init__(self, post, place, bufs, own, first, codec):
        self.post, self.place = post, place
        self.encode, self.decode = codec
        self.hr, self.fs, self.fr = bufs
        self.own, self.first = own, first

    def start(self):
        self.halves = [
            self.post.go(self.first(k), self.hr.at[k], self.place.peer((1, 3)[k], 0))
            for k in range(2)
        ]

    def middle(self):
        self.whole = []
        for k, dz in enumerate((1, 3)):
            lo = HALF * k
            self.fs[k, HALF - lo : ROWS - lo, :] = self.encode(self.own(dz, HALF - lo, HALF))
            self.halves[k].wait_recv()
            both = self.own(dz, lo, HALF) + self.decode(self.hr[k])
            self.fs[k, lo : lo + HALF, :] = self.encode(both)
            self.whole.append(self.post.go(self.fs.at[k], self.fr.at[k], self.place.peer(dz, 0)))

    def end(self):
        for copy in self.whole:
            copy.wait_recv()
        return self.own(0, 0, ROWS) + self.decode(self.fr[0]) + self.decode(self.fr[1])


class Reduce:
    def __init__(self, post, place, part, bufs, own, ref, codec):
        hs, hr, fs, fr, xs, xr = bufs
        self.post, self.place, self.own, self.ref = post, place, own, ref
        self.encode, self.decode = codec
        self.hs, self.xs, self.xr = hs.at[part], xs.at[part], xr.at[part]
        self.rings = []
        for chain, other in enumerate((1, 0)):
            self.rings.append(
                Ring(
                    post, place, (hr.at[part, chain], fs.at[part, chain], fr.at[part, chain]),
                    functools.partial(self.left, other),
                    functools.partial(self.left_first, other, chain), codec,
                )
            )
        self.rings.append(
            Ring(
                post, place, (hr.at[part, 2], fs.at[part, 2], fr.at[part, 2]),
                self.right, self.right_first, codec,
            )
        )
        self.crossing = {}

    def left(self, other, dz, lo, n):
        return self.own(dz, other, lo, n, LEFT)

    def left_first(self, other, chain, k):
        return self.ref(2, other, HALF * k, HALF, LEFT, self.hs.at[chain, k])

    def right(self, dz, lo, n):
        return self.own(dz, 0, lo, n, RIGHT) + self.decode(self.xr[dz, lo : lo + n, :])

    def right_first(self, k):
        self.hs[2, k] = self.encode(self.right(2, HALF * k, HALF))
        return self.hs.at[2, k]

    def start_far(self, other):
        self.rings[1 - other].start()

    def start_cross(self, dz):
        src = self.ref(dz, 1, 0, ROWS, RIGHT, self.xs.at[dz])
        self.crossing[dz] = self.post.go(src, self.xr.at[dz], self.place.peer(0, 1))

    def stage2(self):
        self.crossing[2].wait_recv()
        self.rings[2].start()

    def stage3(self):
        self.xs[4] = self.encode(self.rings[0].end())
        self.crossing[4] = self.post.go(self.xs.at[4], self.xr.at[4], self.place.peer(0, 1))

    def stage4(self):
        self.crossing[1].wait_recv()
        self.crossing[3].wait_recv()
        self.rings[2].middle()

    def stage5(self):
        mine = self.rings[1].end()
        self.crossing[4].wait_recv()
        return mine + self.decode(self.xr[4])

    def stage6(self):
        self.crossing[0].wait_recv()
        return self.rings[2].end()


def reduce_scratch():
    code = BF16
    return [
        pltpu.VMEM((2, 3, 2, HALF, WIDE), code),
        pltpu.VMEM((2, 3, 2, HALF, WIDE), code),
        pltpu.VMEM((2, 3, 2, ROWS, WIDE), code),
        pltpu.VMEM((2, 3, 2, ROWS, WIDE), code),
        pltpu.VMEM((2, 5, ROWS, WIDE), code),
        pltpu.VMEM((2, 5, ROWS, WIDE), code),
    ]


class Gather:
    def __init__(self, post, place, part, whole):
        self.post, self.place, self.part, self.whole = post, place, part, whole

    def span(self, dz, other, cols, lo=0, n=ROWS):
        start = pl.multiple_of(self.place.block(dz, other) * ROWS + lo, HALF)
        return self.whole.at[self.part, pl.ds(start, n), cols]

    def send(self, dz, other, cols, to_dz, to_other, lo=0, n=ROWS):
        span = self.span(dz, other, cols, lo, n)
        return self.post.go(span, span, self.place.peer(to_dz, to_other))

    def spread(self, other, cols):
        return [self.send(0, other, cols, dz, 0) for dz in (1, 3)]

    def relay(self, other, cols, pair):
        pair[0].wait_recv()
        first = self.send(3, other, cols, 1, 0, 0, HALF)
        pair[1].wait_recv()
        return [first, self.send(1, other, cols, 3, 0, HALF, HALF)]

    def stage0(self):
        self.cross_left = self.send(0, 0, LEFT, 0, 1)
        self.right = self.spread(0, RIGHT)
        self.cross_right = [self.send(0, 0, RIGHT, 0, 1)]
        self.left = self.spread(0, LEFT)

    def stage1(self):
        self.right_far = self.relay(0, RIGHT, self.right)
        for dz in (3, 1):
            self.cross_right.append(self.send(dz, 0, RIGHT, 0, 1))

    def stage2(self):
        self.cross_left.wait_recv()
        self.left_other = self.spread(1, LEFT)

    def stage3(self):
        self.left_far = self.relay(0, LEFT, self.left)

    def stage4(self):
        for copy in self.right_far:
            copy.wait_recv()
        self.cross_right.append(self.send(2, 0, RIGHT, 0, 1))

    def stage5(self):
        self.left_far += self.relay(1, LEFT, self.left_other)

    def stage6(self):
        for copy in self.left_far + self.cross_right:
            copy.wait_recv()


def greet(place):
    barrier = pltpu.get_barrier_semaphore()
    for dz in range(4):
        for other in range(2):
            if (dz, other) != (0, 0):
                pl.semaphore_signal(
                    barrier, inc=1, device_id=place.peer(dz, other), device_id_type=MESH
                )
    return barrier


def follow_reduces(reduces, done):
    for reduce in reduces:
        reduce.rings[0].middle()
    for reduce in reduces:
        reduce.stage2()
        reduce.start_cross(1)
        reduce.start_cross(3)
    for reduce in reduces:
        reduce.rings[1].middle()
    for reduce in reduces:
        reduce.stage3()
    for reduce in reduces:
        reduce.stage4()
        reduce.start_cross(0)
    for part, reduce in enumerate(reduces):
        done(part, reduce.stage5(), reduce.stage6())


def forward_kernel(
    offs, wts, obj, proj, par_all,
    opad, lift, t0, t1, dbuf, hs, hr, fs, fr, xs, xr,
    load_sem, sends, recvs,
):
    place = Place()
    barrier = greet(place)
    load = pltpu.make_async_copy(obj, opad.at[:, pl.ds(PAD, GRID), :], load_sem)
    load.start()
    opad[:, :PAD, :] = jnp.zeros((2, PAD, GRID), BF16)
    opad[:, PAD + GRID :, :] = jnp.zeros((2, PAD, GRID), BF16)
    lift[:, :PAD] = jnp.zeros((2 * ROWS, PAD), BF16)
    lift[:, PAD + GRID :] = jnp.zeros((2 * ROWS, PAD), BF16)
    ang = place.ang
    off_y = offs[2 * ang].astype(F32)
    off_x = offs[2 * ang + 1].astype(F32)
    taps = [wts[8 * ang + k] for k in range(8)]
    t0[...] = band(t0.shape, 0, off_y + float(PAD - 1), taps[:4], 1)
    t1[...] = band(t1.shape, 1, off_x + float(PAD - 1), taps[4:], 1)
    row_ids = lax.broadcasted_iota(jnp.int32, par_all.shape[1:], 0)
    par = jnp.zeros(par_all.shape[1:], F32)
    for k, value in enumerate(taps + [off_y, off_x]):
        par = jnp.where(row_ids == k, value, par)
    par_all[pl.ds(place.me, 1)] = par[None]
    load.wait()

    pl.semaphore_wait(barrier, NSLAB - 1)
    post = Post(sends, recvs)
    par_copies = []
    for dz in range(4):
        for other in range(2):
            if (dz, other) != (0, 0):
                span = par_all.at[place.me]
                par_copies.append(post.go(span, span, place.peer(dz, other)))

    def slot(dz, other):
        return 2 * dz + other

    def project(dz, other):
        start = pl.multiple_of(place.block(dz, other) * ROWS, ROWS)
        for part in range(2):
            rows = opad[part, pl.ds(start, 3 * PAD), :]
            lift[part * ROWS : (part + 1) * ROWS, PAD : PAD + GRID] = dot(t0[...], rows).astype(BF16)
        for q in range(GRID // 256):
            tile = dot(lift[:, 256 * q : 256 * q + 512], t1[...])
            dbuf[slot(dz, other), :, :, 256 * q : 256 * q + 256] = tile.reshape(2, ROWS, 256)

    bufs = (hs, hr, fs, fr, xs, xr)
    reduces = []
    for part in range(2):

        def own(dz, other, lo, n, cols, part=part):
            return dbuf[slot(dz, other), part, pl.ds(lo, n), cols]

        def ref(dz, other, lo, n, cols, room, part=part):
            room[...] = encode_fine(own(dz, other, lo, n, cols, part))
            return room

        reduces.append(Reduce(post, place, part, bufs, own, ref, (encode_fine, decode_fine)))
    for dz, other in ((2, 1), (2, 0), (1, 1), (3, 1), (0, 1), (1, 0), (3, 0), (0, 0)):
        project(dz, other)
        for reduce in reduces:
            if dz == 2:
                reduce.start_far(other)
                if other == 1:
                    reduce.start_cross(2)
    rows = pl.ds(pl.multiple_of(place.block(0, 0) * ROWS, ROWS), ROWS)
    gathers = [Gather(post, place, part, proj) for part in range(2)]

    def done(part, left, right):
        proj[part, rows, LEFT] = encode_fine(left)
        proj[part, rows, RIGHT] = encode_fine(right)
        gathers[part].stage0()

    follow_reduces(reduces, done)
    for k in range(1, 7):
        for gather in gathers:
            getattr(gather, "stage%d" % k)()
    for copy in par_copies:
        copy.wait_recv()
    post.finish()


def forward(offs, wts, obj):
    return pl.pallas_call(
        forward_kernel,
        out_shape=(
            jax.ShapeDtypeStruct((2, GRID, GRID), BF16),
            jax.ShapeDtypeStruct((NSLAB, 16, 512), F32),
        ),
        in_specs=[
            pl.BlockSpec(memory_space=pltpu.SMEM),
            pl.BlockSpec(memory_space=pltpu.SMEM),
            pl.BlockSpec(memory_space=pl.ANY),
        ],
        out_specs=(
            pl.BlockSpec(memory_space=pltpu.VMEM),
            pl.BlockSpec(memory_space=pltpu.VMEM),
        ),
        scratch_shapes=[
            pltpu.VMEM((2, GRID + 2 * PAD, GRID), BF16),
            pltpu.VMEM((2 * ROWS, GRID + 2 * PAD), BF16),
            pltpu.VMEM((ROWS, 3 * PAD), BF16),
            pltpu.VMEM((512, 256), BF16),
            pltpu.VMEM((NSLAB, 2, ROWS, GRID), F32),
        ]
        + reduce_scratch()
        + [
            pltpu.SemaphoreType.DMA,
            pltpu.SemaphoreType.DMA((96,)),
            pltpu.SemaphoreType.DMA((96,)),
        ],
        compiler_params=pltpu.CompilerParams(
            collective_id=0, has_side_effects=True, vmem_limit_bytes=VMEM_LIMIT
        ),
        name="forward",
    )(offs, wts, obj)


def dft_tables():
    index = np.arange(PATCH)
    phase = 2.0 * np.pi * ((index[:, None] * index[None, :]) % PATCH) / PATCH
    cosines = np.cos(phase) / math.sqrt(PATCH)
    sines = np.sin(phase) / math.sqrt(PATCH)
    whole = np.block([[cosines, -sines], [sines, cosines]]).astype(np.float32)
    high = whole.astype(jnp.bfloat16)
    low = (whole - high.astype(np.float32)).astype(jnp.bfloat16)
    across = np.concatenate([high, high, low], axis=0)
    down = np.concatenate([high.T, high.T, low.T], axis=1)
    return [np.ascontiguousarray(t) for t in (down, across, high, high.T)]


def split_join(values, axis):
    high = values.astype(BF16)
    low = (values - high.astype(F32)).astype(BF16)
    return jnp.concatenate([high, low, high], axis=axis)


CHUNKS = 8
CHUNK = GRID // CHUNKS


def slots_kernel(
    corners, count, proj, probe, diff, *refs,
):
    tables, refs = refs[:4], refs[4:]
    image, probe_part, proj_in, diff_in = refs[:4]
    left_f, right_f, left_i, right_i, wide, total, image_out, in_sem, out_sem, sem = refs[4:]

    def chunk_rows(k):
        return pl.ds(pl.multiple_of(k * CHUNK, CHUNK), CHUNK)

    def load(k):
        rows = chunk_rows(k)
        return pltpu.make_async_copy(proj.at[:, rows, :], proj_in.at[:, rows, :], in_sem.at[k])

    def store(k):
        rows = chunk_rows(k)
        return pltpu.make_async_copy(image_out.at[:, rows, :], image.at[:, rows, :], out_sem.at[k])

    for k in range(CHUNKS):
        load(k).start()
    later = [
        pltpu.make_async_copy(src, dst, sem.at[k])
        for k, (src, dst) in enumerate(
            zip(tables + (diff,), (left_f, right_f, left_i, right_i, diff_in))
        )
    ]
    for copy in later:
        copy.start()
    probe_part[...] = jnp.zeros(probe_part.shape, F32)

    def open_chunk(k, carry):
        rows = chunk_rows(k)
        for tile in range(GRID // 128 + 1):
            total[:, tile, rows, :] = jnp.zeros((2, CHUNK, 128), F32)
        load(k).wait()
        for tile in range(GRID // 128):
            wide[:, tile, rows, :] = decode_fine(proj_in[:, rows, 128 * tile : 128 * tile + 128])
        return carry

    lax.fori_loop(0, CHUNKS, open_chunk, 0)
    for copy in later:
        copy.wait()
    live = count[0]
    lane = lax.broadcasted_iota(jnp.int32, (PATCH, 128), 1)
    zero = jnp.zeros((PATCH, 128), F32)
    probe_re = probe[0]
    probe_im = probe[1]

    def pair_step(pair, carry):
        waves = []
        places = []
        for k in range(2):
            slot = 2 * pair + k
            row = corners[2 * slot]
            col = corners[2 * slot + 1]
            turn = lax.rem(col, 128)
            tile = col // 128
            early = lane < turn
            patch = []
            for part in range(2):
                window = [wide[part, tile + m, pl.ds(row, PATCH), :] for m in range(3)]
                joined = jnp.concatenate(
                    [jnp.where(early, window[2], window[0]), window[1]], axis=1
                )
                patch.append(pltpu.roll(joined, lax.rem(PATCH - turn, PATCH), 1))
            places.append((slot, row, turn, tile, early, patch))
            waves.append(
                jnp.concatenate(
                    [
                        probe_re * patch[0] - probe_im * patch[1],
                        probe_re * patch[1] + probe_im * patch[0],
                    ],
                    axis=0,
                )
            )
        half = dot(left_f[...], split_join(jnp.concatenate(waves, axis=1), 0))
        half = jnp.concatenate(
            [
                jnp.concatenate([half[:PATCH, cols], half[PATCH:, cols]], axis=1)
                for cols in (slice(0, PATCH), slice(PATCH, 2 * PATCH))
            ],
            axis=0,
        )
        far = dot(split_join(half, 1), right_f[...])
        resid = []
        for k in range(2):
            slot = places[k][0]
            far_re = far[PATCH * k : PATCH * k + PATCH, :PATCH]
            far_im = far[PATCH * k : PATCH * k + PATCH, PATCH:]
            weight = jnp.where(slot < live, 1.0 / math.sqrt(POSITIONS), 0.0)
            misfit = (far_re * far_re + far_im * far_im - diff_in[slot]) * weight
            resid.append(
                jnp.concatenate(
                    [(misfit * far_re).astype(BF16), (misfit * far_im).astype(BF16)], axis=0
                )
            )
        inner = dot(left_i[...], jnp.concatenate(resid, axis=1)).astype(BF16)
        inner = jnp.concatenate(
            [
                jnp.concatenate([inner[:PATCH, cols], inner[PATCH:, cols]], axis=1)
                for cols in (slice(0, PATCH), slice(PATCH, 2 * PATCH))
            ],
            axis=0,
        )
        chi = dot(inner, right_i[...])
        for k in range(2):
            slot, row, turn, tile, early, patch = places[k]
            chi_re = chi[PATCH * k : PATCH * k + PATCH, :PATCH]
            chi_im = chi[PATCH * k : PATCH * k + PATCH, PATCH:]
            probe_part[0] += patch[0] * chi_re + patch[1] * chi_im
            probe_part[1] += patch[0] * chi_im - patch[1] * chi_re
            grads = (
                probe_re * chi_re + probe_im * chi_im,
                probe_re * chi_im - probe_im * chi_re,
            )
            for part in range(2):
                turned = pltpu.roll(grads[part], turn, 1)
                head = turned[:, :128]
                spread = (
                    jnp.where(early, zero, head), turned[:, 128:], jnp.where(early, head, zero)
                )
                for m in range(3):
                    total[part, tile + m, pl.ds(row, PATCH), :] += spread[m]
        return carry

    lax.fori_loop(0, (live + 1) // 2, pair_step, 0)

    def close_chunk(k, carry):
        rows = chunk_rows(k)
        for tile in range(GRID // 128):
            image_out[:, rows, 128 * tile : 128 * tile + 128] = encode(total[:, tile, rows, :])
        store(k).start()
        return carry

    lax.fori_loop(0, CHUNKS, close_chunk, 0)
    for k in range(CHUNKS):
        store(k).wait()


def slots(corners, count, proj, probe, diffraction):
    tables = [jnp.asarray(t) for t in dft_tables()]
    whole = pl.BlockSpec(memory_space=pltpu.VMEM)
    scalar = pl.BlockSpec(memory_space=pltpu.SMEM)
    far = pl.BlockSpec(memory_space=pl.ANY)
    dma = pltpu.SemaphoreType.DMA
    return pl.pallas_call(
        slots_kernel,
        out_shape=(
            jax.ShapeDtypeStruct((2, GRID, GRID), BF16),
            jax.ShapeDtypeStruct((2, PATCH, PATCH), F32),
        ),
        in_specs=[scalar, scalar, far, whole, far] + [far] * 4,
        out_specs=(far, whole),
        scratch_shapes=[
            pltpu.VMEM((2, GRID, GRID), BF16),
            pltpu.VMEM((SLOTS, PATCH, PATCH), F32),
            pltpu.VMEM((512, 1536), BF16),
            pltpu.VMEM((1536, 512), BF16),
            pltpu.VMEM((512, 512), BF16),
            pltpu.VMEM((512, 512), BF16),
            pltpu.VMEM((2, GRID // 128 + 1, GRID, 128), F32),
            pltpu.VMEM((2, GRID // 128 + 1, GRID, 128), F32),
            pltpu.VMEM((2, GRID, GRID), BF16),
            dma((CHUNKS,)), dma((CHUNKS,)), dma((5,)),
        ],
        compiler_params=pltpu.CompilerParams(vmem_limit_bytes=VMEM_LIMIT),
        name="slots",
    )(corners, count, proj, probe, diffraction, *tables)


def backward_kernel(
    image, par_all, probe_part, result, probe_out,
    t0, t1, ext, padded, gbuf, cbuf, yhs, yhr, yfs, yfr, xsend, xrecv, keep, fin, landed,
    pcode, pall, pbuf, pcore, py, pxl, psum, hs, hr, fs, fr, xs, xr,
    sends, recvs, fsend, frecv,
):
    place = Place()
    ang, me, z, xh = place.ang, place.me, place.z, place.xh
    core = lax.rem(ang, 2)
    chip = ang // 2
    y = lax.rem(chip, 4)
    xl = chip // 4
    mine = place.block(0, 0)

    def ang_id(xl_, y_, core_):
        return (xl_ * 4 + y_) * 2 + core_

    def y_peer(dy):
        return (ang_id(xl, lax.rem(y + dy, 4), core), me)

    xl_peer = (ang_id(1 - xl, y, core), me)
    core_peer = (ang_id(xl, y, 1 - core), me)
    turn_peer = (ang_id(xh, z, core), y * 2 + xl)
    stays = jnp.logical_and(xl == xh, y == z)
    above = (ang, slab_of(lax.rem(mine + NSLAB - 1, NSLAB)))
    below = (ang, slab_of(lax.rem(mine + 1, NSLAB)))

    barrier = greet(place)
    for peer in (y_peer(1), y_peer(2), y_peer(3), xl_peer, core_peer):
        pl.semaphore_signal(barrier, inc=1, device_id=peer, device_id_type=MESH)

    @pl.when(jnp.logical_not(stays))
    def _():
        pl.semaphore_signal(barrier, inc=1, device_id=turn_peer, device_id_type=MESH)

    def tables(s, carry):
        rows = [par_all[s, k : k + 1, :] for k in range(10)]
        t0[pl.ds(pl.multiple_of(s * ROWS, ROWS), ROWS), :] = band(
            (ROWS, 384), 0, HALO + 1 - rows[8][:, :384], [r[:, :384] for r in rows[:4]], -1
        )
        t1[s] = band((512, 256), 1, PAD + 1 - rows[9][:, :256], [r[:, :256] for r in rows[4:8]], -1)
        return carry

    lax.fori_loop(0, NSLAB, tables, 0)
    ext[:, HALO + ROWS + HALO :, :] = jnp.zeros((2, 384 - ROWS - 2 * HALO, GRID), BF16)
    padded[:, :PAD] = jnp.zeros((NSLAB * ROWS, PAD), BF16)
    padded[:, PAD + GRID :] = jnp.zeros((NSLAB * ROWS, PAD), BF16)
    pl.semaphore_wait(barrier, NSLAB - 1 + 5 + jnp.where(stays, 0, 1))

    post = Post(sends, recvs)
    peers = [(dz, other) for dz in range(4) for other in range(2)][1:]
    bufs = (hs, hr, fs, fr, xs, xr)
    reduces = []
    for part in range(2):

        def ref(dz, other, lo, n, cols, room, part=part):
            start = pl.multiple_of(place.block(dz, other) * ROWS + lo, HALF)
            return image.at[part, pl.ds(start, n), cols]

        def own(dz, other, lo, n, cols, part=part, ref=ref):
            return decode(ref(dz, other, lo, n, cols, None)[...])

        reduces.append(Reduce(post, place, part, bufs, own, ref, (encode, decode)))
    halos = {}

    def done(part, left, right):
        ext[part, HALO : HALO + ROWS, LEFT] = left.astype(BF16)
        ext[part, HALO : HALO + ROWS, RIGHT] = right.astype(BF16)
        halos[part] = [
            post.go(ext.at[part, pl.ds(HALO, HALO), :], ext.at[part, pl.ds(HALO + ROWS, HALO), :], above),
            post.go(ext.at[part, pl.ds(ROWS, HALO), :], ext.at[part, pl.ds(0, HALO), :], below),
        ]

    rings = {}

    class YPlace:
        @staticmethod
        def peer(dy, other):
            return y_peer(dy)

    def spread_slices(part):
        for copy in halos[part]:
            copy.wait_recv()

        @pl.when(mine == 0)
        def _():
            ext[part, :HALO, :] = jnp.zeros((HALO, GRID), BF16)

        @pl.when(mine == NSLAB - 1)
        def _():
            ext[part, HALO + ROWS : 2 * HALO + ROWS, :] = jnp.zeros((HALO, GRID), BF16)

        for q in range(GRID // 256):
            cols = pl.ds(256 * q, 256)
            padded[:, PAD + 256 * q : PAD + 256 * q + 256] = dot(t0[...], ext[part, :, cols]).astype(BF16)

        cores = {}

        def slice_step(j):
            dy, other = j // 2, j % 2
            s = lax.rem(y + dy, 4) * 2 + (1 - xl if other else xl)
            rows = pl.ds(pl.multiple_of(s * ROWS, ROWS), ROWS)
            stack = jnp.concatenate(
                [padded[rows, 256 * q : 256 * q + 512] for q in range(GRID // 256)], axis=0
            )
            tiles = encode(dot(stack, t1[s]))
            for q in range(GRID // 256):
                cols = slice(256 * q, 256 * q + 256)
                for half in range(2):
                    lo = ROWS * q + HALF * half
                    gbuf[part, half, j, :, cols] = tiles[lo : lo + HALF]
            cores[j] = post.go(gbuf.at[part, 1 - core, j], cbuf.at[part, j], core_peer)

        def arrived(*steps):
            for j in steps:
                cores[j].wait_recv()

        def own(dy, lo, n):
            both = [
                decode(gbuf[part, core, j]) + decode(cbuf[part, j])
                for j in range(2 * dy + lo // HALF, 2 * dy + (lo + n) // HALF)
            ]
            return both[0] if len(both) == 1 else jnp.concatenate(both, axis=0)

        def far(k):
            yhs[part, k] = encode(own(2, HALF * k, HALF))
            return yhs.at[part, k]

        ring = Ring(
            post, YPlace, (yhr.at[part], yfs.at[part], yfr.at[part]), own, far, (encode, decode)
        )
        slice_step(4)
        slice_step(5)
        slice_step(2)
        arrived(4, 5)
        ring.start()
        slice_step(3)
        slice_step(6)
        slice_step(7)
        arrived(2, 3, 6, 7)
        ring.middle()
        slice_step(0)
        slice_step(1)
        rings[part] = (ring, functools.partial(arrived, 0, 1))

    sides = {}

    def settle_y(part):
        ring, ready = rings[part]
        ready()
        total = ring.end()
        xsend[part] = encode(total[HALF:])
        sides[part] = post.go(xsend.at[part], xrecv.at[part], xl_peer)
        keep[part] = total[:HALF]

    def settle(part):
        sides[part].wait_recv()
        fin[part] = encode(keep[part] + decode(xrecv[part]))

        @pl.when(stays)
        def _():
            landed[part] = fin[part]

        @pl.when(jnp.logical_not(stays))
        def _():
            turn_copy(part).start()

    def turn_copy(part):
        return pltpu.make_async_remote_copy(
            src_ref=fin.at[part], dst_ref=landed.at[part], send_sem=fsend.at[part],
            recv_sem=frecv.at[part], device_id=turn_peer, device_id_type=MESH,
        )

    pcode[...] = encode(probe_part[...])
    probe_copies = []
    for dz, other in peers:
        rows = pl.ds(pl.multiple_of(place.slab(dz, other) * 64, 64), 64)
        probe_copies.append(post.go(pcode.at[rows, :], pbuf.at[2 * dz + other], place.peer(dz, other)))
    first, second = reduces

    def open_reduce(reduce):
        reduce.start_cross(2)
        reduce.start_far(1)
        reduce.start_far(0)

    def more_cross(reduce):
        reduce.start_cross(1)
        reduce.start_cross(3)

    open_reduce(first)
    first.rings[0].middle()
    open_reduce(second)
    first.stage2()
    more_cross(first)
    first.rings[1].middle()
    first.start_cross(0)
    first.stage3()
    second.rings[0].middle()

    total = probe_part[pl.ds(pl.multiple_of(me * 64, 64), 64), :]
    for copy, (dz, other) in zip(probe_copies, peers):
        copy.wait_recv()
        total = total + decode(pbuf[2 * dz + other])
    psum[0] = encode(total)
    core_probe = post.go(psum.at[0], pcore, core_peer)

    first.stage4()
    second.stage2()
    more_cross(second)
    second.rings[1].middle()

    core_probe.wait_recv()
    psum[1] = encode(decode(psum[0]) + decode(pcore[...]))
    y_copies = [post.go(psum.at[1], py.at[j], y_peer(j)) for j in range(1, 4)]

    done(0, first.stage5(), first.stage6())
    second.start_cross(0)
    second.stage3()

    for copy in y_copies:
        copy.wait_recv()
    psum[2] = encode((decode(psum[1]) + decode(py[1])) + (decode(py[2]) + decode(py[3])))
    xl_probe = post.go(psum.at[2], pxl, xl_peer)

    second.stage4()
    done(1, second.stage5(), second.stage6())
    spread_slices(0)

    xl_probe.wait_recv()
    span = pall.at[pl.ds(pl.multiple_of(me * 64, 64), 64), :]
    span[...] = encode(decode(psum[2]) + decode(pxl[...]))
    out_copies = [post.go(span, span, place.peer(*peer)) for peer in peers]

    spread_slices(1)
    settle_y(0)
    settle(0)
    settle_y(1)
    settle(1)
    for copy in out_copies:
        copy.wait_recv()

    @pl.when(jnp.logical_not(stays))
    def _():
        turn_copy(0).wait()
        turn_copy(1).wait()

    for part in range(2):
        result[:, part, :] = decode(landed[part])
    probe_out[...] = decode(pall[...])
    post.finish()


def backward(image, par_all, probe_part):
    whole = pl.BlockSpec(memory_space=pltpu.VMEM)
    dma = pltpu.SemaphoreType.DMA
    return pl.pallas_call(
        backward_kernel,
        out_shape=(
            jax.ShapeDtypeStruct((HALF, 2, GRID), F32),
            jax.ShapeDtypeStruct((2 * PATCH, PATCH), F32),
        ),
        in_specs=[whole] * 3,
        out_specs=(whole, whole),
        scratch_shapes=[
            pltpu.VMEM((NSLAB * ROWS, 384), BF16),
            pltpu.VMEM((NSLAB, 512, 256), BF16),
            pltpu.VMEM((2, 384, GRID), BF16),
            pltpu.VMEM((NSLAB * ROWS, GRID + 2 * PAD), BF16),
            pltpu.VMEM((2, 2, NSLAB, HALF, GRID), BF16),
            pltpu.VMEM((2, NSLAB, HALF, GRID), BF16),
            pltpu.VMEM((2, 2, HALF, GRID), BF16),
            pltpu.VMEM((2, 2, HALF, GRID), BF16),
            pltpu.VMEM((2, 2, ROWS, GRID), BF16),
            pltpu.VMEM((2, 2, ROWS, GRID), BF16),
            pltpu.VMEM((2, HALF, GRID), BF16),
            pltpu.VMEM((2, HALF, GRID), BF16),
            pltpu.VMEM((2, HALF, GRID), F32),
            pltpu.VMEM((2, HALF, GRID), BF16),
            pltpu.VMEM((2, HALF, GRID), BF16),
            pltpu.VMEM((2 * PATCH, PATCH), BF16),
            pltpu.VMEM((2 * PATCH, PATCH), BF16),
            pltpu.VMEM((NSLAB, 64, PATCH), BF16),
            pltpu.VMEM((64, PATCH), BF16),
            pltpu.VMEM((4, 64, PATCH), BF16),
            pltpu.VMEM((64, PATCH), BF16),
            pltpu.VMEM((3, 64, PATCH), BF16),
        ]
        + reduce_scratch()
        + [dma((96,)), dma((96,)), dma((2,)), dma((2,))],
        compiler_params=pltpu.CompilerParams(
            collective_id=1, has_side_effects=True, vmem_limit_bytes=VMEM_LIMIT
        ),
        name="backward",
    )(image, par_all, probe_part)


def per_device(
    object_field, probe_field, diffraction, scan_offsets, counts, band_weights, band_offsets
):
    proj, par_all = forward(
        band_offsets.reshape(2 * ANGLES),
        band_weights.astype(F32).reshape(8 * ANGLES),
        object_field.reshape(2, GRID, GRID),
    )
    image, probe_part = slots(
        scan_offsets.reshape(2 * SLOTS), counts[0], proj, probe_field, diffraction[0, 0]
    )
    result, probe_out = backward(image, par_all, probe_part.reshape(2 * PATCH, PATCH))
    return (result[:, :, None, :], probe_out.reshape(2, PATCH, PATCH))


def solution(mesh):
    placed = (
        P(None, "slab", None, None),
        P(),
        P("ang", "slab", None, None, None),
        P("ang", "slab", None, None),
        P("slab", "ang"),
        P(None, "slab", None, None),
        P(None, "slab", None),
    )
    return jax.shard_map(
        per_device,
        mesh=mesh,
        in_specs=placed,
        out_specs=(P("ang", None, "slab", None), P()),
        check_vma=False,
    )
```

```python
import functools
import math

import jax
import jax.numpy as jnp
import numpy as np
from jax import lax
from jax.experimental import pallas as pl
from jax.experimental.pallas import tpu as pltpu
from jax.sharding import PartitionSpec as P

MESH = pl.DeviceIdType.MESH
F32 = jnp.float32
BF16 = jnp.bfloat16
GRID = 1024
PATCH = 256
SLOTS = 8
NSLAB = 8
ROWS = GRID // NSLAB
HALF = ROWS // 2
PAD = 128
HALO = 80
POSITIONS = 512
VMEM_LIMIT = 56 << 20


def block_of(slab):
    return (slab % 2) * 4 + slab // 2


def slab_of(block):
    return (block % 4) * 2 + block // 4


def band(shape, axis_out, start, weights, step):
    inner = lax.broadcasted_iota(jnp.int32, shape, 1 - axis_out)
    outer = lax.broadcasted_iota(jnp.int32, shape, axis_out)
    distance = (inner - outer).astype(F32)
    summed = jnp.zeros(shape, F32)
    for tap, weight in enumerate(weights):
        summed = jnp.where(distance == start + step * tap, weight, summed)
    return summed.astype(BF16)


def encode(values):
    return (values * jnp.abs(values)).astype(BF16)


def decode(codes):
    square = codes.astype(F32)
    return square * lax.rsqrt(jnp.maximum(jnp.abs(square), 1e-37))


def encode_fine(values):
    square = values * jnp.abs(values) * 2.0**32
    return (square * jnp.abs(square)).astype(BF16)


def decode_fine(codes):
    fourth = codes.astype(F32)
    square = fourth * lax.rsqrt(jnp.maximum(jnp.abs(fourth), 1e-37))
    return square * (lax.rsqrt(jnp.maximum(jnp.abs(square), 1e-30)) * 2.0**-16)


def dot(left, right):
    return jnp.dot(left, right, preferred_element_type=F32)


WIDE = GRID // 2
LEFT = pl.ds(0, WIDE)
RIGHT = pl.ds(WIDE, WIDE)


class Post:
    def __init__(self, sends, recvs):
        self.sends = sends
        self.recvs = recvs
        self.opened = []

    def go(self, src, dst, peer):
        k = len(self.opened)
        copy = pltpu.make_async_remote_copy(
            src_ref=src, dst_ref=dst, send_sem=self.sends.at[k], recv_sem=self.recvs.at[k],
            device_id=peer, device_id_type=MESH,
        )
        copy.start()
        self.opened.append(copy)
        return copy

    def finish(self):
        for copy in self.opened:
            copy.wait_send()


class Place:
    def __init__(self):
        self.ang = lax.axis_index("ang")
        self.me = lax.axis_index("slab")
        self.z = self.me // 2
        self.xh = self.me % 2

    def slab(self, dz, other):
        x = 1 - self.xh if other else self.xh
        return lax.rem(self.z + dz, 4) * 2 + x

    def peer(self, dz, other):
        return (self.ang, self.slab(dz, other))

    def block(self, dz, other):
        return block_of(self.slab(dz, other))


class Ring:
    def __init__(self, post, place, bufs, own, first, codec):
        self.post, self.place = post, place
        self.encode, self.decode = codec
        self.hr, self.fs, self.fr = bufs
        self.own, self.first = own, first

    def start(self):
        self.halves = [
            self.post.go(self.first(k), self.hr.at[k], self.place.peer((1, 3)[k], 0))
            for k in range(2)
        ]

    def middle(self):
        self.whole = []
        for k, dz in enumerate((1, 3)):
            lo = HALF * k
            self.fs[k, HALF - lo : ROWS - lo, :] = self.encode(self.own(dz, HALF - lo, HALF))
            self.halves[k].wait_recv()
            both = self.own(dz, lo, HALF) + self.decode(self.hr[k])
            self.fs[k, lo : lo + HALF, :] = self.encode(both)
            self.whole.append(self.post.go(self.fs.at[k], self.fr.at[k], self.place.peer(dz, 0)))

    def end(self):
        for copy in self.whole:
            copy.wait_recv()
        return self.own(0, 0, ROWS) + self.decode(self.fr[0]) + self.decode(self.fr[1])


class Reduce:
    def __init__(self, post, place, part, bufs, own, ref, codec):
        hs, hr, fs, fr, xs, xr = bufs
        self.post, self.place, self.own, self.ref = post, place, own, ref
        self.encode, self.decode = codec
        self.hs, self.xs, self.xr = hs.at[part], xs.at[part], xr.at[part]
        self.rings = []
        for chain, other in enumerate((1, 0)):
            self.rings.append(
                Ring(
                    post, place, (hr.at[part, chain], fs.at[part, chain], fr.at[part, chain]),
                    functools.partial(self.left, other),
                    functools.partial(self.left_first, other, chain), codec,
                )
            )
        self.rings.append(
            Ring(
                post, place, (hr.at[part, 2], fs.at[part, 2], fr.at[part, 2]),
                self.right, self.right_first, codec,
            )
        )
        self.crossing = {}

    def left(self, other, dz, lo, n):
        return self.own(dz, other, lo, n, LEFT)

    def left_first(self, other, chain, k):
        return self.ref(2, other, HALF * k, HALF, LEFT, self.hs.at[chain, k])

    def right(self, dz, lo, n):
        return self.own(dz, 0, lo, n, RIGHT) + self.decode(self.xr[dz, lo : lo + n, :])

    def right_first(self, k):
        self.hs[2, k] = self.encode(self.right(2, HALF * k, HALF))
        return self.hs.at[2, k]

    def start_far(self, other):
        self.rings[1 - other].start()

    def start_cross(self, dz):
        src = self.ref(dz, 1, 0, ROWS, RIGHT, self.xs.at[dz])
        self.crossing[dz] = self.post.go(src, self.xr.at[dz], self.place.peer(0, 1))

    def stage2(self):
        self.crossing[2].wait_recv()
        self.rings[2].start()

    def stage3(self):
        self.xs[4] = self.encode(self.rings[0].end())
        self.crossing[4] = self.post.go(self.xs.at[4], self.xr.at[4], self.place.peer(0, 1))

    def stage4(self):
        self.crossing[1].wait_recv()
        self.crossing[3].wait_recv()
        self.rings[2].middle()

    def stage5(self):
        mine = self.rings[1].end()
        self.crossing[4].wait_recv()
        return mine + self.decode(self.xr[4])

    def stage6(self):
        self.crossing[0].wait_recv()
        return self.rings[2].end()


def reduce_scratch():
    code = BF16
    return [
        pltpu.VMEM((2, 3, 2, HALF, WIDE), code),
        pltpu.VMEM((2, 3, 2, HALF, WIDE), code),
        pltpu.VMEM((2, 3, 2, ROWS, WIDE), code),
        pltpu.VMEM((2, 3, 2, ROWS, WIDE), code),
        pltpu.VMEM((2, 5, ROWS, WIDE), code),
        pltpu.VMEM((2, 5, ROWS, WIDE), code),
    ]


class Gather:
    def __init__(self, post, place, part, whole):
        self.post, self.place, self.part, self.whole = post, place, part, whole

    def span(self, dz, other, cols, lo=0, n=ROWS):
        start = pl.multiple_of(self.place.block(dz, other) * ROWS + lo, HALF)
        return self.whole.at[self.part, pl.ds(start, n), cols]

    def send(self, dz, other, cols, to_dz, to_other, lo=0, n=ROWS):
        span = self.span(dz, other, cols, lo, n)
        return self.post.go(span, span, self.place.peer(to_dz, to_other))

    def spread(self, other, cols):
        return [self.send(0, other, cols, dz, 0) for dz in (1, 3)]

    def relay(self, other, cols, pair):
        pair[0].wait_recv()
        first = self.send(3, other, cols, 1, 0, 0, HALF)
        pair[1].wait_recv()
        return [first, self.send(1, other, cols, 3, 0, HALF, HALF)]

    def stage0(self):
        self.cross_left = self.send(0, 0, LEFT, 0, 1)
        self.right = self.spread(0, RIGHT)
        self.cross_right = [self.send(0, 0, RIGHT, 0, 1)]
        self.left = self.spread(0, LEFT)

    def stage1(self):
        self.right_far = self.relay(0, RIGHT, self.right)
        for dz in (3, 1):
            self.cross_right.append(self.send(dz, 0, RIGHT, 0, 1))

    def stage2(self):
        self.cross_left.wait_recv()
        self.left_other = self.spread(1, LEFT)

    def stage3(self):
        self.left_far = self.relay(0, LEFT, self.left)

    def stage4(self):
        for copy in self.right_far:
            copy.wait_recv()
        self.cross_right.append(self.send(2, 0, RIGHT, 0, 1))

    def stage5(self):
        self.left_far += self.relay(1, LEFT, self.left_other)

    def stage6(self):
        for copy in self.left_far + self.cross_right:
            copy.wait_recv()


def greet(place):
    barrier = pltpu.get_barrier_semaphore()
    for dz in range(4):
        for other in range(2):
            if (dz, other) != (0, 0):
                pl.semaphore_signal(
                    barrier, inc=1, device_id=place.peer(dz, other), device_id_type=MESH
                )
    return barrier


def follow_reduces(reduces, done):
    for reduce in reduces:
        reduce.rings[0].middle()
    for reduce in reduces:
        reduce.stage2()
        reduce.start_cross(1)
        reduce.start_cross(3)
    for reduce in reduces:
        reduce.rings[1].middle()
    for reduce in reduces:
        reduce.stage3()
    for reduce in reduces:
        reduce.stage4()
        reduce.start_cross(0)
    for part, reduce in enumerate(reduces):
        done(part, reduce.stage5(), reduce.stage6())


def forward_kernel(
    offs, wts, obj, proj, par_all,
    opad, lift, t0, t1, dbuf, hs, hr, fs, fr, xs, xr,
    load_sem, sends, recvs,
):
    place = Place()
    barrier = greet(place)
    load = pltpu.make_async_copy(obj, opad.at[:, pl.ds(PAD, GRID), :], load_sem)
    load.start()
    opad[:, :PAD, :] = jnp.zeros((2, PAD, GRID), BF16)
    opad[:, PAD + GRID :, :] = jnp.zeros((2, PAD, GRID), BF16)
    lift[:, :PAD] = jnp.zeros((2 * ROWS, PAD), BF16)
    lift[:, PAD + GRID :] = jnp.zeros((2 * ROWS, PAD), BF16)
    ang = place.ang
    off_y = offs[ang, 0, 0].astype(F32)
    off_x = offs[ang, 0, 1].astype(F32)
    taps = [wts[ang, 0, k // 4, k % 4] for k in range(8)]
    t0[...] = band(t0.shape, 0, off_y + float(PAD - 1), taps[:4], 1)
    t1[...] = band(t1.shape, 1, off_x + float(PAD - 1), taps[4:], 1)
    row_ids = lax.broadcasted_iota(jnp.int32, par_all.shape[1:], 0)
    par = jnp.zeros(par_all.shape[1:], F32)
    for k, value in enumerate(taps + [off_y, off_x]):
        par = jnp.where(row_ids == k, value, par)
    par_all[pl.ds(place.me, 1)] = par[None]
    load.wait()

    pl.semaphore_wait(barrier, NSLAB - 1)
    post = Post(sends, recvs)
    par_copies = []
    for dz in range(4):
        for other in range(2):
            if (dz, other) != (0, 0):
                span = par_all.at[place.me]
                par_copies.append(post.go(span, span, place.peer(dz, other)))

    def slot(dz, other):
        return 2 * dz + other

    def project(dz, other):
        start = pl.multiple_of(place.block(dz, other) * ROWS, ROWS)
        for part in range(2):
            rows = opad[part, pl.ds(start, 3 * PAD), :]
            lift[part * ROWS : (part + 1) * ROWS, PAD : PAD + GRID] = dot(t0[...], rows).astype(BF16)
        for q in range(GRID // 256):
            tile = dot(lift[:, 256 * q : 256 * q + 512], t1[...])
            dbuf[slot(dz, other), :, :, 256 * q : 256 * q + 256] = tile.reshape(2, ROWS, 256)

    bufs = (hs, hr, fs, fr, xs, xr)
    reduces = []
    for part in range(2):

        def own(dz, other, lo, n, cols, part=part):
            return dbuf[slot(dz, other), part, pl.ds(lo, n), cols]

        def ref(dz, other, lo, n, cols, room, part=part):
            room[...] = encode_fine(own(dz, other, lo, n, cols, part))
            return room

        reduces.append(Reduce(post, place, part, bufs, own, ref, (encode_fine, decode_fine)))
    for dz, other in ((2, 1), (2, 0), (1, 1), (3, 1), (0, 1), (1, 0), (3, 0), (0, 0)):
        project(dz, other)
        for reduce in reduces:
            if dz == 2:
                reduce.start_far(other)
                if other == 1:
                    reduce.start_cross(2)
    rows = pl.ds(pl.multiple_of(place.block(0, 0) * ROWS, ROWS), ROWS)
    gathers = [Gather(post, place, part, proj) for part in range(2)]

    def done(part, left, right):
        proj[part, rows, LEFT] = encode_fine(left)
        proj[part, rows, RIGHT] = encode_fine(right)
        gathers[part].stage0()

    follow_reduces(reduces, done)
    for k in range(1, 7):
        for gather in gathers:
            getattr(gather, "stage%d" % k)()
    for copy in par_copies:
        copy.wait_recv()
    post.finish()


def forward(offs, wts, obj):
    return pl.pallas_call(
        forward_kernel,
        out_shape=(
            jax.ShapeDtypeStruct((2, GRID, GRID), BF16),
            jax.ShapeDtypeStruct((NSLAB, 16, 512), F32),
        ),
        in_specs=[
            pl.BlockSpec(memory_space=pltpu.SMEM),
            pl.BlockSpec(memory_space=pltpu.SMEM),
            pl.BlockSpec(memory_space=pl.ANY),
        ],
        out_specs=(
            pl.BlockSpec(memory_space=pltpu.VMEM),
            pl.BlockSpec(memory_space=pltpu.VMEM),
        ),
        scratch_shapes=[
            pltpu.VMEM((2, GRID + 2 * PAD, GRID), BF16),
            pltpu.VMEM((2 * ROWS, GRID + 2 * PAD), BF16),
            pltpu.VMEM((ROWS, 3 * PAD), BF16),
            pltpu.VMEM((512, 256), BF16),
            pltpu.VMEM((NSLAB, 2, ROWS, GRID), F32),
        ]
        + reduce_scratch()
        + [
            pltpu.SemaphoreType.DMA,
            pltpu.SemaphoreType.DMA((96,)),
            pltpu.SemaphoreType.DMA((96,)),
        ],
        compiler_params=pltpu.CompilerParams(
            collective_id=0, has_side_effects=True, vmem_limit_bytes=VMEM_LIMIT
        ),
        name="forward",
    )(offs, wts, obj)


def dft_tables():
    index = np.arange(PATCH)
    phase = 2.0 * np.pi * ((index[:, None] * index[None, :]) % PATCH) / PATCH
    cosines = np.cos(phase) / math.sqrt(PATCH)
    sines = np.sin(phase) / math.sqrt(PATCH)
    whole = np.block([[cosines, -sines], [sines, cosines]]).astype(np.float32)
    high = whole.astype(jnp.bfloat16)
    low = (whole - high.astype(np.float32)).astype(jnp.bfloat16)
    across = np.concatenate([high, high, low], axis=0)
    down = np.concatenate([high.T, high.T, low.T], axis=1)
    return [np.ascontiguousarray(t) for t in (down, across, high, high.T)]


def split_join(values, axis):
    high = values.astype(BF16)
    low = (values - high.astype(F32)).astype(BF16)
    return jnp.concatenate([high, low, high], axis=axis)


CHUNKS = 8
CHUNK = GRID // CHUNKS


def slots_kernel(
    corners, count, proj, probe, diff, *refs,
):
    tables, refs = refs[:4], refs[4:]
    image, probe_part, proj_in, diff_in = refs[:4]
    left_f, right_f, left_i, right_i, wide, total, image_out, in_sem, out_sem, sem = refs[4:]

    def chunk_rows(k):
        return pl.ds(pl.multiple_of(k * CHUNK, CHUNK), CHUNK)

    def load(k):
        rows = chunk_rows(k)
        return pltpu.make_async_copy(proj.at[:, rows, :], proj_in.at[:, rows, :], in_sem.at[k])

    def store(k):
        rows = chunk_rows(k)
        return pltpu.make_async_copy(image_out.at[:, rows, :], image.at[:, rows, :], out_sem.at[k])

    for k in range(CHUNKS):
        load(k).start()
    later = [
        pltpu.make_async_copy(src, dst, sem.at[k])
        for k, (src, dst) in enumerate(
            zip(tables + (diff,), (left_f, right_f, left_i, right_i, diff_in))
        )
    ]
    for copy in later:
        copy.start()
    probe_part[...] = jnp.zeros(probe_part.shape, F32)

    def open_chunk(k, carry):
        rows = chunk_rows(k)
        for tile in range(GRID // 128 + 1):
            total[:, tile, rows, :] = jnp.zeros((2, CHUNK, 128), F32)
        load(k).wait()
        for tile in range(GRID // 128):
            wide[:, tile, rows, :] = decode_fine(proj_in[:, rows, 128 * tile : 128 * tile + 128])
        return carry

    lax.fori_loop(0, CHUNKS, open_chunk, 0)
    for copy in later:
        copy.wait()
    live = count[0, 0]
    lane = lax.broadcasted_iota(jnp.int32, (PATCH, 128), 1)
    zero = jnp.zeros((PATCH, 128), F32)
    probe_re = probe[0]
    probe_im = probe[1]

    def pair_step(pair, carry):
        waves = []
        places = []
        for k in range(2):
            slot = 2 * pair + k
            row = corners[0, 0, slot, 0]
            col = corners[0, 0, slot, 1]
            turn = lax.rem(col, 128)
            tile = col // 128
            early = lane < turn
            patch = []
            for part in range(2):
                window = [wide[part, tile + m, pl.ds(row, PATCH), :] for m in range(3)]
                joined = jnp.concatenate(
                    [jnp.where(early, window[2], window[0]), window[1]], axis=1
                )
                patch.append(pltpu.roll(joined, lax.rem(PATCH - turn, PATCH), 1))
            places.append((slot, row, turn, tile, early, patch))
            waves.append(
                jnp.concatenate(
                    [
                        probe_re * patch[0] - probe_im * patch[1],
                        probe_re * patch[1] + probe_im * patch[0],
                    ],
                    axis=0,
                )
            )
        half = dot(left_f[...], split_join(jnp.concatenate(waves, axis=1), 0))
        half = jnp.concatenate(
            [
                jnp.concatenate([half[:PATCH, cols], half[PATCH:, cols]], axis=1)
                for cols in (slice(0, PATCH), slice(PATCH, 2 * PATCH))
            ],
            axis=0,
        )
        far = dot(split_join(half, 1), right_f[...])
        resid = []
        for k in range(2):
            slot = places[k][0]
            far_re = far[PATCH * k : PATCH * k + PATCH, :PATCH]
            far_im = far[PATCH * k : PATCH * k + PATCH, PATCH:]
            weight = jnp.where(slot < live, 1.0 / math.sqrt(POSITIONS), 0.0)
            misfit = (far_re * far_re + far_im * far_im - diff_in[slot]) * weight
            resid.append(
                jnp.concatenate(
                    [(misfit * far_re).astype(BF16), (misfit * far_im).astype(BF16)], axis=0
                )
            )
        inner = dot(left_i[...], jnp.concatenate(resid, axis=1)).astype(BF16)
        inner = jnp.concatenate(
            [
                jnp.concatenate([inner[:PATCH, cols], inner[PATCH:, cols]], axis=1)
                for cols in (slice(0, PATCH), slice(PATCH, 2 * PATCH))
            ],
            axis=0,
        )
        chi = dot(inner, right_i[...])
        for k in range(2):
            slot, row, turn, tile, early, patch = places[k]
            chi_re = chi[PATCH * k : PATCH * k + PATCH, :PATCH]
            chi_im = chi[PATCH * k : PATCH * k + PATCH, PATCH:]
            probe_part[0] += patch[0] * chi_re + patch[1] * chi_im
            probe_part[1] += patch[0] * chi_im - patch[1] * chi_re
            grads = (
                probe_re * chi_re + probe_im * chi_im,
                probe_re * chi_im - probe_im * chi_re,
            )
            for part in range(2):
                turned = pltpu.roll(grads[part], turn, 1)
                head = turned[:, :128]
                spread = (
                    jnp.where(early, zero, head), turned[:, 128:], jnp.where(early, head, zero)
                )
                for m in range(3):
                    total[part, tile + m, pl.ds(row, PATCH), :] += spread[m]
        return carry

    lax.fori_loop(0, (live + 1) // 2, pair_step, 0)

    def close_chunk(k, carry):
        rows = chunk_rows(k)
        for tile in range(GRID // 128):
            image_out[:, rows, 128 * tile : 128 * tile + 128] = encode(total[:, tile, rows, :])
        store(k).start()
        return carry

    lax.fori_loop(0, CHUNKS, close_chunk, 0)
    for k in range(CHUNKS):
        store(k).wait()


def slots(corners, count, proj, probe, diffraction):
    tables = [jnp.asarray(t) for t in dft_tables()]
    whole = pl.BlockSpec(memory_space=pltpu.VMEM)
    scalar = pl.BlockSpec(memory_space=pltpu.SMEM)
    far = pl.BlockSpec(memory_space=pl.ANY)
    dma = pltpu.SemaphoreType.DMA
    return pl.pallas_call(
        slots_kernel,
        out_shape=(
            jax.ShapeDtypeStruct((2, GRID, GRID), BF16),
            jax.ShapeDtypeStruct((2, PATCH, PATCH), F32),
        ),
        in_specs=[scalar, scalar, far, whole, far] + [far] * 4,
        out_specs=(far, whole),
        scratch_shapes=[
            pltpu.VMEM((2, GRID, GRID), BF16),
            pltpu.VMEM((SLOTS, PATCH, PATCH), F32),
            pltpu.VMEM((512, 1536), BF16),
            pltpu.VMEM((1536, 512), BF16),
            pltpu.VMEM((512, 512), BF16),
            pltpu.VMEM((512, 512), BF16),
            pltpu.VMEM((2, GRID // 128 + 1, GRID, 128), F32),
            pltpu.VMEM((2, GRID // 128 + 1, GRID, 128), F32),
            pltpu.VMEM((2, GRID, GRID), BF16),
            dma((CHUNKS,)), dma((CHUNKS,)), dma((5,)),
        ],
        compiler_params=pltpu.CompilerParams(vmem_limit_bytes=VMEM_LIMIT),
        name="slots",
    )(corners, count, proj, probe, diffraction, *tables)


def backward_kernel(
    image, par_all, probe_part, result, probe_out,
    t0, t1, ext, padded, gbuf, cbuf, yhs, yhr, yfs, yfr, xsend, xrecv, keep, fin,
    pcode, pall, pbuf, pcore, py, pxl, psum, hs, hr, fs, fr, xs, xr,
    sends, recvs, fsend, frecv,
):
    place = Place()
    ang, me, z, xh = place.ang, place.me, place.z, place.xh
    core = lax.rem(ang, 2)
    chip = ang // 2
    y = lax.rem(chip, 4)
    xl = chip // 4
    mine = place.block(0, 0)

    def ang_id(xl_, y_, core_):
        return (xl_ * 4 + y_) * 2 + core_

    def y_peer(dy):
        return (ang_id(xl, lax.rem(y + dy, 4), core), me)

    xl_peer = (ang_id(1 - xl, y, core), me)
    core_peer = (ang_id(xl, y, 1 - core), me)
    turn_peer = (ang_id(xh, z, core), y * 2 + xl)
    stays = jnp.logical_and(xl == xh, y == z)
    above = (ang, slab_of(lax.rem(mine + NSLAB - 1, NSLAB)))
    below = (ang, slab_of(lax.rem(mine + 1, NSLAB)))

    barrier = greet(place)
    for peer in (y_peer(1), y_peer(2), y_peer(3), xl_peer, core_peer):
        pl.semaphore_signal(barrier, inc=1, device_id=peer, device_id_type=MESH)

    @pl.when(jnp.logical_not(stays))
    def _():
        pl.semaphore_signal(barrier, inc=1, device_id=turn_peer, device_id_type=MESH)

    def tables(s, carry):
        rows = [par_all[s, k : k + 1, :] for k in range(10)]
        t0[pl.ds(pl.multiple_of(s * ROWS, ROWS), ROWS), :] = band(
            (ROWS, 384), 0, HALO + 1 - rows[8][:, :384], [r[:, :384] for r in rows[:4]], -1
        )
        t1[s] = band((512, 256), 1, PAD + 1 - rows[9][:, :256], [r[:, :256] for r in rows[4:8]], -1)
        return carry

    lax.fori_loop(0, NSLAB, tables, 0)
    ext[:, HALO + ROWS + HALO :, :] = jnp.zeros((2, 384 - ROWS - 2 * HALO, GRID), BF16)
    padded[:, :PAD] = jnp.zeros((NSLAB * ROWS, PAD), BF16)
    padded[:, PAD + GRID :] = jnp.zeros((NSLAB * ROWS, PAD), BF16)
    pl.semaphore_wait(barrier, NSLAB - 1 + 5 + jnp.where(stays, 0, 1))

    post = Post(sends, recvs)
    peers = [(dz, other) for dz in range(4) for other in range(2)][1:]
    bufs = (hs, hr, fs, fr, xs, xr)
    reduces = []
    for part in range(2):

        def ref(dz, other, lo, n, cols, room, part=part):
            start = pl.multiple_of(place.block(dz, other) * ROWS + lo, HALF)
            return image.at[part, pl.ds(start, n), cols]

        def own(dz, other, lo, n, cols, part=part, ref=ref):
            return decode(ref(dz, other, lo, n, cols, None)[...])

        reduces.append(Reduce(post, place, part, bufs, own, ref, (encode, decode)))
    halos = {}

    def done(part, left, right):
        ext[part, HALO : HALO + ROWS, LEFT] = left.astype(BF16)
        ext[part, HALO : HALO + ROWS, RIGHT] = right.astype(BF16)
        halos[part] = [
            post.go(ext.at[part, pl.ds(HALO, HALO), :], ext.at[part, pl.ds(HALO + ROWS, HALO), :], above),
            post.go(ext.at[part, pl.ds(ROWS, HALO), :], ext.at[part, pl.ds(0, HALO), :], below),
        ]

    rings = {}

    class YPlace:
        @staticmethod
        def peer(dy, other):
            return y_peer(dy)

    def spread_slices(part):
        for copy in halos[part]:
            copy.wait_recv()

        @pl.when(mine == 0)
        def _():
            ext[part, :HALO, :] = jnp.zeros((HALO, GRID), BF16)

        @pl.when(mine == NSLAB - 1)
        def _():
            ext[part, HALO + ROWS : 2 * HALO + ROWS, :] = jnp.zeros((HALO, GRID), BF16)

        for q in range(GRID // 256):
            cols = pl.ds(256 * q, 256)
            padded[:, PAD + 256 * q : PAD + 256 * q + 256] = dot(t0[...], ext[part, :, cols]).astype(BF16)

        cores = {}

        def slice_step(j):
            dy, other = j // 2, j % 2
            s = lax.rem(y + dy, 4) * 2 + (1 - xl if other else xl)
            rows = pl.ds(pl.multiple_of(s * ROWS, ROWS), ROWS)
            stack = jnp.concatenate(
                [padded[rows, 256 * q : 256 * q + 512] for q in range(GRID // 256)], axis=0
            )
            tiles = encode(dot(stack, t1[s]))
            for q in range(GRID // 256):
                cols = slice(256 * q, 256 * q + 256)
                for half in range(2):
                    lo = ROWS * q + HALF * half
                    gbuf[part, half, j, :, cols] = tiles[lo : lo + HALF]
            cores[j] = post.go(gbuf.at[part, 1 - core, j], cbuf.at[part, j], core_peer)

        def arrived(*steps):
            for j in steps:
                cores[j].wait_recv()

        def own(dy, lo, n):
            both = [
                decode(gbuf[part, core, j]) + decode(cbuf[part, j])
                for j in range(2 * dy + lo // HALF, 2 * dy + (lo + n) // HALF)
            ]
            return both[0] if len(both) == 1 else jnp.concatenate(both, axis=0)

        def far(k):
            yhs[part, k] = encode(own(2, HALF * k, HALF))
            return yhs.at[part, k]

        ring = Ring(
            post, YPlace, (yhr.at[part], yfs.at[part], yfr.at[part]), own, far, (encode, decode)
        )
        slice_step(4)
        slice_step(5)
        slice_step(2)
        arrived(4, 5)
        ring.start()
        slice_step(3)
        slice_step(6)
        slice_step(7)
        arrived(2, 3, 6, 7)
        ring.middle()
        slice_step(0)
        slice_step(1)
        rings[part] = (ring, functools.partial(arrived, 0, 1))

    sides = {}

    def settle_y(part):
        ring, ready = rings[part]
        ready()
        total = ring.end()
        xsend[part] = encode(total[HALF:])
        sides[part] = post.go(xsend.at[part], xrecv.at[part], xl_peer)
        keep[part] = total[:HALF]

    def settle(part):
        sides[part].wait_recv()
        fin[part] = encode(keep[part] + decode(xrecv[part]))

        @pl.when(stays)
        def _():
            result[part] = fin[part]

        @pl.when(jnp.logical_not(stays))
        def _():
            turn_copy(part).start()

    def turn_copy(part):
        return pltpu.make_async_remote_copy(
            src_ref=fin.at[part], dst_ref=result.at[part], send_sem=fsend.at[part],
            recv_sem=frecv.at[part], device_id=turn_peer, device_id_type=MESH,
        )

    pcode[...] = encode(probe_part[...])
    probe_copies = []
    for dz, other in peers:
        rows = pl.ds(pl.multiple_of(place.slab(dz, other) * 64, 64), 64)
        probe_copies.append(post.go(pcode.at[rows, :], pbuf.at[2 * dz + other], place.peer(dz, other)))
    first, second = reduces

    def open_reduce(reduce):
        reduce.start_cross(2)
        reduce.start_far(1)
        reduce.start_far(0)

    def more_cross(reduce):
        reduce.start_cross(1)
        reduce.start_cross(3)

    open_reduce(first)
    first.rings[0].middle()
    open_reduce(second)
    first.stage2()
    more_cross(first)
    first.rings[1].middle()
    first.start_cross(0)
    first.stage3()
    second.rings[0].middle()

    total = probe_part[pl.ds(pl.multiple_of(me * 64, 64), 64), :]
    for copy, (dz, other) in zip(probe_copies, peers):
        copy.wait_recv()
        total = total + decode(pbuf[2 * dz + other])
    psum[0] = encode(total)
    core_probe = post.go(psum.at[0], pcore, core_peer)

    first.stage4()
    second.stage2()
    more_cross(second)
    second.rings[1].middle()

    core_probe.wait_recv()
    psum[1] = encode(decode(psum[0]) + decode(pcore[...]))
    y_copies = [post.go(psum.at[1], py.at[j], y_peer(j)) for j in range(1, 4)]

    done(0, first.stage5(), first.stage6())
    second.start_cross(0)
    second.stage3()

    for copy in y_copies:
        copy.wait_recv()
    psum[2] = encode((decode(psum[1]) + decode(py[1])) + (decode(py[2]) + decode(py[3])))
    xl_probe = post.go(psum.at[2], pxl, xl_peer)

    second.stage4()
    done(1, second.stage5(), second.stage6())
    spread_slices(0)

    xl_probe.wait_recv()
    span = pall.at[pl.ds(pl.multiple_of(me * 64, 64), 64), :]
    span[...] = encode(decode(psum[2]) + decode(pxl[...]))
    out_copies = [post.go(span, span, place.peer(*peer)) for peer in peers]

    spread_slices(1)
    settle_y(0)
    settle(0)
    settle_y(1)
    settle(1)
    for copy in out_copies:
        copy.wait_recv()

    @pl.when(jnp.logical_not(stays))
    def _():
        turn_copy(0).wait()
        turn_copy(1).wait()

    probe_out[...] = decode(pall[...])
    post.finish()


def backward(image, par_all, probe_part):
    whole = pl.BlockSpec(memory_space=pltpu.VMEM)
    dma = pltpu.SemaphoreType.DMA
    return pl.pallas_call(
        backward_kernel,
        out_shape=(
            jax.ShapeDtypeStruct((2, HALF, GRID), BF16),
            jax.ShapeDtypeStruct((2 * PATCH, PATCH), F32),
        ),
        in_specs=[whole] * 3,
        out_specs=(whole, whole),
        scratch_shapes=[
            pltpu.VMEM((NSLAB * ROWS, 384), BF16),
            pltpu.VMEM((NSLAB, 512, 256), BF16),
            pltpu.VMEM((2, 384, GRID), BF16),
            pltpu.VMEM((NSLAB * ROWS, GRID + 2 * PAD), BF16),
            pltpu.VMEM((2, 2, NSLAB, HALF, GRID), BF16),
            pltpu.VMEM((2, NSLAB, HALF, GRID), BF16),
            pltpu.VMEM((2, 2, HALF, GRID), BF16),
            pltpu.VMEM((2, 2, HALF, GRID), BF16),
            pltpu.VMEM((2, 2, ROWS, GRID), BF16),
            pltpu.VMEM((2, 2, ROWS, GRID), BF16),
            pltpu.VMEM((2, HALF, GRID), BF16),
            pltpu.VMEM((2, HALF, GRID), BF16),
            pltpu.VMEM((2, HALF, GRID), F32),
            pltpu.VMEM((2, HALF, GRID), BF16),
            pltpu.VMEM((2 * PATCH, PATCH), BF16),
            pltpu.VMEM((2 * PATCH, PATCH), BF16),
            pltpu.VMEM((NSLAB, 64, PATCH), BF16),
            pltpu.VMEM((64, PATCH), BF16),
            pltpu.VMEM((4, 64, PATCH), BF16),
            pltpu.VMEM((64, PATCH), BF16),
            pltpu.VMEM((3, 64, PATCH), BF16),
        ]
        + reduce_scratch()
        + [dma((96,)), dma((96,)), dma((2,)), dma((2,))],
        compiler_params=pltpu.CompilerParams(
            collective_id=1, has_side_effects=True, vmem_limit_bytes=VMEM_LIMIT
        ),
        name="backward",
    )(image, par_all, probe_part)


def per_device(
    object_field, probe_field, diffraction, scan_offsets, counts, band_weights, band_offsets
):
    proj, par_all = forward(
        band_offsets,
        band_weights.astype(F32),
        object_field.reshape(2, GRID, GRID),
    )
    image, probe_part = slots(
        scan_offsets, counts, proj, probe_field, diffraction[0, 0]
    )
    result, probe_out = backward(image, par_all, probe_part.reshape(2 * PATCH, PATCH))
    object_grad = decode(jnp.transpose(result, (1, 0, 2)))[:, :, None, :]
    return (object_grad, probe_out.reshape(2, PATCH, PATCH))


def solution(mesh):
    placed = (
        P(None, "slab", None, None),
        P(),
        P("ang", "slab", None, None, None),
        P("ang", "slab", None, None),
        P("slab", "ang"),
        P(None, "slab", None, None),
        P(None, "slab", None),
    )
    return jax.shard_map(
        per_device,
        mesh=mesh,
        in_specs=placed,
        out_specs=(P("ang", None, "slab", None), P()),
        check_vma=False,
    )
```

```python
import functools
import math

import jax
import jax.numpy as jnp
import numpy as np
from jax import lax
from jax.experimental import pallas as pl
from jax.experimental.pallas import tpu as pltpu
from jax.sharding import PartitionSpec as P

MESH = pl.DeviceIdType.MESH
F32 = jnp.float32
BF16 = jnp.bfloat16
GRID = 1024
PATCH = 256
SLOTS = 8
NSLAB = 8
ROWS = GRID // NSLAB
HALF = ROWS // 2
PAD = 128
HALO = 80
POSITIONS = 512
VMEM_LIMIT = 56 << 20


def block_of(slab):
    return (slab % 2) * 4 + slab // 2


def slab_of(block):
    return (block % 4) * 2 + block // 4


def band(shape, axis_out, start, weights, step):
    inner = lax.broadcasted_iota(jnp.int32, shape, 1 - axis_out)
    outer = lax.broadcasted_iota(jnp.int32, shape, axis_out)
    distance = (inner - outer).astype(F32)
    summed = jnp.zeros(shape, F32)
    for tap, weight in enumerate(weights):
        summed = jnp.where(distance == start + step * tap, weight, summed)
    return summed.astype(BF16)


def encode(values):
    return (values * jnp.abs(values)).astype(BF16)


def decode(codes):
    square = codes.astype(F32)
    return square * lax.rsqrt(jnp.maximum(jnp.abs(square), 1e-37))


def encode_fine(values):
    square = values * jnp.abs(values) * 2.0**32
    return (square * jnp.abs(square)).astype(BF16)


def decode_fine(codes):
    fourth = codes.astype(F32)
    square = fourth * lax.rsqrt(jnp.maximum(jnp.abs(fourth), 1e-37))
    return square * (lax.rsqrt(jnp.maximum(jnp.abs(square), 1e-30)) * 2.0**-16)


def dot(left, right):
    return jnp.dot(left, right, preferred_element_type=F32)


WIDE = GRID // 2
LEFT = pl.ds(0, WIDE)
RIGHT = pl.ds(WIDE, WIDE)


class Post:
    def __init__(self, sends, recvs):
        self.sends = sends
        self.recvs = recvs
        self.opened = []

    def go(self, src, dst, peer):
        k = len(self.opened)
        copy = pltpu.make_async_remote_copy(
            src_ref=src, dst_ref=dst, send_sem=self.sends.at[k], recv_sem=self.recvs.at[k],
            device_id=peer, device_id_type=MESH,
        )
        copy.start()
        self.opened.append(copy)
        return copy

    def finish(self):
        for copy in self.opened:
            copy.wait_send()


class Place:
    def __init__(self):
        self.ang = lax.axis_index("ang")
        self.me = lax.axis_index("slab")
        self.z = self.me // 2
        self.xh = self.me % 2

    def slab(self, dz, other):
        x = 1 - self.xh if other else self.xh
        return lax.rem(self.z + dz, 4) * 2 + x

    def peer(self, dz, other):
        return (self.ang, self.slab(dz, other))

    def block(self, dz, other):
        return block_of(self.slab(dz, other))


class Ring:
    def __init__(self, post, place, bufs, own, first, codec):
        self.post, self.place = post, place
        self.encode, self.decode = codec
        self.hr, self.fs, self.fr = bufs
        self.own, self.first = own, first

    def start(self):
        self.halves = [
            self.post.go(self.first(k), self.hr.at[k], self.place.peer((1, 3)[k], 0))
            for k in range(2)
        ]

    def middle(self):
        self.whole = []
        for k, dz in enumerate((1, 3)):
            lo = HALF * k
            self.fs[k, HALF - lo : ROWS - lo, :] = self.encode(self.own(dz, HALF - lo, HALF))
            self.halves[k].wait_recv()
            both = self.own(dz, lo, HALF) + self.decode(self.hr[k])
            self.fs[k, lo : lo + HALF, :] = self.encode(both)
            self.whole.append(self.post.go(self.fs.at[k], self.fr.at[k], self.place.peer(dz, 0)))

    def end(self):
        for copy in self.whole:
            copy.wait_recv()
        return self.own(0, 0, ROWS) + self.decode(self.fr[0]) + self.decode(self.fr[1])


class Reduce:
    def __init__(self, post, place, part, bufs, own, ref, codec):
        hs, hr, fs, fr, xs, xr = bufs
        self.post, self.place, self.own, self.ref = post, place, own, ref
        self.encode, self.decode = codec
        self.hs, self.xs, self.xr = hs.at[part], xs.at[part], xr.at[part]
        self.rings = []
        for chain, other in enumerate((1, 0)):
            self.rings.append(
                Ring(
                    post, place, (hr.at[part, chain], fs.at[part, chain], fr.at[part, chain]),
                    functools.partial(self.left, other),
                    functools.partial(self.left_first, other, chain), codec,
                )
            )
        self.rings.append(
            Ring(
                post, place, (hr.at[part, 2], fs.at[part, 2], fr.at[part, 2]),
                self.right, self.right_first, codec,
            )
        )
        self.crossing = {}

    def left(self, other, dz, lo, n):
        return self.own(dz, other, lo, n, LEFT)

    def left_first(self, other, chain, k):
        return self.ref(2, other, HALF * k, HALF, LEFT, self.hs.at[chain, k])

    def right(self, dz, lo, n):
        return self.own(dz, 0, lo, n, RIGHT) + self.decode(self.xr[dz, lo : lo + n, :])

    def right_first(self, k):
        self.hs[2, k] = self.encode(self.right(2, HALF * k, HALF))
        return self.hs.at[2, k]

    def start_far(self, other):
        self.rings[1 - other].start()

    def start_cross(self, dz):
        src = self.ref(dz, 1, 0, ROWS, RIGHT, self.xs.at[dz])
        self.crossing[dz] = self.post.go(src, self.xr.at[dz], self.place.peer(0, 1))

    def stage2(self):
        self.crossing[2].wait_recv()
        self.rings[2].start()

    def stage3(self):
        self.xs[4] = self.encode(self.rings[0].end())
        self.crossing[4] = self.post.go(self.xs.at[4], self.xr.at[4], self.place.peer(0, 1))

    def stage4(self):
        self.crossing[1].wait_recv()
        self.crossing[3].wait_recv()
        self.rings[2].middle()

    def stage5(self):
        mine = self.rings[1].end()
        self.crossing[4].wait_recv()
        return mine + self.decode(self.xr[4])

    def stage6(self):
        self.crossing[0].wait_recv()
        return self.rings[2].end()


def reduce_scratch():
    code = BF16
    return [
        pltpu.VMEM((2, 3, 2, HALF, WIDE), code),
        pltpu.VMEM((2, 3, 2, HALF, WIDE), code),
        pltpu.VMEM((2, 3, 2, ROWS, WIDE), code),
        pltpu.VMEM((2, 3, 2, ROWS, WIDE), code),
        pltpu.VMEM((2, 5, ROWS, WIDE), code),
        pltpu.VMEM((2, 5, ROWS, WIDE), code),
    ]


class Gather:
    def __init__(self, post, place, part, whole):
        self.post, self.place, self.part, self.whole = post, place, part, whole

    def span(self, dz, other, cols, lo=0, n=ROWS):
        start = pl.multiple_of(self.place.block(dz, other) * ROWS + lo, HALF)
        return self.whole.at[self.part, pl.ds(start, n), cols]

    def send(self, dz, other, cols, to_dz, to_other, lo=0, n=ROWS):
        span = self.span(dz, other, cols, lo, n)
        return self.post.go(span, span, self.place.peer(to_dz, to_other))

    def spread(self, other, cols):
        return [self.send(0, other, cols, dz, 0) for dz in (1, 3)]

    def relay(self, other, cols, pair):
        pair[0].wait_recv()
        first = self.send(3, other, cols, 1, 0, 0, HALF)
        pair[1].wait_recv()
        return [first, self.send(1, other, cols, 3, 0, HALF, HALF)]

    def stage0(self):
        self.cross_left = self.send(0, 0, LEFT, 0, 1)
        self.right = self.spread(0, RIGHT)
        self.cross_right = [self.send(0, 0, RIGHT, 0, 1)]
        self.left = self.spread(0, LEFT)

    def stage1(self):
        self.right_far = self.relay(0, RIGHT, self.right)
        for dz in (3, 1):
            self.cross_right.append(self.send(dz, 0, RIGHT, 0, 1))

    def stage2(self):
        self.cross_left.wait_recv()
        self.left_other = self.spread(1, LEFT)

    def stage3(self):
        self.left_far = self.relay(0, LEFT, self.left)

    def stage4(self):
        for copy in self.right_far:
            copy.wait_recv()
        self.cross_right.append(self.send(2, 0, RIGHT, 0, 1))

    def stage5(self):
        self.left_far += self.relay(1, LEFT, self.left_other)

    def stage6(self):
        for copy in self.left_far + self.cross_right:
            copy.wait_recv()


def greet(place):
    barrier = pltpu.get_barrier_semaphore()
    for dz in range(4):
        for other in range(2):
            if (dz, other) != (0, 0):
                pl.semaphore_signal(
                    barrier, inc=1, device_id=place.peer(dz, other), device_id_type=MESH
                )
    return barrier


def follow_reduces(reduces, done):
    for reduce in reduces:
        reduce.rings[0].middle()
    for reduce in reduces:
        reduce.stage2()
        reduce.start_cross(1)
        reduce.start_cross(3)
    for reduce in reduces:
        reduce.rings[1].middle()
    for reduce in reduces:
        reduce.stage3()
    for reduce in reduces:
        reduce.stage4()
        reduce.start_cross(0)
    for part, reduce in enumerate(reduces):
        done(part, reduce.stage5(), reduce.stage6())


def forward_kernel(
    offs, wts, obj, proj, par_all,
    opad, lift, t0, t1, dbuf, hs, hr, fs, fr, xs, xr,
    load_sem, sends, recvs,
):
    place = Place()
    barrier = greet(place)
    load = pltpu.make_async_copy(obj, opad.at[:, pl.ds(PAD, GRID), :], load_sem)
    load.start()
    opad[:, :PAD, :] = jnp.zeros((2, PAD, GRID), BF16)
    opad[:, PAD + GRID :, :] = jnp.zeros((2, PAD, GRID), BF16)
    lift[:, :PAD] = jnp.zeros((2 * ROWS, PAD), BF16)
    lift[:, PAD + GRID :] = jnp.zeros((2 * ROWS, PAD), BF16)
    off_y = offs[0].astype(F32)
    off_x = offs[1].astype(F32)
    taps = [wts[k] for k in range(8)]
    t0[...] = band(t0.shape, 0, off_y + float(PAD - 1), taps[:4], 1)
    t1[...] = band(t1.shape, 1, off_x + float(PAD - 1), taps[4:], 1)
    row_ids = lax.broadcasted_iota(jnp.int32, par_all.shape[1:], 0)
    par = jnp.zeros(par_all.shape[1:], F32)
    for k, value in enumerate(taps + [off_y, off_x]):
        par = jnp.where(row_ids == k, value, par)
    par_all[pl.ds(place.me, 1)] = par[None]
    load.wait()

    pl.semaphore_wait(barrier, NSLAB - 1)
    post = Post(sends, recvs)
    par_copies = []
    for dz in range(4):
        for other in range(2):
            if (dz, other) != (0, 0):
                span = par_all.at[place.me]
                par_copies.append(post.go(span, span, place.peer(dz, other)))

    def slot(dz, other):
        return 2 * dz + other

    def project(dz, other):
        start = pl.multiple_of(place.block(dz, other) * ROWS, ROWS)
        for part in range(2):
            rows = opad[part, pl.ds(start, 3 * PAD), :]
            lift[part * ROWS : (part + 1) * ROWS, PAD : PAD + GRID] = dot(t0[...], rows).astype(BF16)
        for q in range(GRID // 256):
            tile = dot(lift[:, 256 * q : 256 * q + 512], t1[...])
            dbuf[slot(dz, other), :, :, 256 * q : 256 * q + 256] = tile.reshape(2, ROWS, 256)

    bufs = (hs, hr, fs, fr, xs, xr)
    reduces = []
    for part in range(2):

        def own(dz, other, lo, n, cols, part=part):
            return dbuf[slot(dz, other), part, pl.ds(lo, n), cols]

        def ref(dz, other, lo, n, cols, room, part=part):
            room[...] = encode_fine(own(dz, other, lo, n, cols, part))
            return room

        reduces.append(Reduce(post, place, part, bufs, own, ref, (encode_fine, decode_fine)))
    for dz, other in ((2, 1), (2, 0), (1, 1), (3, 1), (0, 1), (1, 0), (3, 0), (0, 0)):
        project(dz, other)
        for reduce in reduces:
            if dz == 2:
                reduce.start_far(other)
                if other == 1:
                    reduce.start_cross(2)
    rows = pl.ds(pl.multiple_of(place.block(0, 0) * ROWS, ROWS), ROWS)
    gathers = [Gather(post, place, part, proj) for part in range(2)]

    def done(part, left, right):
        proj[part, rows, LEFT] = encode_fine(left)
        proj[part, rows, RIGHT] = encode_fine(right)
        gathers[part].stage0()

    follow_reduces(reduces, done)
    for k in range(1, 7):
        for gather in gathers:
            getattr(gather, "stage%d" % k)()
    for copy in par_copies:
        copy.wait_recv()
    post.finish()


def forward(offs, wts, obj):
    return pl.pallas_call(
        forward_kernel,
        out_shape=(
            jax.ShapeDtypeStruct((2, GRID, GRID), BF16),
            jax.ShapeDtypeStruct((NSLAB, 16, 512), F32),
        ),
        in_specs=[
            pl.BlockSpec(memory_space=pltpu.SMEM),
            pl.BlockSpec(memory_space=pltpu.SMEM),
            pl.BlockSpec(memory_space=pl.ANY),
        ],
        out_specs=(
            pl.BlockSpec(memory_space=pltpu.VMEM),
            pl.BlockSpec(memory_space=pltpu.VMEM),
        ),
        scratch_shapes=[
            pltpu.VMEM((2, GRID + 2 * PAD, GRID), BF16),
            pltpu.VMEM((2 * ROWS, GRID + 2 * PAD), BF16),
            pltpu.VMEM((ROWS, 3 * PAD), BF16),
            pltpu.VMEM((512, 256), BF16),
            pltpu.VMEM((NSLAB, 2, ROWS, GRID), F32),
        ]
        + reduce_scratch()
        + [
            pltpu.SemaphoreType.DMA,
            pltpu.SemaphoreType.DMA((96,)),
            pltpu.SemaphoreType.DMA((96,)),
        ],
        compiler_params=pltpu.CompilerParams(
            collective_id=0, has_side_effects=True, vmem_limit_bytes=VMEM_LIMIT
        ),
        name="forward",
    )(offs, wts, obj)


def dft_tables():
    index = np.arange(PATCH)
    phase = 2.0 * np.pi * ((index[:, None] * index[None, :]) % PATCH) / PATCH
    cosines = np.cos(phase) / math.sqrt(PATCH)
    sines = np.sin(phase) / math.sqrt(PATCH)
    whole = np.block([[cosines, -sines], [sines, cosines]]).astype(np.float32)
    high = whole.astype(jnp.bfloat16)
    low = (whole - high.astype(np.float32)).astype(jnp.bfloat16)
    across = np.concatenate([high, high, low], axis=0)
    down = np.concatenate([high.T, high.T, low.T], axis=1)
    return [np.ascontiguousarray(t) for t in (down, across, high, high.T)]


def split_join(values, axis):
    high = values.astype(BF16)
    low = (values - high.astype(F32)).astype(BF16)
    return jnp.concatenate([high, low, high], axis=axis)


CHUNKS = 8
CHUNK = GRID // CHUNKS


def slots_kernel(
    corners, count, proj, probe, diff, *refs,
):
    tables, refs = refs[:4], refs[4:]
    image, probe_part, proj_in, diff_in = refs[:4]
    left_f, right_f, left_i, right_i, wide, total, image_out, in_sem, out_sem, sem = refs[4:]

    def chunk_rows(k):
        return pl.ds(pl.multiple_of(k * CHUNK, CHUNK), CHUNK)

    def load(k):
        rows = chunk_rows(k)
        return pltpu.make_async_copy(proj.at[:, rows, :], proj_in.at[:, rows, :], in_sem.at[k])

    def store(k):
        rows = chunk_rows(k)
        return pltpu.make_async_copy(image_out.at[:, rows, :], image.at[:, rows, :], out_sem.at[k])

    for k in range(CHUNKS):
        load(k).start()
    later = [
        pltpu.make_async_copy(src, dst, sem.at[k])
        for k, (src, dst) in enumerate(
            zip(tables + (diff,), (left_f, right_f, left_i, right_i, diff_in))
        )
    ]
    for copy in later:
        copy.start()
    probe_part[...] = jnp.zeros(probe_part.shape, F32)

    def open_chunk(k, carry):
        rows = chunk_rows(k)
        for tile in range(GRID // 128 + 1):
            total[:, tile, rows, :] = jnp.zeros((2, CHUNK, 128), F32)
        load(k).wait()
        for tile in range(GRID // 128):
            wide[:, tile, rows, :] = decode_fine(proj_in[:, rows, 128 * tile : 128 * tile + 128])
        return carry

    lax.fori_loop(0, CHUNKS, open_chunk, 0)
    for copy in later:
        copy.wait()
    live = count[0, 0]
    lane = lax.broadcasted_iota(jnp.int32, (PATCH, 128), 1)
    zero = jnp.zeros((PATCH, 128), F32)
    probe_re = probe[0]
    probe_im = probe[1]

    def pair_step(pair, carry):
        waves = []
        places = []
        for k in range(2):
            slot = 2 * pair + k
            row = corners[0, 0, slot, 0]
            col = corners[0, 0, slot, 1]
            turn = lax.rem(col, 128)
            tile = col // 128
            early = lane < turn
            patch = []
            for part in range(2):
                window = [wide[part, tile + m, pl.ds(row, PATCH), :] for m in range(3)]
                joined = jnp.concatenate(
                    [jnp.where(early, window[2], window[0]), window[1]], axis=1
                )
                patch.append(pltpu.roll(joined, lax.rem(PATCH - turn, PATCH), 1))
            places.append((slot, row, turn, tile, early, patch))
            waves.append(
                jnp.concatenate(
                    [
                        probe_re * patch[0] - probe_im * patch[1],
                        probe_re * patch[1] + probe_im * patch[0],
                    ],
                    axis=0,
                )
            )
        half = dot(left_f[...], split_join(jnp.concatenate(waves, axis=1), 0))
        half = jnp.concatenate(
            [
                jnp.concatenate([half[:PATCH, cols], half[PATCH:, cols]], axis=1)
                for cols in (slice(0, PATCH), slice(PATCH, 2 * PATCH))
            ],
            axis=0,
        )
        far = dot(split_join(half, 1), right_f[...])
        resid = []
        for k in range(2):
            slot = places[k][0]
            far_re = far[PATCH * k : PATCH * k + PATCH, :PATCH]
            far_im = far[PATCH * k : PATCH * k + PATCH, PATCH:]
            weight = jnp.where(slot < live, 1.0 / math.sqrt(POSITIONS), 0.0)
            misfit = (far_re * far_re + far_im * far_im - diff_in[slot]) * weight
            resid.append(
                jnp.concatenate(
                    [(misfit * far_re).astype(BF16), (misfit * far_im).astype(BF16)], axis=0
                )
            )
        inner = dot(left_i[...], jnp.concatenate(resid, axis=1)).astype(BF16)
        inner = jnp.concatenate(
            [
                jnp.concatenate([inner[:PATCH, cols], inner[PATCH:, cols]], axis=1)
                for cols in (slice(0, PATCH), slice(PATCH, 2 * PATCH))
            ],
            axis=0,
        )
        chi = dot(inner, right_i[...])
        for k in range(2):
            slot, row, turn, tile, early, patch = places[k]
            chi_re = chi[PATCH * k : PATCH * k + PATCH, :PATCH]
            chi_im = chi[PATCH * k : PATCH * k + PATCH, PATCH:]
            probe_part[0] += patch[0] * chi_re + patch[1] * chi_im
            probe_part[1] += patch[0] * chi_im - patch[1] * chi_re
            grads = (
                probe_re * chi_re + probe_im * chi_im,
                probe_re * chi_im - probe_im * chi_re,
            )
            for part in range(2):
                turned = pltpu.roll(grads[part], turn, 1)
                head = turned[:, :128]
                spread = (
                    jnp.where(early, zero, head), turned[:, 128:], jnp.where(early, head, zero)
                )
                for m in range(3):
                    total[part, tile + m, pl.ds(row, PATCH), :] += spread[m]
        return carry

    lax.fori_loop(0, (live + 1) // 2, pair_step, 0)

    def close_chunk(k, carry):
        rows = chunk_rows(k)
        for tile in range(GRID // 128):
            image_out[:, rows, 128 * tile : 128 * tile + 128] = encode(total[:, tile, rows, :])
        store(k).start()
        return carry

    lax.fori_loop(0, CHUNKS, close_chunk, 0)
    for k in range(CHUNKS):
        store(k).wait()


def slots(corners, count, proj, probe, diffraction):
    tables = [jnp.asarray(t) for t in dft_tables()]
    whole = pl.BlockSpec(memory_space=pltpu.VMEM)
    scalar = pl.BlockSpec(memory_space=pltpu.SMEM)
    far = pl.BlockSpec(memory_space=pl.ANY)
    dma = pltpu.SemaphoreType.DMA
    return pl.pallas_call(
        slots_kernel,
        out_shape=(
            jax.ShapeDtypeStruct((2, GRID, GRID), BF16),
            jax.ShapeDtypeStruct((2, PATCH, PATCH), F32),
        ),
        in_specs=[scalar, scalar, far, whole, far] + [far] * 4,
        out_specs=(far, whole),
        scratch_shapes=[
            pltpu.VMEM((2, GRID, GRID), BF16),
            pltpu.VMEM((SLOTS, PATCH, PATCH), F32),
            pltpu.VMEM((512, 1536), BF16),
            pltpu.VMEM((1536, 512), BF16),
            pltpu.VMEM((512, 512), BF16),
            pltpu.VMEM((512, 512), BF16),
            pltpu.VMEM((2, GRID // 128 + 1, GRID, 128), F32),
            pltpu.VMEM((2, GRID // 128 + 1, GRID, 128), F32),
            pltpu.VMEM((2, GRID, GRID), BF16),
            dma((CHUNKS,)), dma((CHUNKS,)), dma((5,)),
        ],
        compiler_params=pltpu.CompilerParams(vmem_limit_bytes=VMEM_LIMIT),
        name="slots",
    )(corners, count, proj, probe, diffraction, *tables)


def backward_kernel(
    image, par_all, probe_part, result, probe_out,
    t0, t1, ext, padded, gbuf, cbuf, yhs, yhr, yfs, yfr, xsend, xrecv, keep, fin,
    pcode, pall, pbuf, pcore, py, pxl, psum, hs, hr, fs, fr, xs, xr,
    sends, recvs, fsend, frecv,
):
    place = Place()
    ang, me, z, xh = place.ang, place.me, place.z, place.xh
    core = lax.rem(ang, 2)
    chip = ang // 2
    y = lax.rem(chip, 4)
    xl = chip // 4
    mine = place.block(0, 0)

    def ang_id(xl_, y_, core_):
        return (xl_ * 4 + y_) * 2 + core_

    def y_peer(dy):
        return (ang_id(xl, lax.rem(y + dy, 4), core), me)

    xl_peer = (ang_id(1 - xl, y, core), me)
    core_peer = (ang_id(xl, y, 1 - core), me)
    turn_peer = (ang_id(xh, z, core), y * 2 + xl)
    stays = jnp.logical_and(xl == xh, y == z)
    above = (ang, slab_of(lax.rem(mine + NSLAB - 1, NSLAB)))
    below = (ang, slab_of(lax.rem(mine + 1, NSLAB)))

    barrier = greet(place)
    for peer in (y_peer(1), y_peer(2), y_peer(3), xl_peer, core_peer):
        pl.semaphore_signal(barrier, inc=1, device_id=peer, device_id_type=MESH)

    @pl.when(jnp.logical_not(stays))
    def _():
        pl.semaphore_signal(barrier, inc=1, device_id=turn_peer, device_id_type=MESH)

    def tables(s, carry):
        rows = [par_all[s, k : k + 1, :] for k in range(10)]
        t0[pl.ds(pl.multiple_of(s * ROWS, ROWS), ROWS), :] = band(
            (ROWS, 384), 0, HALO + 1 - rows[8][:, :384], [r[:, :384] for r in rows[:4]], -1
        )
        t1[s] = band((512, 256), 1, PAD + 1 - rows[9][:, :256], [r[:, :256] for r in rows[4:8]], -1)
        return carry

    lax.fori_loop(0, NSLAB, tables, 0)
    ext[:, HALO + ROWS + HALO :, :] = jnp.zeros((2, 384 - ROWS - 2 * HALO, GRID), BF16)
    padded[:, :PAD] = jnp.zeros((NSLAB * ROWS, PAD), BF16)
    padded[:, PAD + GRID :] = jnp.zeros((NSLAB * ROWS, PAD), BF16)
    pl.semaphore_wait(barrier, NSLAB - 1 + 5 + jnp.where(stays, 0, 1))

    post = Post(sends, recvs)
    peers = [(dz, other) for dz in range(4) for other in range(2)][1:]
    bufs = (hs, hr, fs, fr, xs, xr)
    reduces = []
    for part in range(2):

        def ref(dz, other, lo, n, cols, room, part=part):
            start = pl.multiple_of(place.block(dz, other) * ROWS + lo, HALF)
            return image.at[part, pl.ds(start, n), cols]

        def own(dz, other, lo, n, cols, part=part, ref=ref):
            return decode(ref(dz, other, lo, n, cols, None)[...])

        reduces.append(Reduce(post, place, part, bufs, own, ref, (encode, decode)))
    halos = {}

    def done(part, left, right):
        ext[part, HALO : HALO + ROWS, LEFT] = left.astype(BF16)
        ext[part, HALO : HALO + ROWS, RIGHT] = right.astype(BF16)
        halos[part] = [
            post.go(ext.at[part, pl.ds(HALO, HALO), :], ext.at[part, pl.ds(HALO + ROWS, HALO), :], above),
            post.go(ext.at[part, pl.ds(ROWS, HALO), :], ext.at[part, pl.ds(0, HALO), :], below),
        ]

    rings = {}

    class YPlace:
        @staticmethod
        def peer(dy, other):
            return y_peer(dy)

    def spread_slices(part):
        for copy in halos[part]:
            copy.wait_recv()

        @pl.when(mine == 0)
        def _():
            ext[part, :HALO, :] = jnp.zeros((HALO, GRID), BF16)

        @pl.when(mine == NSLAB - 1)
        def _():
            ext[part, HALO + ROWS : 2 * HALO + ROWS, :] = jnp.zeros((HALO, GRID), BF16)

        for q in range(GRID // 256):
            cols = pl.ds(256 * q, 256)
            padded[:, PAD + 256 * q : PAD + 256 * q + 256] = dot(t0[...], ext[part, :, cols]).astype(BF16)

        cores = {}

        def slice_step(j):
            dy, other = j // 2, j % 2
            s = lax.rem(y + dy, 4) * 2 + (1 - xl if other else xl)
            rows = pl.ds(pl.multiple_of(s * ROWS, ROWS), ROWS)
            stack = jnp.concatenate(
                [padded[rows, 256 * q : 256 * q + 512] for q in range(GRID // 256)], axis=0
            )
            tiles = encode(dot(stack, t1[s]))
            for q in range(GRID // 256):
                cols = slice(256 * q, 256 * q + 256)
                for half in range(2):
                    lo = ROWS * q + HALF * half
                    gbuf[part, half, j, :, cols] = tiles[lo : lo + HALF]
            cores[j] = post.go(gbuf.at[part, 1 - core, j], cbuf.at[part, j], core_peer)

        def arrived(*steps):
            for j in steps:
                cores[j].wait_recv()

        def own(dy, lo, n):
            both = [
                decode(gbuf[part, core, j]) + decode(cbuf[part, j])
                for j in range(2 * dy + lo // HALF, 2 * dy + (lo + n) // HALF)
            ]
            return both[0] if len(both) == 1 else jnp.concatenate(both, axis=0)

        def far(k):
            yhs[part, k] = encode(own(2, HALF * k, HALF))
            return yhs.at[part, k]

        ring = Ring(
            post, YPlace, (yhr.at[part], yfs.at[part], yfr.at[part]), own, far, (encode, decode)
        )
        slice_step(4)
        slice_step(5)
        slice_step(2)
        arrived(4, 5)
        ring.start()
        slice_step(3)
        slice_step(6)
        slice_step(7)
        arrived(2, 3, 6, 7)
        ring.middle()
        slice_step(0)
        slice_step(1)
        rings[part] = (ring, functools.partial(arrived, 0, 1))

    sides = {}

    def settle_y(part):
        ring, ready = rings[part]
        ready()
        total = ring.end()
        xsend[part] = encode(total[HALF:])
        sides[part] = post.go(xsend.at[part], xrecv.at[part], xl_peer)
        keep[part] = total[:HALF]

    def settle(part):
        sides[part].wait_recv()
        fin[part] = encode(keep[part] + decode(xrecv[part]))

        @pl.when(stays)
        def _():
            result[part] = fin[part]

        @pl.when(jnp.logical_not(stays))
        def _():
            turn_copy(part).start()

    def turn_copy(part):
        return pltpu.make_async_remote_copy(
            src_ref=fin.at[part], dst_ref=result.at[part], send_sem=fsend.at[part],
            recv_sem=frecv.at[part], device_id=turn_peer, device_id_type=MESH,
        )

    pcode[...] = encode(probe_part[...])
    probe_copies = []
    for dz, other in peers:
        rows = pl.ds(pl.multiple_of(place.slab(dz, other) * 64, 64), 64)
        probe_copies.append(post.go(pcode.at[rows, :], pbuf.at[2 * dz + other], place.peer(dz, other)))
    first, second = reduces

    def open_reduce(reduce):
        reduce.start_cross(2)
        reduce.start_far(1)
        reduce.start_far(0)

    def more_cross(reduce):
        reduce.start_cross(1)
        reduce.start_cross(3)

    open_reduce(first)
    first.rings[0].middle()
    open_reduce(second)
    first.stage2()
    more_cross(first)
    first.rings[1].middle()
    first.start_cross(0)
    first.stage3()
    second.rings[0].middle()

    total = probe_part[pl.ds(pl.multiple_of(me * 64, 64), 64), :]
    for copy, (dz, other) in zip(probe_copies, peers):
        copy.wait_recv()
        total = total + decode(pbuf[2 * dz + other])
    psum[0] = encode(total)
    core_probe = post.go(psum.at[0], pcore, core_peer)

    first.stage4()
    second.stage2()
    more_cross(second)
    second.rings[1].middle()

    core_probe.wait_recv()
    psum[1] = encode(decode(psum[0]) + decode(pcore[...]))
    y_copies = [post.go(psum.at[1], py.at[j], y_peer(j)) for j in range(1, 4)]

    done(0, first.stage5(), first.stage6())
    second.start_cross(0)
    second.stage3()

    for copy in y_copies:
        copy.wait_recv()
    psum[2] = encode((decode(psum[1]) + decode(py[1])) + (decode(py[2]) + decode(py[3])))
    xl_probe = post.go(psum.at[2], pxl, xl_peer)

    second.stage4()
    done(1, second.stage5(), second.stage6())
    spread_slices(0)

    xl_probe.wait_recv()
    span = pall.at[pl.ds(pl.multiple_of(me * 64, 64), 64), :]
    span[...] = encode(decode(psum[2]) + decode(pxl[...]))
    out_copies = [post.go(span, span, place.peer(*peer)) for peer in peers]

    spread_slices(1)
    settle_y(0)
    settle(0)
    settle_y(1)
    settle(1)
    for copy in out_copies:
        copy.wait_recv()

    @pl.when(jnp.logical_not(stays))
    def _():
        turn_copy(0).wait()
        turn_copy(1).wait()

    probe_out[...] = decode(pall[...])
    post.finish()


def backward(image, par_all, probe_part):
    whole = pl.BlockSpec(memory_space=pltpu.VMEM)
    dma = pltpu.SemaphoreType.DMA
    return pl.pallas_call(
        backward_kernel,
        out_shape=(
            jax.ShapeDtypeStruct((2, HALF, GRID), BF16),
            jax.ShapeDtypeStruct((2 * PATCH, PATCH), F32),
        ),
        in_specs=[whole] * 3,
        out_specs=(whole, whole),
        scratch_shapes=[
            pltpu.VMEM((NSLAB * ROWS, 384), BF16),
            pltpu.VMEM((NSLAB, 512, 256), BF16),
            pltpu.VMEM((2, 384, GRID), BF16),
            pltpu.VMEM((NSLAB * ROWS, GRID + 2 * PAD), BF16),
            pltpu.VMEM((2, 2, NSLAB, HALF, GRID), BF16),
            pltpu.VMEM((2, NSLAB, HALF, GRID), BF16),
            pltpu.VMEM((2, 2, HALF, GRID), BF16),
            pltpu.VMEM((2, 2, HALF, GRID), BF16),
            pltpu.VMEM((2, 2, ROWS, GRID), BF16),
            pltpu.VMEM((2, 2, ROWS, GRID), BF16),
            pltpu.VMEM((2, HALF, GRID), BF16),
            pltpu.VMEM((2, HALF, GRID), BF16),
            pltpu.VMEM((2, HALF, GRID), F32),
            pltpu.VMEM((2, HALF, GRID), BF16),
            pltpu.VMEM((2 * PATCH, PATCH), BF16),
            pltpu.VMEM((2 * PATCH, PATCH), BF16),
            pltpu.VMEM((NSLAB, 64, PATCH), BF16),
            pltpu.VMEM((64, PATCH), BF16),
            pltpu.VMEM((4, 64, PATCH), BF16),
            pltpu.VMEM((64, PATCH), BF16),
            pltpu.VMEM((3, 64, PATCH), BF16),
        ]
        + reduce_scratch()
        + [dma((96,)), dma((96,)), dma((2,)), dma((2,))],
        compiler_params=pltpu.CompilerParams(
            collective_id=1, has_side_effects=True, vmem_limit_bytes=VMEM_LIMIT
        ),
        name="backward",
    )(image, par_all, probe_part)


def per_device(
    object_field, probe_field, diffraction, scan_offsets, counts, band_weights, band_offsets
):
    ang = lax.axis_index("ang")
    weights = lax.dynamic_index_in_dim(band_weights, ang, 0, keepdims=False)[0]
    offsets = lax.dynamic_index_in_dim(band_offsets, ang, 0, keepdims=False)[0]
    proj, par_all = forward(
        offsets,
        weights.astype(F32).reshape(8),
        object_field.reshape(2, GRID, GRID),
    )
    image, probe_part = slots(
        scan_offsets, counts, proj, probe_field, diffraction[0, 0]
    )
    result, probe_out = backward(image, par_all, probe_part.reshape(2 * PATCH, PATCH))
    object_grad = decode(jnp.transpose(result, (1, 0, 2)))[:, :, None, :]
    return (object_grad, probe_out.reshape(2, PATCH, PATCH))


def solution(mesh):
    placed = (
        P(None, "slab", None, None),
        P(),
        P("ang", "slab", None, None, None),
        P("ang", "slab", None, None),
        P("slab", "ang"),
        P(None, "slab", None, None),
        P(None, "slab", None),
    )
    return jax.shard_map(
        per_device,
        mesh=mesh,
        in_specs=placed,
        out_specs=(P("ang", None, "slab", None), P()),
        check_vma=False,
    )
```

```python
import functools
import math

import jax
import jax.numpy as jnp
import numpy as np
from jax import lax
from jax.experimental import pallas as pl
from jax.experimental.pallas import tpu as pltpu
from jax.sharding import PartitionSpec as P

MESH = pl.DeviceIdType.MESH
F32 = jnp.float32
BF16 = jnp.bfloat16
GRID = 1024
PATCH = 256
SLOTS = 8
NSLAB = 8
ROWS = GRID // NSLAB
HALF = ROWS // 2
PAD = 128
HALO = 80
POSITIONS = 512


def block_of(slab):
    return (slab % 2) * 4 + slab // 2


def slab_of(block):
    return (block % 4) * 2 + block // 4


def band(shape, axis_out, start, weights, step):
    inner = lax.broadcasted_iota(jnp.int32, shape, 1 - axis_out)
    outer = lax.broadcasted_iota(jnp.int32, shape, axis_out)
    distance = (inner - outer).astype(F32)
    summed = jnp.zeros(shape, F32)
    for tap, weight in enumerate(weights):
        summed = jnp.where(distance == start + step * tap, weight, summed)
    return summed.astype(BF16)


def encode(values):
    return (values * jnp.abs(values)).astype(BF16)


def decode(codes):
    square = codes.astype(F32)
    return square * lax.rsqrt(jnp.maximum(jnp.abs(square), 1e-37))


def encode_fine(values):
    square = values * jnp.abs(values) * 2.0**32
    return (square * jnp.abs(square)).astype(BF16)


def decode_fine(codes):
    fourth = codes.astype(F32)
    square = fourth * lax.rsqrt(jnp.maximum(jnp.abs(fourth), 1e-37))
    return square * (lax.rsqrt(jnp.maximum(jnp.abs(square), 1e-30)) * 2.0**-16)


def dot(left, right):
    return jnp.dot(left, right, preferred_element_type=F32)


WIDE = GRID // 2
LEFT = pl.ds(0, WIDE)
RIGHT = pl.ds(WIDE, WIDE)


class Post:
    def __init__(self, sends, recvs):
        self.sends = sends
        self.recvs = recvs
        self.opened = []

    def go(self, src, dst, peer):
        k = len(self.opened)
        copy = pltpu.make_async_remote_copy(
            src_ref=src, dst_ref=dst, send_sem=self.sends.at[k], recv_sem=self.recvs.at[k],
            device_id=peer, device_id_type=MESH,
        )
        copy.start()
        self.opened.append(copy)
        return copy

    def finish(self):
        for copy in self.opened:
            copy.wait_send()


class Place:
    def __init__(self):
        self.ang = lax.axis_index("ang")
        self.me = lax.axis_index("slab")
        self.z = self.me // 2
        self.xh = self.me % 2

    def slab(self, dz, other):
        x = 1 - self.xh if other else self.xh
        return lax.rem(self.z + dz, 4) * 2 + x

    def peer(self, dz, other):
        return (self.ang, self.slab(dz, other))

    def block(self, dz, other):
        return block_of(self.slab(dz, other))


class Ring:
    def __init__(self, post, place, bufs, own, first, codec):
        self.post, self.place = post, place
        self.encode, self.decode = codec
        self.hr, self.fs, self.fr = bufs
        self.own, self.first = own, first

    def start(self):
        self.halves = [
            self.post.go(self.first(k), self.hr.at[k], self.place.peer((1, 3)[k], 0))
            for k in range(2)
        ]

    def middle(self):
        self.whole = []
        for k, dz in enumerate((1, 3)):
            lo = HALF * k
            self.fs[k, HALF - lo : ROWS - lo, :] = self.encode(self.own(dz, HALF - lo, HALF))
            self.halves[k].wait_recv()
            both = self.own(dz, lo, HALF) + self.decode(self.hr[k])
            self.fs[k, lo : lo + HALF, :] = self.encode(both)
            self.whole.append(self.post.go(self.fs.at[k], self.fr.at[k], self.place.peer(dz, 0)))

    def end(self):
        for copy in self.whole:
            copy.wait_recv()
        return self.own(0, 0, ROWS) + self.decode(self.fr[0]) + self.decode(self.fr[1])


class Reduce:
    def __init__(self, post, place, part, bufs, own, ref, codec):
        hs, hr, fs, fr, xs, xr = bufs
        self.post, self.place, self.own, self.ref = post, place, own, ref
        self.encode, self.decode = codec
        self.hs, self.xs, self.xr = hs.at[part], xs.at[part], xr.at[part]
        self.rings = []
        for chain, other in enumerate((1, 0)):
            self.rings.append(
                Ring(
                    post, place, (hr.at[part, chain], fs.at[part, chain], fr.at[part, chain]),
                    functools.partial(self.left, other),
                    functools.partial(self.left_first, other, chain), codec,
                )
            )
        self.rings.append(
            Ring(
                post, place, (hr.at[part, 2], fs.at[part, 2], fr.at[part, 2]),
                self.right, self.right_first, codec,
            )
        )
        self.crossing = {}

    def left(self, other, dz, lo, n):
        return self.own(dz, other, lo, n, LEFT)

    def left_first(self, other, chain, k):
        return self.ref(2, other, HALF * k, HALF, LEFT, self.hs.at[chain, k])

    def right(self, dz, lo, n):
        return self.own(dz, 0, lo, n, RIGHT) + self.decode(self.xr[dz, lo : lo + n, :])

    def right_first(self, k):
        self.hs[2, k] = self.encode(self.right(2, HALF * k, HALF))
        return self.hs.at[2, k]

    def start_far(self, other):
        self.rings[1 - other].start()

    def start_cross(self, dz):
        src = self.ref(dz, 1, 0, ROWS, RIGHT, self.xs.at[dz])
        self.crossing[dz] = self.post.go(src, self.xr.at[dz], self.place.peer(0, 1))

    def stage2(self):
        self.crossing[2].wait_recv()
        self.rings[2].start()

    def stage3(self):
        self.xs[4] = self.encode(self.rings[0].end())
        self.crossing[4] = self.post.go(self.xs.at[4], self.xr.at[4], self.place.peer(0, 1))

    def stage4(self):
        self.crossing[1].wait_recv()
        self.crossing[3].wait_recv()
        self.rings[2].middle()

    def stage5(self):
        mine = self.rings[1].end()
        self.crossing[4].wait_recv()
        return mine + self.decode(self.xr[4])

    def stage6(self):
        self.crossing[0].wait_recv()
        return self.rings[2].end()


def reduce_scratch():
    code = BF16
    return [
        pltpu.VMEM((2, 3, 2, HALF, WIDE), code),
        pltpu.VMEM((2, 3, 2, HALF, WIDE), code),
        pltpu.VMEM((2, 3, 2, ROWS, WIDE), code),
        pltpu.VMEM((2, 3, 2, ROWS, WIDE), code),
        pltpu.VMEM((2, 5, ROWS, WIDE), code),
        pltpu.VMEM((2, 5, ROWS, WIDE), code),
    ]


class Gather:
    def __init__(self, post, place, part, whole):
        self.post, self.place, self.part, self.whole = post, place, part, whole

    def span(self, dz, other, cols, lo=0, n=ROWS):
        start = pl.multiple_of(self.place.block(dz, other) * ROWS + lo, HALF)
        return self.whole.at[self.part, pl.ds(start, n), cols]

    def send(self, dz, other, cols, to_dz, to_other, lo=0, n=ROWS):
        span = self.span(dz, other, cols, lo, n)
        return self.post.go(span, span, self.place.peer(to_dz, to_other))

    def spread(self, other, cols):
        return [self.send(0, other, cols, dz, 0) for dz in (1, 3)]

    def relay(self, other, cols, pair):
        pair[0].wait_recv()
        first = self.send(3, other, cols, 1, 0, 0, HALF)
        pair[1].wait_recv()
        return [first, self.send(1, other, cols, 3, 0, HALF, HALF)]

    def stage0(self):
        self.cross_left = self.send(0, 0, LEFT, 0, 1)
        self.right = self.spread(0, RIGHT)
        self.cross_right = [self.send(0, 0, RIGHT, 0, 1)]
        self.left = self.spread(0, LEFT)

    def stage1(self):
        self.right_far = self.relay(0, RIGHT, self.right)
        for dz in (3, 1):
            self.cross_right.append(self.send(dz, 0, RIGHT, 0, 1))

    def stage2(self):
        self.cross_left.wait_recv()
        self.left_other = self.spread(1, LEFT)

    def stage3(self):
        self.left_far = self.relay(0, LEFT, self.left)

    def stage4(self):
        for copy in self.right_far:
            copy.wait_recv()
        self.cross_right.append(self.send(2, 0, RIGHT, 0, 1))

    def stage5(self):
        self.left_far += self.relay(1, LEFT, self.left_other)

    def stage6(self):
        for copy in self.left_far + self.cross_right:
            copy.wait_recv()


def greet(place):
    barrier = pltpu.get_barrier_semaphore()
    for dz in range(4):
        for other in range(2):
            if (dz, other) != (0, 0):
                pl.semaphore_signal(
                    barrier, inc=1, device_id=place.peer(dz, other), device_id_type=MESH
                )
    return barrier


def follow_reduces(reduces, done):
    for reduce in reduces:
        reduce.rings[0].middle()
    for reduce in reduces:
        reduce.stage2()
        reduce.start_cross(1)
        reduce.start_cross(3)
    for reduce in reduces:
        reduce.rings[1].middle()
    for reduce in reduces:
        reduce.stage3()
    for reduce in reduces:
        reduce.stage4()
        reduce.start_cross(0)
    for part, reduce in enumerate(reduces):
        done(part, reduce.stage5(), reduce.stage6())


def forward_kernel(
    offs, wts, obj, proj, par_all,
    opad, lift, t0, t1, dbuf, hs, hr, fs, fr, xs, xr,
    load_sem, sends, recvs,
):
    place = Place()
    barrier = greet(place)
    load = pltpu.make_async_copy(obj, opad.at[:, pl.ds(PAD, GRID), :], load_sem)
    load.start()
    opad[:, :PAD, :] = jnp.zeros((2, PAD, GRID), BF16)
    opad[:, PAD + GRID :, :] = jnp.zeros((2, PAD, GRID), BF16)
    lift[:, :PAD] = jnp.zeros((2 * ROWS, PAD), BF16)
    lift[:, PAD + GRID :] = jnp.zeros((2 * ROWS, PAD), BF16)
    off_y = offs[0].astype(F32)
    off_x = offs[1].astype(F32)
    taps = [wts[k] for k in range(8)]
    t0[...] = band(t0.shape, 0, off_y + float(PAD - 1), taps[:4], 1)
    t1[...] = band(t1.shape, 1, off_x + float(PAD - 1), taps[4:], 1)
    row_ids = lax.broadcasted_iota(jnp.int32, par_all.shape[1:], 0)
    par = jnp.zeros(par_all.shape[1:], F32)
    for k, value in enumerate(taps + [off_y, off_x]):
        par = jnp.where(row_ids == k, value, par)
    par_all[pl.ds(place.me, 1)] = par[None]
    load.wait()

    pl.semaphore_wait(barrier, NSLAB - 1)
    post = Post(sends, recvs)
    par_copies = []
    for dz in range(4):
        for other in range(2):
            if (dz, other) != (0, 0):
                span = par_all.at[place.me]
                par_copies.append(post.go(span, span, place.peer(dz, other)))

    def slot(dz, other):
        return 2 * dz + other

    def project(dz, other):
        start = pl.multiple_of(place.block(dz, other) * ROWS, ROWS)
        for part in range(2):
            rows = opad[part, pl.ds(start, 3 * PAD), :]
            lift[part * ROWS : (part + 1) * ROWS, PAD : PAD + GRID] = dot(t0[...], rows).astype(BF16)
        for q in range(GRID // 256):
            tile = dot(lift[:, 256 * q : 256 * q + 512], t1[...])
            dbuf[slot(dz, other), :, :, 256 * q : 256 * q + 256] = tile.reshape(2, ROWS, 256)

    bufs = (hs, hr, fs, fr, xs, xr)
    reduces = []
    for part in range(2):

        def own(dz, other, lo, n, cols, part=part):
            return dbuf[slot(dz, other), part, pl.ds(lo, n), cols]

        def ref(dz, other, lo, n, cols, room, part=part):
            room[...] = encode_fine(own(dz, other, lo, n, cols, part))
            return room

        reduces.append(Reduce(post, place, part, bufs, own, ref, (encode_fine, decode_fine)))
    for dz, other in ((2, 1), (2, 0), (1, 1), (3, 1), (0, 1), (1, 0), (3, 0), (0, 0)):
        project(dz, other)
        for reduce in reduces:
            if dz == 2:
                reduce.start_far(other)
                if other == 1:
                    reduce.start_cross(2)
    rows = pl.ds(pl.multiple_of(place.block(0, 0) * ROWS, ROWS), ROWS)
    gathers = [Gather(post, place, part, proj) for part in range(2)]

    def done(part, left, right):
        proj[part, rows, LEFT] = encode_fine(left)
        proj[part, rows, RIGHT] = encode_fine(right)
        gathers[part].stage0()

    follow_reduces(reduces, done)
    for k in range(1, 7):
        for gather in gathers:
            getattr(gather, "stage%d" % k)()
    for copy in par_copies:
        copy.wait_recv()
    post.finish()


def forward(offs, wts, obj):
    return pl.pallas_call(
        forward_kernel,
        out_shape=(
            jax.ShapeDtypeStruct((2, GRID, GRID), BF16),
            jax.ShapeDtypeStruct((NSLAB, 16, 512), F32),
        ),
        in_specs=[
            pl.BlockSpec(memory_space=pltpu.SMEM),
            pl.BlockSpec(memory_space=pltpu.SMEM),
            pl.BlockSpec(memory_space=pl.ANY),
        ],
        out_specs=(
            pl.BlockSpec(memory_space=pltpu.VMEM),
            pl.BlockSpec(memory_space=pltpu.VMEM),
        ),
        scratch_shapes=[
            pltpu.VMEM((2, GRID + 2 * PAD, GRID), BF16),
            pltpu.VMEM((2 * ROWS, GRID + 2 * PAD), BF16),
            pltpu.VMEM((ROWS, 3 * PAD), BF16),
            pltpu.VMEM((512, 256), BF16),
            pltpu.VMEM((NSLAB, 2, ROWS, GRID), F32),
        ]
        + reduce_scratch()
        + [
            pltpu.SemaphoreType.DMA,
            pltpu.SemaphoreType.DMA((96,)),
            pltpu.SemaphoreType.DMA((96,)),
        ],
        compiler_params=pltpu.CompilerParams(
            collective_id=0, has_side_effects=True, vmem_limit_bytes=34 << 20
        ),
        name="forward",
    )(offs, wts, obj)


def dft_tables():
    index = np.arange(PATCH)
    phase = 2.0 * np.pi * ((index[:, None] * index[None, :]) % PATCH) / PATCH
    cosines = np.cos(phase) / math.sqrt(PATCH)
    sines = np.sin(phase) / math.sqrt(PATCH)
    whole = np.block([[cosines, -sines], [sines, cosines]]).astype(np.float32)
    high = whole.astype(jnp.bfloat16)
    low = (whole - high.astype(np.float32)).astype(jnp.bfloat16)
    across = np.concatenate([high, high, low], axis=0)
    down = np.concatenate([high.T, high.T, low.T], axis=1)
    return [np.ascontiguousarray(t) for t in (down, across, high, high.T)]


def split_join(values, axis):
    high = values.astype(BF16)
    low = (values - high.astype(F32)).astype(BF16)
    return jnp.concatenate([high, low, high], axis=axis)


CHUNKS = 8
CHUNK = GRID // CHUNKS


def slots_kernel(
    corners, count, proj, probe, diff, *refs,
):
    tables, refs = refs[:4], refs[4:]
    image, probe_part, proj_in, diff_in = refs[:4]
    left_f, right_f, left_i, right_i, wide, total, image_out, in_sem, out_sem, sem = refs[4:]

    def chunk_rows(k):
        return pl.ds(pl.multiple_of(k * CHUNK, CHUNK), CHUNK)

    def load(k):
        rows = chunk_rows(k)
        return pltpu.make_async_copy(proj.at[:, rows, :], proj_in.at[:, rows, :], in_sem.at[k])

    def store(k):
        rows = chunk_rows(k)
        return pltpu.make_async_copy(image_out.at[:, rows, :], image.at[:, rows, :], out_sem.at[k])

    for k in range(CHUNKS):
        load(k).start()
    later = [
        pltpu.make_async_copy(src, dst, sem.at[k])
        for k, (src, dst) in enumerate(
            zip(tables + (diff,), (left_f, right_f, left_i, right_i, diff_in))
        )
    ]
    for copy in later:
        copy.start()
    probe_part[...] = jnp.zeros(probe_part.shape, F32)

    def open_chunk(k, carry):
        rows = chunk_rows(k)
        for tile in range(GRID // 128 + 1):
            total[:, tile, rows, :] = jnp.zeros((2, CHUNK, 128), F32)
        load(k).wait()
        for tile in range(GRID // 128):
            wide[:, tile, rows, :] = decode_fine(proj_in[:, rows, 128 * tile : 128 * tile + 128])
        return carry

    lax.fori_loop(0, CHUNKS, open_chunk, 0)
    for copy in later:
        copy.wait()
    live = count[0, 0]
    lane = lax.broadcasted_iota(jnp.int32, (PATCH, 128), 1)
    zero = jnp.zeros((PATCH, 128), F32)
    probe_re = probe[0]
    probe_im = probe[1]

    def pair_step(pair, carry):
        waves = []
        places = []
        for k in range(2):
            slot = 2 * pair + k
            row = corners[0, 0, slot, 0]
            col = corners[0, 0, slot, 1]
            turn = lax.rem(col, 128)
            tile = col // 128
            early = lane < turn
            patch = []
            for part in range(2):
                window = [wide[part, tile + m, pl.ds(row, PATCH), :] for m in range(3)]
                joined = jnp.concatenate(
                    [jnp.where(early, window[2], window[0]), window[1]], axis=1
                )
                patch.append(pltpu.roll(joined, lax.rem(PATCH - turn, PATCH), 1))
            places.append((slot, row, turn, tile, early, patch))
            waves.append(
                jnp.concatenate(
                    [
                        probe_re * patch[0] - probe_im * patch[1],
                        probe_re * patch[1] + probe_im * patch[0],
                    ],
                    axis=0,
                )
            )
        half = dot(left_f[...], split_join(jnp.concatenate(waves, axis=1), 0))
        half = jnp.concatenate(
            [
                jnp.concatenate([half[:PATCH, cols], half[PATCH:, cols]], axis=1)
                for cols in (slice(0, PATCH), slice(PATCH, 2 * PATCH))
            ],
            axis=0,
        )
        far = dot(split_join(half, 1), right_f[...])
        resid = []
        for k in range(2):
            slot = places[k][0]
            far_re = far[PATCH * k : PATCH * k + PATCH, :PATCH]
            far_im = far[PATCH * k : PATCH * k + PATCH, PATCH:]
            weight = jnp.where(slot < live, 1.0 / math.sqrt(POSITIONS), 0.0)
            misfit = (far_re * far_re + far_im * far_im - diff_in[slot]) * weight
            resid.append(
                jnp.concatenate(
                    [(misfit * far_re).astype(BF16), (misfit * far_im).astype(BF16)], axis=0
                )
            )
        inner = dot(left_i[...], jnp.concatenate(resid, axis=1)).astype(BF16)
        inner = jnp.concatenate(
            [
                jnp.concatenate([inner[:PATCH, cols], inner[PATCH:, cols]], axis=1)
                for cols in (slice(0, PATCH), slice(PATCH, 2 * PATCH))
            ],
            axis=0,
        )
        chi = dot(inner, right_i[...])
        for k in range(2):
            slot, row, turn, tile, early, patch = places[k]
            chi_re = chi[PATCH * k : PATCH * k + PATCH, :PATCH]
            chi_im = chi[PATCH * k : PATCH * k + PATCH, PATCH:]
            probe_part[0] += patch[0] * chi_re + patch[1] * chi_im
            probe_part[1] += patch[0] * chi_im - patch[1] * chi_re
            grads = (
                probe_re * chi_re + probe_im * chi_im,
                probe_re * chi_im - probe_im * chi_re,
            )
            for part in range(2):
                turned = pltpu.roll(grads[part], turn, 1)
                head = turned[:, :128]
                spread = (
                    jnp.where(early, zero, head), turned[:, 128:], jnp.where(early, head, zero)
                )
                for m in range(3):
                    total[part, tile + m, pl.ds(row, PATCH), :] += spread[m]
        return carry

    lax.fori_loop(0, (live + 1) // 2, pair_step, 0)

    def close_chunk(k, carry):
        rows = chunk_rows(k)
        for tile in range(GRID // 128):
            image_out[:, rows, 128 * tile : 128 * tile + 128] = encode(total[:, tile, rows, :])
        store(k).start()
        return carry

    lax.fori_loop(0, CHUNKS, close_chunk, 0)
    for k in range(CHUNKS):
        store(k).wait()


def slots(corners, count, proj, probe, diffraction):
    tables = [jnp.asarray(t) for t in dft_tables()]
    whole = pl.BlockSpec(memory_space=pltpu.VMEM)
    scalar = pl.BlockSpec(memory_space=pltpu.SMEM)
    far = pl.BlockSpec(memory_space=pl.ANY)
    dma = pltpu.SemaphoreType.DMA
    return pl.pallas_call(
        slots_kernel,
        out_shape=(
            jax.ShapeDtypeStruct((2, GRID, GRID), BF16),
            jax.ShapeDtypeStruct((2, PATCH, PATCH), F32),
        ),
        in_specs=[scalar, scalar, far, whole, far] + [far] * 4,
        out_specs=(far, whole),
        scratch_shapes=[
            pltpu.VMEM((2, GRID, GRID), BF16),
            pltpu.VMEM((SLOTS, PATCH, PATCH), F32),
            pltpu.VMEM((512, 1536), BF16),
            pltpu.VMEM((1536, 512), BF16),
            pltpu.VMEM((512, 512), BF16),
            pltpu.VMEM((512, 512), BF16),
            pltpu.VMEM((2, GRID // 128 + 1, GRID, 128), F32),
            pltpu.VMEM((2, GRID // 128 + 1, GRID, 128), F32),
            pltpu.VMEM((2, GRID, GRID), BF16),
            dma((CHUNKS,)), dma((CHUNKS,)), dma((5,)),
        ],
        compiler_params=pltpu.CompilerParams(vmem_limit_bytes=44 << 20),
        name="slots",
    )(corners, count, proj, probe, diffraction, *tables)


def backward_kernel(
    image, par_all, probe_part, result, probe_out,
    t0, t1, ext, padded, gbuf, cbuf, yhs, yhr, yfs, yfr, xsend, xrecv, keep, fin,
    pcode, pall, pbuf, pcore, py, pxl, psum, hs, hr, fs, fr, xs, xr,
    sends, recvs, fsend, frecv,
):
    place = Place()
    ang, me, z, xh = place.ang, place.me, place.z, place.xh
    core = lax.rem(ang, 2)
    chip = ang // 2
    y = lax.rem(chip, 4)
    xl = chip // 4
    mine = place.block(0, 0)

    def ang_id(xl_, y_, core_):
        return (xl_ * 4 + y_) * 2 + core_

    def y_peer(dy):
        return (ang_id(xl, lax.rem(y + dy, 4), core), me)

    xl_peer = (ang_id(1 - xl, y, core), me)
    core_peer = (ang_id(xl, y, 1 - core), me)
    turn_peer = (ang_id(xh, z, core), y * 2 + xl)
    stays = jnp.logical_and(xl == xh, y == z)
    above = (ang, slab_of(lax.rem(mine + NSLAB - 1, NSLAB)))
    below = (ang, slab_of(lax.rem(mine + 1, NSLAB)))

    barrier = greet(place)
    for peer in (y_peer(1), y_peer(2), y_peer(3), xl_peer, core_peer):
        pl.semaphore_signal(barrier, inc=1, device_id=peer, device_id_type=MESH)

    @pl.when(jnp.logical_not(stays))
    def _():
        pl.semaphore_signal(barrier, inc=1, device_id=turn_peer, device_id_type=MESH)

    def tables(s, carry):
        rows = [par_all[s, k : k + 1, :] for k in range(10)]
        t0[pl.ds(pl.multiple_of(s * ROWS, ROWS), ROWS), :] = band(
            (ROWS, 384), 0, HALO + 1 - rows[8][:, :384], [r[:, :384] for r in rows[:4]], -1
        )
        t1[s] = band((512, 256), 1, PAD + 1 - rows[9][:, :256], [r[:, :256] for r in rows[4:8]], -1)
        return carry

    lax.fori_loop(0, NSLAB, tables, 0)
    ext[:, HALO + ROWS + HALO :, :] = jnp.zeros((2, 384 - ROWS - 2 * HALO, GRID), BF16)
    padded[:, :PAD] = jnp.zeros((NSLAB * ROWS, PAD), BF16)
    padded[:, PAD + GRID :] = jnp.zeros((NSLAB * ROWS, PAD), BF16)
    pl.semaphore_wait(barrier, NSLAB - 1 + 5 + jnp.where(stays, 0, 1))

    post = Post(sends, recvs)
    peers = [(dz, other) for dz in range(4) for other in range(2)][1:]
    bufs = (hs, hr, fs, fr, xs, xr)
    reduces = []
    for part in range(2):

        def ref(dz, other, lo, n, cols, room, part=part):
            start = pl.multiple_of(place.block(dz, other) * ROWS + lo, HALF)
            return image.at[part, pl.ds(start, n), cols]

        def own(dz, other, lo, n, cols, part=part, ref=ref):
            return decode(ref(dz, other, lo, n, cols, None)[...])

        reduces.append(Reduce(post, place, part, bufs, own, ref, (encode, decode)))
    halos = {}

    def done(part, left, right):
        ext[part, HALO : HALO + ROWS, LEFT] = left.astype(BF16)
        ext[part, HALO : HALO + ROWS, RIGHT] = right.astype(BF16)
        halos[part] = [
            post.go(ext.at[part, pl.ds(HALO, HALO), :], ext.at[part, pl.ds(HALO + ROWS, HALO), :], above),
            post.go(ext.at[part, pl.ds(ROWS, HALO), :], ext.at[part, pl.ds(0, HALO), :], below),
        ]

    rings = {}

    class YPlace:
        @staticmethod
        def peer(dy, other):
            return y_peer(dy)

    def spread_slices(part):
        for copy in halos[part]:
            copy.wait_recv()

        @pl.when(mine == 0)
        def _():
            ext[part, :HALO, :] = jnp.zeros((HALO, GRID), BF16)

        @pl.when(mine == NSLAB - 1)
        def _():
            ext[part, HALO + ROWS : 2 * HALO + ROWS, :] = jnp.zeros((HALO, GRID), BF16)

        for q in range(GRID // 256):
            cols = pl.ds(256 * q, 256)
            padded[:, PAD + 256 * q : PAD + 256 * q + 256] = dot(t0[...], ext[part, :, cols]).astype(BF16)

        cores = {}

        def slice_step(j):
            dy, other = j // 2, j % 2
            s = lax.rem(y + dy, 4) * 2 + (1 - xl if other else xl)
            rows = pl.ds(pl.multiple_of(s * ROWS, ROWS), ROWS)
            stack = jnp.concatenate(
                [padded[rows, 256 * q : 256 * q + 512] for q in range(GRID // 256)], axis=0
            )
            tiles = encode(dot(stack, t1[s]))
            for q in range(GRID // 256):
                cols = slice(256 * q, 256 * q + 256)
                for half in range(2):
                    lo = ROWS * q + HALF * half
                    gbuf[part, half, j, :, cols] = tiles[lo : lo + HALF]
            cores[j] = post.go(gbuf.at[part, 1 - core, j], cbuf.at[part, j], core_peer)

        def arrived(*steps):
            for j in steps:
                cores[j].wait_recv()

        def own(dy, lo, n):
            both = [
                decode(gbuf[part, core, j]) + decode(cbuf[part, j])
                for j in range(2 * dy + lo // HALF, 2 * dy + (lo + n) // HALF)
            ]
            return both[0] if len(both) == 1 else jnp.concatenate(both, axis=0)

        def far(k):
            yhs[part, k] = encode(own(2, HALF * k, HALF))
            return yhs.at[part, k]

        ring = Ring(
            post, YPlace, (yhr.at[part], yfs.at[part], yfr.at[part]), own, far, (encode, decode)
        )
        slice_step(4)
        slice_step(5)
        slice_step(2)
        arrived(4, 5)
        ring.start()
        slice_step(3)
        slice_step(6)
        slice_step(7)
        arrived(2, 3, 6, 7)
        ring.middle()
        slice_step(0)
        slice_step(1)
        rings[part] = (ring, functools.partial(arrived, 0, 1))

    sides = {}

    def settle_y(part):
        ring, ready = rings[part]
        ready()
        total = ring.end()
        xsend[part] = encode(total[HALF:])
        sides[part] = post.go(xsend.at[part], xrecv.at[part], xl_peer)
        keep[part] = total[:HALF]

    def settle(part):
        sides[part].wait_recv()
        fin[part] = encode(keep[part] + decode(xrecv[part]))

        @pl.when(stays)
        def _():
            result[part] = fin[part]

        @pl.when(jnp.logical_not(stays))
        def _():
            turn_copy(part).start()

    def turn_copy(part):
        return pltpu.make_async_remote_copy(
            src_ref=fin.at[part], dst_ref=result.at[part], send_sem=fsend.at[part],
            recv_sem=frecv.at[part], device_id=turn_peer, device_id_type=MESH,
        )

    pcode[...] = encode(probe_part[...])
    probe_copies = []
    for dz, other in peers:
        rows = pl.ds(pl.multiple_of(place.slab(dz, other) * 64, 64), 64)
        probe_copies.append(post.go(pcode.at[rows, :], pbuf.at[2 * dz + other], place.peer(dz, other)))
    first, second = reduces

    def open_reduce(reduce):
        reduce.start_cross(2)
        reduce.start_far(1)
        reduce.start_far(0)

    def more_cross(reduce):
        reduce.start_cross(1)
        reduce.start_cross(3)

    open_reduce(first)
    first.rings[0].middle()
    open_reduce(second)
    first.stage2()
    more_cross(first)
    first.rings[1].middle()
    first.start_cross(0)
    first.stage3()
    second.rings[0].middle()

    total = probe_part[pl.ds(pl.multiple_of(me * 64, 64), 64), :]
    for copy, (dz, other) in zip(probe_copies, peers):
        copy.wait_recv()
        total = total + decode(pbuf[2 * dz + other])
    psum[0] = encode(total)
    core_probe = post.go(psum.at[0], pcore, core_peer)

    first.stage4()
    second.stage2()
    more_cross(second)
    second.rings[1].middle()

    core_probe.wait_recv()
    psum[1] = encode(decode(psum[0]) + decode(pcore[...]))
    y_copies = [post.go(psum.at[1], py.at[j], y_peer(j)) for j in range(1, 4)]

    done(0, first.stage5(), first.stage6())
    second.start_cross(0)
    second.stage3()

    for copy in y_copies:
        copy.wait_recv()
    psum[2] = encode((decode(psum[1]) + decode(py[1])) + (decode(py[2]) + decode(py[3])))
    xl_probe = post.go(psum.at[2], pxl, xl_peer)

    second.stage4()
    done(1, second.stage5(), second.stage6())
    spread_slices(0)

    xl_probe.wait_recv()
    span = pall.at[pl.ds(pl.multiple_of(me * 64, 64), 64), :]
    span[...] = encode(decode(psum[2]) + decode(pxl[...]))
    out_copies = [post.go(span, span, place.peer(*peer)) for peer in peers]

    spread_slices(1)
    settle_y(0)
    settle(0)
    settle_y(1)
    settle(1)
    for copy in out_copies:
        copy.wait_recv()

    @pl.when(jnp.logical_not(stays))
    def _():
        turn_copy(0).wait()
        turn_copy(1).wait()

    probe_out[...] = decode(pall[...])
    post.finish()


def backward(image, par_all, probe_part):
    whole = pl.BlockSpec(memory_space=pltpu.VMEM)
    dma = pltpu.SemaphoreType.DMA
    return pl.pallas_call(
        backward_kernel,
        out_shape=(
            jax.ShapeDtypeStruct((2, HALF, GRID), BF16),
            jax.ShapeDtypeStruct((2 * PATCH, PATCH), F32),
        ),
        in_specs=[whole] * 3,
        out_specs=(whole, whole),
        scratch_shapes=[
            pltpu.VMEM((NSLAB * ROWS, 384), BF16),
            pltpu.VMEM((NSLAB, 512, 256), BF16),
            pltpu.VMEM((2, 384, GRID), BF16),
            pltpu.VMEM((NSLAB * ROWS, GRID + 2 * PAD), BF16),
            pltpu.VMEM((2, 2, NSLAB, HALF, GRID), BF16),
            pltpu.VMEM((2, NSLAB, HALF, GRID), BF16),
            pltpu.VMEM((2, 2, HALF, GRID), BF16),
            pltpu.VMEM((2, 2, HALF, GRID), BF16),
            pltpu.VMEM((2, 2, ROWS, GRID), BF16),
            pltpu.VMEM((2, 2, ROWS, GRID), BF16),
            pltpu.VMEM((2, HALF, GRID), BF16),
            pltpu.VMEM((2, HALF, GRID), BF16),
            pltpu.VMEM((2, HALF, GRID), F32),
            pltpu.VMEM((2, HALF, GRID), BF16),
            pltpu.VMEM((2 * PATCH, PATCH), BF16),
            pltpu.VMEM((2 * PATCH, PATCH), BF16),
            pltpu.VMEM((NSLAB, 64, PATCH), BF16),
            pltpu.VMEM((64, PATCH), BF16),
            pltpu.VMEM((4, 64, PATCH), BF16),
            pltpu.VMEM((64, PATCH), BF16),
            pltpu.VMEM((3, 64, PATCH), BF16),
        ]
        + reduce_scratch()
        + [dma((96,)), dma((96,)), dma((2,)), dma((2,))],
        compiler_params=pltpu.CompilerParams(
            collective_id=1, has_side_effects=True, vmem_limit_bytes=38 << 20
        ),
        name="backward",
    )(image, par_all, probe_part)


def per_device(
    object_field, probe_field, diffraction, scan_offsets, counts, band_weights, band_offsets
):
    ang = lax.axis_index("ang")
    weights = lax.dynamic_index_in_dim(band_weights, ang, 0, keepdims=False)[0]
    offsets = lax.dynamic_index_in_dim(band_offsets, ang, 0, keepdims=False)[0]
    proj, par_all = forward(
        offsets,
        weights.astype(F32).reshape(8),
        object_field.reshape(2, GRID, GRID),
    )
    image, probe_part = slots(
        scan_offsets, counts, proj, probe_field, diffraction[0, 0]
    )
    result, probe_out = backward(image, par_all, probe_part.reshape(2 * PATCH, PATCH))
    object_grad = decode(jnp.transpose(result, (1, 0, 2)))[:, :, None, :]
    return (object_grad, probe_out.reshape(2, PATCH, PATCH))


def solution(mesh):
    placed = (
        P(None, "slab", None, None),
        P(),
        P("ang", "slab", None, None, None),
        P("ang", "slab", None, None),
        P("slab", "ang"),
        P(None, "slab", None, None),
        P(None, "slab", None),
    )
    return jax.shard_map(
        per_device,
        mesh=mesh,
        in_specs=placed,
        out_specs=(P("ang", None, "slab", None), P()),
        check_vma=False,
    )
```
